32 devices in a mesh: user: 4 (over y, x), item: 8 (over z, core).
Axes of the slice: x: 2, y: 2, z: 4, core: 2. Of those that a mesh axis runs over, the one named last changes fastest.
Arguments:
- user_emb: bfloat16 [8192, 256], P(('user', 'item')), may hold values from -200 to 200
- item_emb: bfloat16 [8192, 256], P(('item', 'user')), may hold values from -6 to 6
- user_hidden: bfloat16 [8192, 2048], P(('user', 'item')), may hold values from -6 to 6
- item_hidden: bfloat16 [8192, 2048], P(('item', 'user')), may hold values from -6 to 6
- user_expert: int32 [8192, 1], P(('user', 'item')), may hold values from 0 to 31; in each aligned block of 256 rows (0 to 255, 256 to 511, ...) at most 16 rows name the same one
- item_expert: int32 [8192, 1], P(('item', 'user')), may hold values from 0 to 31; in each aligned block of 256 rows (0 to 255, 256 to 511, ...) at most 16 rows name the same one
- positive: int32 [8192], P(('user', 'item')), may hold values from 0 to 8191
Outputs:
- row_loss: float32 [8192], P(('user', 'item'))
- user_weight_grad: float32 [32, 2048, 256], P('user', 'item')
- item_weight_grad: float32 [32, 2048, 256], P('user', 'item')
The draws below stay inside these ranges and needn't reach their ends.
Inputs may be any that keep to these rules, and one draw needn't show every extreme that they name: `user_expert`: among the rows of one device no expert is named more than 16 times; some expert reaches 16 in some device. `item_expert`: among the rows of one device no expert is named more than 16 times; some expert reaches 16 in some device.
All inputs are finite; a program needn't handle non-finite values.
Results may differ from the reference program's by a relative error of at most 0.0031.
Values may be sent and summed in bfloat16 or wider, within the bound.
No kernel may reach another device: no remote copies, remote signals or barrier semaphores. Data moves between devices by JAX's collectives and lax.ppermute only.
A program may use at most 128 MiB of HBM per device.

```python
import math
import jax
import jax.numpy as jnp
import numpy as np
from jax import lax

EMB = 256
FF = 2048
EXPERTS = 32
ROW_DEV = 256
CAP = 16
TOKENS = 8192
N_USER = 4
N_ITEM = 8


def base_items(key):
    items = jnp.clip(jax.random.normal(key, (TOKENS, EMB), jnp.float32), -5.0, 5.0)
    noise_key = jax.random.fold_in(key, 5)
    noise = jnp.clip(jax.random.normal(noise_key, (TOKENS, EMB), jnp.float32), -5.0, 5.0)
    rows = jnp.arange(TOKENS, dtype=jnp.int32)
    follow = (rows % 61 == 1)[:, None]
    before = jnp.roll(items, 1, axis=0)
    return jnp.where(follow, 0.99 * before + 0.15 * noise, items)


def draw_item_emb(key, part):
    items = base_items(key)
    return jnp.clip(items, -6.0, 6.0).astype(jnp.bfloat16)


def draw_user_emb(key, part):
    items = jnp.clip(base_items(key), -6.0, 6.0)
    key = jax.random.fold_in(key, 23)
    first_key, second_key = jax.random.split(key)
    users = jnp.clip(jax.random.normal(first_key, (TOKENS, EMB), jnp.float32), -5.0, 5.0)
    rows = jnp.arange(TOKENS, dtype=jnp.int32)
    target = rows // 53 * 61 * 7 % (61 * (TOKENS // 61 - 1))
    strength = jax.random.uniform(second_key, (TOKENS, 1), jnp.float32, 6.0, 14.0)
    aligned = jnp.clip(strength * items[target], -200.0, 200.0)
    users = jnp.where((rows % 53 == 0)[:, None], aligned, users)
    return users.astype(jnp.bfloat16)


def with_ends(values, own_key, low, high):
    longest = values.shape.index(max(values.shape))
    spots = []
    for shift in (0, 1):
        where = [jax.random.randint(jax.random.fold_in(own_key, axis), (), 0, length) for axis, length in enumerate(values.shape)]
        where[longest] = (where[longest] + shift) % values.shape[longest]
        spots.append(tuple(where))
    return values.at[spots[0]].set(low).at[spots[1]].set(high)


def block_scale(stream_key, dims, shards, least, top_value):
    def one(position, parts):
        heights = jax.random.uniform(jax.random.fold_in(jax.random.fold_in(stream_key, 6), position), (parts,), jnp.float32, least / len(shards), top_value / len(shards))
        return jnp.repeat(jnp.exp(heights), dims[position] // parts).reshape((-1,) + (1,) * (len(dims) - position - 1))

    level = one(*shards[0])
    for cut in shards[1:]:
        level = level * one(*cut)
    return level


def assign_block(rng, own, number, rows, count, top, most, lean):
    order = jax.random.permutation(rng, count)
    crowded, ordinary = load_shares(count, rows * top, most, lean, True), load_shares(count, rows * top, most, lean, False)
    places = jnp.arange(count)

    def named(lengths, offset_by):
        used = int((lengths > 0).sum())
        fixed = max(1, used // 4)
        passed = fixed + (places - fixed + offset_by * (used - fixed)) % max(1, count - fixed)
        return jnp.zeros((count,), jnp.int32).at[order[jnp.where(places < fixed, places, passed)]].set(jnp.asarray(lengths, jnp.int32))

    lengths = jnp.where(number % 4 == 0, named(crowded, number // 4), named(ordinary, number - number // 4 - 1))
    mixed = jax.random.permutation(jax.random.fold_in(own, 3), count)
    giver, taker = mixed[0:count // 2 * 2:2], mixed[1:count // 2 * 2:2]
    slack = jnp.minimum(lengths[giver] - 1, most - lengths[taker]) // 2
    slack = jnp.where((giver == order[0]) | (taker == order[0]) | (lengths[taker] == 0), 0, jnp.maximum(slack, 0))
    passed = jax.random.randint(jax.random.fold_in(own, 4), (count // 2,), 0, 1 << 20) % (slack + 1)
    lengths = lengths.at[giver].add(-passed).at[taker].add(passed)
    items = jnp.searchsorted(jnp.cumsum(lengths), jnp.arange(rows * top), side="right").astype(jnp.int32)
    grid = items.reshape(top, rows).T
    grid = grid[jax.random.permutation(jax.random.fold_in(own, 1), rows)]
    offset_by = jax.random.randint(jax.random.fold_in(own, 2), (rows, 1), 0, top)
    return jnp.take_along_axis(grid, (jnp.arange(top)[None, :] + offset_by) % top, axis=1)


def load_shares(number_of, total, limit, lean, full):
    portions = [(1 << 20) // math.isqrt(grade ** lean) + 1 for grade in range(1, number_of + 1)]
    largest = limit if full else min(limit, max(-(-total // number_of), total * portions[0] // sum(portions)))
    least = 1 if total - largest >= number_of - 1 else 0
    holding, rest = [largest] + [least] * (number_of - 1), total - largest - least * (number_of - 1)
    while rest > 0:
        free = [i for i in range(1, number_of) if holding[i] < largest] or [i for i in range(1, number_of) if holding[i] < limit]
        mass, left = sum([portions[i] for i in free]), rest
        for i in free:
            more = min(limit - holding[i], max(1, left * portions[i] // mass), rest)
            holding[i] = holding[i] + more
            rest = rest - more
    return np.array(holding)


def normal_values(own_key, shape, deviation, most, cuts=(), held_as=jnp.bfloat16):
    drawn = deviation * jax.random.normal(own_key, shape, jnp.float32)
    if cuts:
        drawn = drawn * block_scale(own_key, shape, cuts, -0.22, 0.18)
    return jnp.clip(drawn, -most, most).astype(held_as)


def setup_inputs(seed: int = 0) -> dict:
    keys = jax.random.split(jax.random.key(seed), 8)
    user_emb = draw_user_emb(jax.random.fold_in(keys[7], 71), 0)
    item_emb = draw_item_emb(jax.random.fold_in(keys[7], 71), 0)
    user_hidden = normal_values(keys[2], (TOKENS, FF), 1.0, 6.0, ((0, 32),))
    item_hidden = normal_values(keys[3], (TOKENS, FF), 1.0, 6.0, ((0, 32),))
    user_expert_keys = jax.random.split(jax.random.fold_in(keys[4], 1), TOKENS // ROW_DEV)
    user_expert_turns = jax.random.permutation(jax.random.fold_in(keys[4], 3), TOKENS // ROW_DEV)
    user_expert = jax.vmap(lambda own, number: assign_block(jax.random.fold_in(keys[4], 2), own, number, ROW_DEV, EXPERTS, 1, CAP, 2))(user_expert_keys, user_expert_turns).reshape((TOKENS, 1))
    item_expert_keys = jax.random.split(jax.random.fold_in(keys[5], 1), TOKENS // ROW_DEV)
    item_expert_turns = jax.random.permutation(jax.random.fold_in(keys[5], 3), TOKENS // ROW_DEV)
    item_expert = jax.vmap(lambda own, number: assign_block(jax.random.fold_in(keys[5], 2), own, number, ROW_DEV, EXPERTS, 1, CAP, 2))(item_expert_keys, item_expert_turns).reshape((TOKENS, 1))
    positive = with_ends(jax.random.randint(keys[6], (TOKENS,), 0, TOKENS), jax.random.fold_in(keys[6], 1), 0, TOKENS - 1).astype(jnp.int32)
    return dict(user_emb=user_emb, item_emb=item_emb, user_hidden=user_hidden, item_hidden=item_hidden, user_expert=user_expert, item_expert=item_expert, positive=positive)


def expert_sums(hidden, grad, expert):
    span = CAP * N_USER * N_ITEM
    order = jnp.argsort(expert, stable=True)
    ranked = jnp.concatenate([expert[order], jnp.full((span,), -1, jnp.int32)])
    rows_hidden = jnp.concatenate([hidden[order].astype(jnp.float32), jnp.zeros((span, FF), jnp.float32)])
    low = lax.optimization_barrier(grad.astype(jnp.bfloat16)).astype(jnp.float32)
    rows_grad = jnp.concatenate([low[order], jnp.zeros((span, EMB), jnp.float32)])

    def one(index):
        begin = jnp.sum((expert < index).astype(jnp.int32)).astype(jnp.int32)
        part_hidden = lax.dynamic_slice_in_dim(rows_hidden, begin, span)
        part_grad = lax.dynamic_slice_in_dim(rows_grad, begin, span)
        part_expert = lax.dynamic_slice_in_dim(ranked, begin, span)
        kept = jnp.where((part_expert == index)[:, None], part_hidden, 0.0)
        return jnp.dot(kept.T, part_grad, precision=lax.Precision.HIGHEST)
    return lax.map(one, jnp.arange(EXPERTS, dtype=jnp.int32))

def reference(user_emb, item_emb, user_hidden, item_hidden, user_expert, item_expert, positive):
    scale = 1.0 / math.sqrt(EMB)
    queries_all = user_emb.astype(jnp.float32)
    keys_all = item_emb.astype(jnp.float32)
    columns = jnp.arange(TOKENS, dtype=jnp.int32)
    size = math.gcd(TOKENS, 512)

    def one(carry, index):
        begin = index * size
        queries = lax.dynamic_slice_in_dim(queries_all, begin, size)
        wanted = lax.dynamic_slice_in_dim(positive, begin, size)
        scores = jnp.dot(queries, keys_all.T, precision=lax.Precision.HIGHEST) * scale
        top = lax.optimization_barrier(jnp.max(scores, axis=1))
        level = top + jnp.log(lax.optimization_barrier(jnp.sum(jnp.exp(scores - top[:, None]), axis=1)))
        hits = columns[None, :] == wanted[:, None]
        picked = lax.optimization_barrier(jnp.sum(jnp.where(hits, scores, 0.0), axis=1))
        probs = jnp.exp(scores - level[:, None])
        grads = (jnp.where(hits, probs - 1.0, probs) * scale).astype(jnp.bfloat16)
        grads = lax.optimization_barrier(grads).astype(jnp.float32)
        user_part = jnp.dot(grads, keys_all, precision=lax.Precision.HIGHEST)
        carry = carry + jnp.dot(grads.T, queries, precision=lax.Precision.HIGHEST)
        return (carry, (level - picked, user_part))
    item_grad, (losses, user_grad) = lax.scan(one, jnp.zeros((TOKENS, EMB), jnp.float32), jnp.arange(TOKENS // size, dtype=jnp.int32))
    row_loss = losses.reshape(TOKENS)
    user_grad = user_grad.reshape(TOKENS, EMB)
    user_weight_grad = expert_sums(user_hidden, user_grad, user_expert[:, 0])
    item_weight_grad = expert_sums(item_hidden, item_grad, item_expert[:, 0])
    return (row_loss, user_weight_grad, item_weight_grad)
```

```python
import functools
import math

import jax
import jax.numpy as jnp
from jax import lax
from jax.experimental import pallas as pl
from jax.experimental.pallas import tpu as pltpu
from jax.sharding import PartitionSpec as P

EMB = 256
EXPERTS = 32
CAP = 16
SCALE = 1.0 / math.sqrt(EMB)
EXTRA = 16
DIGIT = 128
MIB = 1 << 20

F32 = jnp.float32
BF16 = jnp.bfloat16
SCALARS = pl.BlockSpec(memory_space=pltpu.SMEM)


def mm(a, b, ca, cb):
    return lax.dot_general(a, b, (((ca,), (cb,)), ((), ())), preferred_element_type=F32)


def number(rows, index):
    rows = rows.astype(F32)
    high = rows[2 * index : 2 * index + 1]
    return (high * DIGIT + rows[2 * index + 1 : 2 * index + 2]).astype(jnp.int32)


def exchange(pieces, axis):
    size = lax.axis_size(axis)
    return [
        piece if k == 0 else lax.ppermute(piece, axis, [(j, j ^ k) for j in range(size)])
        for k, piece in enumerate(pieces)
    ]


def pack_kernel(emb_ref, positive_ref, user_ref, item_ref, out_ref, target_ref):
    rows = emb_ref.shape[0]
    down = lax.broadcasted_iota(jnp.int32, (rows, rows), 0)
    across = lax.broadcasted_iota(jnp.int32, (rows, rows), 1)

    def slots(expert):
        wide = jnp.broadcast_to(expert.astype(F32), (rows, rows))
        before = jnp.where((wide == wide.T) & (down < across), 1.0, 0.0)
        return expert * CAP + jnp.sum(before, axis=0, keepdims=True).astype(jnp.int32)

    user = slots(user_ref[...])
    item = slots(item_ref[...])
    target_ref[0:1, :] = user
    target_ref[1:2, :] = item
    line = lax.broadcasted_iota(jnp.int32, (EXTRA, rows), 0)
    block = jnp.zeros((EXTRA, rows), jnp.int32)
    for index, values in enumerate((positive_ref[...], user, item)):
        block = jnp.where(line == 2 * index, values // DIGIT, block)
        block = jnp.where(line == 2 * index + 1, values % DIGIT, block)
    out_ref[:rows, :] = emb_ref[...]
    out_ref[rows:, :] = block.astype(F32).astype(BF16)


def pack(emb, positive, user_expert, item_expert):
    rows, width = emb.shape
    return pl.pallas_call(
        pack_kernel,
        out_shape=[
            jax.ShapeDtypeStruct((rows + EXTRA, width), BF16),
            jax.ShapeDtypeStruct((2, rows), jnp.int32),
        ],
    )(emb, positive.reshape(1, rows), user_expert.reshape(1, rows), item_expert.reshape(1, rows))


def stats_kernel(first_ref, users_ref, *refs, rows, chunk):
    *items_refs, out_ref, s_ref = refs
    own = items_refs[0].shape[0]
    n_cols = own * len(items_refs)
    for half in range(users_ref.shape[0]):
        queries = users_ref[half, :rows, :] * jnp.asarray(SCALE, BF16)
        for k, items_ref in enumerate(items_refs):
            s_ref[half, k * own : (k + 1) * own, :] = mm(items_ref[...], queries, 1, 1)
        positive = number(users_ref[half, rows:, :], 0)
        tops = jnp.full((8, rows), -jnp.inf, F32)
        for c in range(0, n_cols, chunk):
            part = s_ref[half, c : c + chunk, :]
            tops = jnp.maximum(tops, jnp.max(part.reshape(chunk // 8, 8, rows), axis=0))
        top = jnp.max(tops, axis=0, keepdims=True)
        total = jnp.zeros((8, rows), F32)
        picked = jnp.zeros((8, rows), F32)
        for c in range(0, n_cols, chunk):
            part = s_ref[half, c : c + chunk, :]
            probs = jnp.exp(part - top)
            total = total + jnp.sum(probs.reshape(chunk // 8, 8, rows), axis=0)
            wanted = positive - (first_ref[c // own] + c % own)
            hit = lax.broadcasted_iota(jnp.int32, (chunk, rows), 0) == wanted
            chosen = jnp.where(hit, part, 0.0)
            picked = picked + jnp.sum(chosen.reshape(chunk // 8, 8, rows), axis=0)
        here = pl.ds(half * rows, rows)
        out_ref[0:1, here] = top
        out_ref[1:2, here] = jnp.sum(total, axis=0, keepdims=True)
        out_ref[2:3, here] = jnp.sum(picked, axis=0, keepdims=True)


def stats(first, users, items, rows):
    blocks, height, emb = users.shape
    own = items[0].shape[0]
    n_cols = own * len(items)
    pair = 2
    return pl.pallas_call(
        functools.partial(stats_kernel, rows=rows, chunk=64),
        grid=(blocks // pair,),
        in_specs=[SCALARS, pl.BlockSpec((pair, height, emb), lambda b: (b, 0, 0))]
        + [pl.BlockSpec((own, emb), lambda b: (0, 0))] * len(items),
        out_specs=pl.BlockSpec((3, pair * rows), lambda b: (0, b)),
        out_shape=jax.ShapeDtypeStruct((3, blocks * rows), F32),
        scratch_shapes=[pltpu.VMEM((pair, n_cols, rows), F32)],
        compiler_params=pltpu.CompilerParams(vmem_limit_bytes=40 * MIB),
        cost_estimate=pl.CostEstimate(
            flops=6 * 2 * blocks * rows * n_cols * emb,
            bytes_accessed=blocks * rows * emb * 2 + n_cols * emb * 2,
            transcendentals=blocks * rows * n_cols,
        ),
    )(first, users, *items)


def grad_kernel(first_ref, users_ref, stats_ref, *refs, rows, chunk, count):
    items_refs = refs[:count]
    loss_ref, user_ref = refs[count : count + 2]
    part_refs = refs[count + 2 : 2 * count + 2]
    s_ref, g_ref, flip_ref = refs[2 * count + 2 :]
    own = items_refs[0].shape[0]
    n_cols = own * count
    step = pl.program_id(0)

    @pl.when(step == 0)
    def _():
        for k in range(count):
            flip_ref[:, k * own : (k + 1) * own] = items_refs[k][...].T
            part_refs[k][...] = jnp.zeros_like(part_refs[k])

    for half in range(users_ref.shape[0]):
        here = pl.ds(half * rows, rows)
        queries = users_ref[half, :rows, :]
        scaled = queries * jnp.asarray(SCALE, BF16)
        for k in range(count):
            s_ref[half, k * own : (k + 1) * own, :] = mm(items_refs[k][...], scaled, 1, 1)
        positive = number(users_ref[half, rows:, :], 0)
        tops = stats_ref[:, 0, here]
        top = jnp.max(tops, axis=0, keepdims=True)
        total = jnp.sum(stats_ref[:, 1, here] * jnp.exp(tops - top), axis=0, keepdims=True)
        level = top + jnp.log(total)
        loss_ref[0:1, here] = level - jnp.sum(stats_ref[:, 2, here], axis=0, keepdims=True)
        for c in range(0, n_cols, chunk):
            probs = jnp.exp(s_ref[half, c : c + chunk, :] - level)
            wanted = positive - (first_ref[c // own] + c % own)
            hit = lax.broadcasted_iota(jnp.int32, (chunk, rows), 0) == wanted
            g_ref[half, c : c + chunk, :] = jnp.where(hit, probs - 1.0, probs).astype(BF16)
        for k in range(count):
            part_refs[k][...] += mm(g_ref[half, k * own : (k + 1) * own, :], queries, 1, 0)
        user_ref[here, :] = mm(flip_ref[...], g_ref[half], 1, 0).T * SCALE

    @pl.when(step == pl.num_programs(0) - 1)
    def _():
        for k in range(count):
            part_refs[k][...] = part_refs[k][...] * SCALE


def grads(first, users, items, gathered, rows):
    blocks, height, emb = users.shape
    count = len(items)
    own = items[0].shape[0]
    n_cols = own * count
    pair = 2
    groups = gathered.shape[0]
    results = pl.pallas_call(
        functools.partial(grad_kernel, rows=rows, chunk=64, count=count),
        grid=(blocks // pair,),
        in_specs=[
            SCALARS,
            pl.BlockSpec((pair, height, emb), lambda b: (b, 0, 0)),
            pl.BlockSpec((groups, 3, pair * rows), lambda b: (0, 0, b)),
        ]
        + [pl.BlockSpec((own, emb), lambda b: (0, 0))] * count,
        out_specs=[
            pl.BlockSpec((1, pair * rows), lambda b: (0, b)),
            pl.BlockSpec((pair * rows, emb), lambda b: (b, 0)),
        ]
        + [pl.BlockSpec((own, emb), lambda b: (0, 0))] * count,
        out_shape=[
            jax.ShapeDtypeStruct((1, blocks * rows), F32),
            jax.ShapeDtypeStruct((blocks * rows, emb), F32),
        ]
        + [jax.ShapeDtypeStruct((own, emb), F32)] * count,
        scratch_shapes=[
            pltpu.VMEM((pair, n_cols, rows), F32),
            pltpu.VMEM((pair, n_cols, rows), BF16),
            pltpu.VMEM((emb, n_cols), BF16),
        ],
        compiler_params=pltpu.CompilerParams(vmem_limit_bytes=48 * MIB),
        cost_estimate=pl.CostEstimate(
            flops=8 * 2 * blocks * rows * n_cols * emb,
            bytes_accessed=blocks * rows * emb * 6 + n_cols * emb * 6,
            transcendentals=blocks * rows * n_cols,
        ),
    )(first, users, gathered, *items)
    return results[0], results[1], results[2:]


def hidden_kernel(me_ref, users_ref, hidden_ref, *out_refs):
    rows = users_ref.shape[2]
    span = out_refs[0].shape[2]
    place = lax.broadcasted_iota(jnp.int32, (span, rows), 0)
    for tower in range(2):
        target = number(users_ref[0], 1 + tower)
        values = hidden_ref[0, tower * rows : (tower + 1) * rows, :]
        for k, out_ref in enumerate(out_refs):
            onehot = (place == target - (me_ref[0] ^ k) * span).astype(F32).astype(BF16)
            out_ref[tower, 0] = mm(onehot, values, 1, 0).astype(BF16)


def slot_hidden(me, users, hidden, groups):
    blocks, height, rows = users.shape
    width = hidden.shape[2]
    span = EXPERTS * CAP // groups
    return pl.pallas_call(
        hidden_kernel,
        grid=(blocks,),
        in_specs=[
            SCALARS,
            pl.BlockSpec((1, EXTRA, rows), lambda b: (b, rows // EXTRA, 0)),
            pl.BlockSpec((1, 2 * rows, width), lambda b: (b, 0, 0)),
        ],
        out_specs=[pl.BlockSpec((2, 1, span, width), lambda b: (0, b, 0, 0))] * groups,
        out_shape=[jax.ShapeDtypeStruct((2, blocks, span, width), BF16)] * groups,
        cost_estimate=pl.CostEstimate(
            flops=4 * blocks * EXPERTS * CAP * rows * width,
            bytes_accessed=2 * blocks * (rows + EXPERTS * CAP) * width * 2,
            transcendentals=0,
        ),
    )(me, users, hidden)


def route_kernel(me_ref, target_ref, *refs, tower, count):
    total = refs[0][...]
    for ref in refs[1:count]:
        total = total + ref[...]
    low = total.astype(BF16)
    span = refs[count].shape[0]
    place = lax.broadcasted_iota(jnp.int32, (span, low.shape[0]), 0)
    target = target_ref[tower : tower + 1, :]
    for k, out_ref in enumerate(refs[count:]):
        onehot = (place == target - (me_ref[0] ^ k) * span).astype(F32).astype(BF16)
        out_ref[...] = mm(onehot, low, 1, 0).astype(BF16)


def route(me, targets, pieces, tower, groups):
    rows, emb = pieces[0].shape
    span = EXPERTS * CAP // groups
    return pl.pallas_call(
        functools.partial(route_kernel, tower=tower, count=len(pieces)),
        in_specs=[SCALARS] + [pl.BlockSpec(memory_space=pltpu.VMEM)] * (1 + len(pieces)),
        out_shape=[jax.ShapeDtypeStruct((span, emb), BF16)] * groups,
        cost_estimate=pl.CostEstimate(
            flops=2 * EXPERTS * CAP * rows * emb,
            bytes_accessed=len(pieces) * rows * emb * 4 + EXPERTS * CAP * emb * 2,
            transcendentals=0,
        ),
    )(me, targets, *pieces)


def outer_kernel(*refs):
    *hidden_refs, grad_ref, out_ref = refs
    _, blocks, span, width = hidden_refs[0].shape
    emb = grad_ref.shape[-1]
    for e in range(span // CAP):
        here = slice(e * CAP, (e + 1) * CAP)
        left = [ref[0, :, here, :].reshape(blocks * CAP, width) for ref in hidden_refs]
        right = [
            grad_ref[:, k, here, :].reshape(blocks * CAP, emb) for k in range(len(hidden_refs))
        ]
        out_ref[e] = mm(jnp.concatenate(left), jnp.concatenate(right), 0, 0)


def outer(hidden, grad, tower):
    _, blocks, span, width = hidden[0].shape
    emb = grad.shape[-1]
    own = span // CAP
    return pl.pallas_call(
        outer_kernel,
        grid=(1,),
        in_specs=[pl.BlockSpec((1, blocks, span, width), lambda _: (tower, 0, 0, 0))] * len(hidden)
        + [pl.BlockSpec(grad.shape, lambda _: (0, 0, 0, 0))],
        out_specs=pl.BlockSpec((own, width, emb), lambda _: (0, 0, 0)),
        out_shape=jax.ShapeDtypeStruct((own, width, emb), F32),
        compiler_params=pltpu.CompilerParams(vmem_limit_bytes=40 * MIB),
        cost_estimate=pl.CostEstimate(
            flops=2 * own * width * emb * len(hidden) * blocks * CAP,
            bytes_accessed=len(hidden) * blocks * span * (width + emb) * 2 + own * width * emb * 4,
            transcendentals=0,
        ),
    )(*hidden, grad)


def shards(user_emb, item_emb, user_hidden, item_hidden, user_expert, item_expert, positive):
    rows, emb = user_emb.shape
    groups = lax.axis_size("user")
    parts = lax.axis_size("item")
    width = user_hidden.shape[1] // parts
    me = lax.axis_index("user").astype(jnp.int32)
    others = me ^ jnp.arange(groups, dtype=jnp.int32)
    first = (lax.axis_index("item").astype(jnp.int32) * groups + others) * rows
    me = me.reshape(1)

    packed, targets = pack(user_emb, positive, user_expert, item_expert)
    users = lax.all_gather(packed, "item", axis=0)
    items = exchange([item_emb] * groups, "user")

    def by_part(hidden):
        return hidden.reshape(rows, parts, width).transpose(1, 0, 2)

    cut = jnp.concatenate([by_part(user_hidden), by_part(item_hidden)], axis=1)
    cols = lax.all_to_all(cut, "item", split_axis=0, concat_axis=0, tiled=True)

    gathered = lax.all_gather(stats(first, users, items, rows), "item", axis=0)
    gathered, cols = lax.optimization_barrier((gathered, cols))
    hidden_rows = exchange(slot_hidden(me, users, cols, groups), "user")

    losses, user_part, item_parts = grads(first, users, items, gathered, rows)
    row_loss = lax.dynamic_slice_in_dim(losses[0], lax.axis_index("item") * rows, rows)
    item_pieces = exchange(item_parts, "user")
    user_grad = lax.psum_scatter(user_part, "item", scatter_dimension=0, tiled=True)

    def spread(pieces, tower):
        got = exchange(route(me, targets, pieces, tower, groups), "user")
        return lax.all_gather(jnp.stack(got), "item", axis=0)

    item_weight_grad = outer(hidden_rows, spread(item_pieces, 1), 1)
    user_weight_grad = outer(hidden_rows, spread([user_grad], 0), 0)
    return (row_loss, user_weight_grad, item_weight_grad)


def solution(mesh):
    placed = (
        P(("user", "item"), None),
        P(("item", "user"), None),
        P(("user", "item"), None),
        P(("item", "user"), None),
        P(("user", "item"), None),
        P(("item", "user"), None),
        P(("user", "item")),
    )
    return jax.shard_map(
        shards,
        mesh=mesh,
        in_specs=placed,
        out_specs=(P(("user", "item")), P("user", "item", None), P("user", "item", None)),
        check_vma=False,
    )
```

```python
import functools
import math

import jax
import jax.numpy as jnp
from jax import lax
from jax.experimental import pallas as pl
from jax.experimental.pallas import tpu as pltpu
from jax.sharding import PartitionSpec as P

EMB = 256
EXPERTS = 32
CAP = 16
SCALE = 1.0 / math.sqrt(EMB)
EXTRA = 16
DIGIT = 128
CORES = 2
MIB = 1 << 20

F32 = jnp.float32
BF16 = jnp.bfloat16
SCALARS = pl.BlockSpec(memory_space=pltpu.SMEM)
WHOLE = pl.BlockSpec(memory_space=pltpu.VMEM)


def mm(a, b, ca, cb):
    return lax.dot_general(a, b, (((ca,), (cb,)), ((), ())), preferred_element_type=F32)


def number(rows, index):
    rows = rows.astype(F32)
    high = rows[2 * index : 2 * index + 1]
    return (high * DIGIT + rows[2 * index + 1 : 2 * index + 2]).astype(jnp.int32)


def swap(piece, axis, bits):
    size = lax.axis_size(axis)
    return lax.ppermute(piece, axis, [(j, j ^ bits) for j in range(size)])


def exchange(pieces, axis, unit=1):
    return [piece if k == 0 else swap(piece, axis, k * unit) for k, piece in enumerate(pieces)]


def tie(*values):
    return lax.optimization_barrier(values)


def pack_kernel(emb_ref, positive_ref, user_ref, item_ref, out_ref):
    rows = emb_ref.shape[0]
    down = lax.broadcasted_iota(jnp.int32, (rows, rows), 0)
    across = lax.broadcasted_iota(jnp.int32, (rows, rows), 1)

    def slots(expert):
        wide = jnp.broadcast_to(expert.astype(F32), (rows, rows))
        before = jnp.where((wide == wide.T) & (down < across), 1.0, 0.0)
        return expert * CAP + jnp.sum(before, axis=0, keepdims=True).astype(jnp.int32)

    user = slots(user_ref[...])
    item = slots(item_ref[...])
    line = lax.broadcasted_iota(jnp.int32, (EXTRA, rows), 0)
    block = jnp.zeros((EXTRA, rows), jnp.int32)
    for index, values in enumerate((positive_ref[...], user, item)):
        block = jnp.where(line == 2 * index, values // DIGIT, block)
        block = jnp.where(line == 2 * index + 1, values % DIGIT, block)
    out_ref[:rows, :] = emb_ref[...]
    out_ref[rows:, :] = block.astype(F32).astype(BF16)


def pack(emb, positive, user_expert, item_expert):
    rows, width = emb.shape
    return pl.pallas_call(
        pack_kernel,
        out_shape=jax.ShapeDtypeStruct((rows + EXTRA, width), BF16),
    )(emb, positive.reshape(1, rows), user_expert.reshape(1, rows), item_expert.reshape(1, rows))


def stats_kernel(first_ref, *refs, blocks, count, chunk):
    users_refs, items_refs = refs[:blocks], refs[blocks : blocks + count]
    out_ref, all_ref, col_ref, s_ref = refs[blocks + count :]
    own, emb = items_refs[0].shape
    rows = users_refs[0].shape[0] - EXTRA
    n_cols = own * count
    for k, ref in enumerate(users_refs):
        all_ref[k] = ref[...]
    for k, ref in enumerate(items_refs):
        col_ref[k * own : (k + 1) * own, :] = ref[...]

    def pair(step, carry):
        for half in range(2):
            block = step * 2 + half
            queries = all_ref[block, :rows, :] * jnp.asarray(SCALE, BF16)
            s_ref[half] = mm(col_ref[...], queries, 1, 1)
            positive = number(all_ref[block, rows:, :], 0)
            tops = jnp.full((8, rows), -jnp.inf, F32)
            for c in range(0, n_cols, chunk):
                part = s_ref[half, c : c + chunk, :]
                tops = jnp.maximum(tops, jnp.max(part.reshape(chunk // 8, 8, rows), axis=0))
            top = jnp.max(tops, axis=0, keepdims=True)
            total = jnp.zeros((8, rows), F32)
            picked = jnp.zeros((8, rows), F32)
            for c in range(0, n_cols, chunk):
                part = s_ref[half, c : c + chunk, :]
                probs = jnp.exp(part - top)
                total = total + jnp.sum(probs.reshape(chunk // 8, 8, rows), axis=0)
                wanted = positive - (first_ref[c // own] + c % own)
                hit = lax.broadcasted_iota(jnp.int32, (chunk, rows), 0) == wanted
                chosen = jnp.where(hit, part, 0.0)
                picked = picked + jnp.sum(chosen.reshape(chunk // 8, 8, rows), axis=0)
            out_ref[block, 0:1, :] = top
            out_ref[block, 1:2, :] = jnp.sum(total, axis=0, keepdims=True)
            out_ref[block, 2:3, :] = jnp.sum(picked, axis=0, keepdims=True)
        return carry

    lax.fori_loop(0, blocks // 2, pair, 0)


def stats(first, users, items):
    height, emb = users[0].shape
    rows = height - EXTRA
    own = items[0].shape[0]
    blocks, count = len(users), len(items)
    return pl.pallas_call(
        functools.partial(stats_kernel, blocks=blocks, count=count, chunk=64),
        in_specs=[SCALARS] + [WHOLE] * (blocks + count),
        out_specs=WHOLE,
        out_shape=jax.ShapeDtypeStruct((blocks, 3, rows), F32),
        scratch_shapes=[
            pltpu.VMEM((blocks, height, emb), BF16),
            pltpu.VMEM((own * count, emb), BF16),
            pltpu.VMEM((2, own * count, rows), F32),
        ],
        compiler_params=pltpu.CompilerParams(vmem_limit_bytes=40 * MIB),
        cost_estimate=pl.CostEstimate(
            flops=6 * 2 * blocks * rows * own * count * emb,
            bytes_accessed=(blocks * rows + own * count) * emb * 2,
            transcendentals=blocks * rows * own * count,
        ),
    )(first, *users, *items)


def grad_kernel(first_ref, *refs, blocks, count, chunk):
    users_refs, items_refs = refs[:blocks], refs[blocks : blocks + count]
    refs = refs[blocks + count :]
    stats_refs, refs = refs[:blocks], refs[blocks:]
    loss_ref, near_ref, far_ref = refs[:3]
    user_refs, refs = refs[3 : 3 + blocks], refs[3 + blocks :]
    all_ref, col_ref, flip_ref, s_ref, g_ref, user_ref = refs
    own, emb = items_refs[0].shape
    rows = users_refs[0].shape[0] - EXTRA
    n_cols = own * count
    for k, ref in enumerate(users_refs):
        all_ref[k] = ref[...]
    for k, ref in enumerate(items_refs):
        col_ref[k * own : (k + 1) * own, :] = ref[...]
        flip_ref[:, k * own : (k + 1) * own] = ref[...].T

    def pair(step, carry):
        for half in range(2):
            block = step * 2 + half
            queries = all_ref[block, :rows, :] * jnp.asarray(SCALE, BF16)
            s_ref[half] = mm(col_ref[...], queries, 1, 1)
            positive = number(all_ref[block, rows:, :], 0)
            found = [ref[block ^ k] for k, ref in enumerate(stats_refs)]
            top = functools.reduce(jnp.maximum, [f[0:1] for f in found])
            total = sum(f[1:2] * jnp.exp(f[0:1] - top) for f in found)
            level = top + jnp.log(total)
            loss_ref[pl.ds(block, 1), :] = level - sum(f[2:3] for f in found)
            for c in range(0, n_cols, chunk):
                probs = jnp.exp(s_ref[half, c : c + chunk, :] - level)
                wanted = positive - (first_ref[c // own] + c % own)
                hit = lax.broadcasted_iota(jnp.int32, (chunk, rows), 0) == wanted
                g_ref[block, c : c + chunk, :] = jnp.where(hit, probs - 1.0, probs).astype(BF16)
            user_ref[block] = mm(flip_ref[...], g_ref[block], 1, 0).T * SCALE
        return carry

    lax.fori_loop(0, blocks // 2, pair, 0)
    for k, ref in enumerate(user_refs):
        ref[...] = user_ref[k]
    for k in range(count):
        left = jnp.concatenate([g_ref[b, k * own : (k + 1) * own, :] for b in range(blocks)], axis=1)
        right = jnp.concatenate([all_ref[b, :rows, :] for b in range(blocks)], axis=0)
        out_ref = near_ref if k < count // CORES else far_ref
        out_ref[k % (count // CORES)] = mm(left, right, 1, 0) * SCALE


def grads(first, users, items, gathered):
    height, emb = users[0].shape
    rows = height - EXTRA
    own = items[0].shape[0]
    blocks, count = len(users), len(items)
    results = pl.pallas_call(
        functools.partial(grad_kernel, blocks=blocks, count=count, chunk=64),
        in_specs=[SCALARS] + [WHOLE] * (2 * blocks + count),
        out_specs=[WHOLE] * (3 + blocks),
        out_shape=[jax.ShapeDtypeStruct((blocks, rows), F32)]
        + [jax.ShapeDtypeStruct((count // CORES, own, emb), F32)] * CORES
        + [jax.ShapeDtypeStruct((rows, emb), F32)] * blocks,
        scratch_shapes=[
            pltpu.VMEM((blocks, height, emb), BF16),
            pltpu.VMEM((own * count, emb), BF16),
            pltpu.VMEM((emb, own * count), BF16),
            pltpu.VMEM((2, own * count, rows), F32),
            pltpu.VMEM((blocks, own * count, rows), BF16),
            pltpu.VMEM((blocks, rows, emb), F32),
        ],
        compiler_params=pltpu.CompilerParams(vmem_limit_bytes=56 * MIB),
        cost_estimate=pl.CostEstimate(
            flops=8 * 2 * blocks * rows * own * count * emb,
            bytes_accessed=(blocks * rows + own * count) * emb * 6,
            transcendentals=blocks * rows * own * count,
        ),
    )(first, *users, *items, *gathered)
    return results[0][0], results[1], results[2], results[3:]


def add_kernel(a_ref, b_ref, *out_refs):
    for k, out_ref in enumerate(out_refs):
        out_ref[...] = a_ref[k] + b_ref[k]


def add(a, b):
    return pl.pallas_call(
        add_kernel,
        in_specs=[WHOLE] * 2,
        out_specs=[WHOLE] * a.shape[0],
        out_shape=[jax.ShapeDtypeStruct(a.shape[1:], F32)] * a.shape[0],
        cost_estimate=pl.CostEstimate(flops=a.size, bytes_accessed=12 * a.size, transcendentals=0),
    )(a, b)


def cut_kernel(in_ref, out_ref):
    width = out_ref.shape[2]
    for k in range(out_ref.shape[0]):
        out_ref[k] = in_ref[:, k * width : (k + 1) * width]


def cut(hidden, parts):
    rows, total = hidden.shape
    return pl.pallas_call(
        cut_kernel,
        in_specs=[WHOLE],
        out_specs=WHOLE,
        out_shape=jax.ShapeDtypeStruct((parts, rows, total // parts), hidden.dtype),
        cost_estimate=pl.CostEstimate(flops=0, bytes_accessed=4 * hidden.size, transcendentals=0),
    )(hidden)


def onehot_of(target, start, span):
    place = lax.broadcasted_iota(jnp.int32, (span, target.shape[1]), 0)
    return (place == target - start).astype(F32).astype(BF16)


def hidden_kernel(me_ref, near_ref, far_ref, hidden_ref, *out_refs, tower):
    span = out_refs[0].shape[1]
    apart = me_ref[1] ^ pl.program_id(0)
    line = apart // CORES
    extra = jnp.where(apart % CORES == 0, near_ref[line].astype(F32), far_ref[line].astype(F32))
    target = number(extra, 1 + tower)
    for k, out_ref in enumerate(out_refs):
        onehot = onehot_of(target, (me_ref[0] ^ k) * span, span)
        out_ref[0] = mm(onehot, hidden_ref[0], 1, 0).astype(BF16)


def slot_hidden(me, near, far, hidden, groups, tower):
    blocks, rows, width = hidden.shape
    span = EXPERTS * CAP // groups
    return pl.pallas_call(
        functools.partial(hidden_kernel, tower=tower),
        grid=(blocks,),
        in_specs=[
            SCALARS,
            pl.BlockSpec(near.shape, lambda b: (0, 0, 0)),
            pl.BlockSpec(far.shape, lambda b: (0, 0, 0)),
            pl.BlockSpec((1, rows, width), lambda b: (b, 0, 0)),
        ],
        out_specs=[pl.BlockSpec((1, span, width), lambda b: (b, 0, 0))] * groups,
        out_shape=[jax.ShapeDtypeStruct((blocks, span, width), BF16)] * groups,
        cost_estimate=pl.CostEstimate(
            flops=2 * blocks * EXPERTS * CAP * rows * width,
            bytes_accessed=blocks * (rows + EXPERTS * CAP) * width * 2,
            transcendentals=0,
        ),
    )(me, near, far, hidden)


def total_kernel(*refs):
    total = refs[0][...]
    for ref in refs[1:-1]:
        total = total + ref[...]
    refs[-1][...] = total.astype(BF16)


def total(pieces):
    shape = pieces[0].shape
    size = shape[0] * shape[1]
    return pl.pallas_call(
        total_kernel,
        in_specs=[WHOLE] * len(pieces),
        out_specs=WHOLE,
        out_shape=jax.ShapeDtypeStruct(shape, BF16),
        cost_estimate=pl.CostEstimate(
            flops=len(pieces) * size, bytes_accessed=4 * len(pieces) * size, transcendentals=0
        ),
    )(*pieces)


def select_kernel(me_ref, extra_ref, *refs, tower, lines):
    out_refs = refs[lines:]
    span = out_refs[0].shape[1]
    for j, grad_ref in enumerate(refs[:lines]):
        target = number(extra_ref[j], 1 + tower)
        for k, out_ref in enumerate(out_refs):
            onehot = onehot_of(target, (me_ref[0] ^ k) * span, span)
            out_ref[j] = mm(onehot, grad_ref[...], 1, 0).astype(BF16)


def select(me, extra, grads, groups, tower):
    lines = len(grads)
    rows, emb = grads[0].shape
    span = EXPERTS * CAP // groups
    return pl.pallas_call(
        functools.partial(select_kernel, tower=tower, lines=lines),
        in_specs=[SCALARS] + [WHOLE] * (1 + lines),
        out_specs=[WHOLE] * groups,
        out_shape=[jax.ShapeDtypeStruct((lines, span, emb), BF16)] * groups,
        cost_estimate=pl.CostEstimate(
            flops=2 * lines * EXPERTS * CAP * rows * emb,
            bytes_accessed=lines * (rows + EXPERTS * CAP) * emb * 2,
            transcendentals=0,
        ),
    )(me, extra, *grads)


def outer_kernel(order_ref, *refs, groups):
    hidden_refs, grad_refs, out_ref = refs[:groups], refs[groups:-1], refs[-1]
    lines = grad_refs[0].shape[0]
    for e in range(out_ref.shape[0]):
        here = slice(e * CAP, (e + 1) * CAP)
        left, right = [], []
        for index, grad_ref in enumerate(grad_refs):
            for j in range(lines):
                block = order_ref[index // groups * lines + j]
                left.append(hidden_refs[index % groups][block, here, :])
                right.append(grad_ref[j, here, :])
        out_ref[e] = mm(jnp.concatenate(left), jnp.concatenate(right), 0, 0)


def outer(order, hidden, grad):
    blocks, span, width = hidden[0].shape
    groups, emb = len(hidden), grad[0].shape[-1]
    own = span // CAP
    return pl.pallas_call(
        functools.partial(outer_kernel, groups=groups),
        in_specs=[SCALARS] + [WHOLE] * (groups + len(grad)),
        out_specs=WHOLE,
        out_shape=jax.ShapeDtypeStruct((own, width, emb), F32),
        compiler_params=pltpu.CompilerParams(vmem_limit_bytes=40 * MIB),
        cost_estimate=pl.CostEstimate(
            flops=2 * width * emb * groups * blocks * span,
            bytes_accessed=groups * blocks * span * (width + emb) * 2 + own * width * emb * 4,
            transcendentals=0,
        ),
    )(order, *hidden, *grad)


def shards(user_emb, item_emb, user_hidden, item_hidden, user_expert, item_expert, positive):
    rows, emb = user_emb.shape
    groups = lax.axis_size("user")
    parts = lax.axis_size("item")
    lines = parts // CORES
    me = lax.axis_index("user").astype(jnp.int32)
    part = lax.axis_index("item").astype(jnp.int32)
    others = me ^ jnp.arange(groups, dtype=jnp.int32)
    both = part ^ jnp.arange(CORES, dtype=jnp.int32)
    first = ((both[:, None] * groups + others[None, :]) * rows).reshape(-1)
    order = (both[:, None] ^ (CORES * jnp.arange(lines, dtype=jnp.int32))[None, :]).reshape(-1)
    me = jnp.stack([me, part])

    def by_part(hidden):
        return lax.all_to_all(cut(hidden, parts), "item", split_axis=0, concat_axis=0, tiled=True)

    def slots_of(cols, tower):
        return slot_hidden(me, extra_near, extra_far, cols, groups, tower)

    packed = pack(user_emb, positive, user_expert, item_expert)
    users = exchange([packed] * lines, "item", CORES)
    near = exchange([item_emb] * groups, "user")
    item_hidden, user_hidden, _ = tie(item_hidden, user_hidden, packed)
    item_cols = by_part(item_hidden)

    items = near + [swap(piece, "item", 1) for piece in near]
    extra_near = jnp.stack([block[rows:] for block in users])
    extra_far = swap(extra_near, "item", 1)
    gathered = exchange([stats(first, users, items)] * lines, "item", CORES)
    *gathered, item_cols, user_hidden = tie(*gathered, item_cols, user_hidden)
    user_cols = by_part(user_hidden)

    row_loss, item_near, item_far, user_parts = grads(first, users, items, gathered)
    user_pieces = exchange(user_parts, "item", CORES)
    item_cols, item_far = tie(item_cols, item_far)
    item_slots = slots_of(item_cols, 1)
    item_pieces = exchange(add(item_near, swap(item_far, "item", 1)), "user")
    *item_slots, item_pieces[0] = tie(*item_slots, item_pieces[0])
    item_rows = exchange(item_slots, "user")

    *user_pieces, user_cols = tie(*user_pieces, user_cols)
    user_lines = exchange([total(user_pieces)] * lines, "item", CORES)
    item_lines = exchange([total(item_pieces)] * lines, "item", CORES)
    user_rows = exchange(slots_of(user_cols, 0), "user")

    def spread(grad_lines, tower):
        got = exchange(select(me, extra_near, grad_lines, groups, tower), "user")
        return got + [swap(piece, "item", 1) for piece in got]

    *user_lines, item_rows[1] = tie(*user_lines, item_rows[1])
    user_grad = spread(user_lines, 0)
    item_grad = spread(item_lines, 1)
    item_weight_grad = outer(order, item_rows, item_grad)
    user_weight_grad = outer(order, user_rows, user_grad)
    return (row_loss, user_weight_grad, item_weight_grad)


def solution(mesh):
    placed = (
        P(("user", "item"), None),
        P(("item", "user"), None),
        P(("user", "item"), None),
        P(("item", "user"), None),
        P(("user", "item"), None),
        P(("item", "user"), None),
        P(("user", "item")),
    )
    return jax.shard_map(
        shards,
        mesh=mesh,
        in_specs=placed,
        out_specs=(P(("user", "item")), P("user", "item", None), P("user", "item", None)),
        check_vma=False,
    )
```

```python
import functools
import math

import jax
import jax.numpy as jnp
from jax import lax
from jax.experimental import pallas as pl
from jax.experimental.pallas import tpu as pltpu
from jax.sharding import PartitionSpec as P

EMB = 256
EXPERTS = 32
CAP = 16
SCALE = 1.0 / math.sqrt(EMB)
EXTRA = 16
DIGIT = 128
CORES = 2
MIB = 1 << 20

F32 = jnp.float32
BF16 = jnp.bfloat16
SCALARS = pl.BlockSpec(memory_space=pltpu.SMEM)
WHOLE = pl.BlockSpec(memory_space=pltpu.VMEM)
SMALL = pl.CostEstimate(flops=1024, bytes_accessed=1024, transcendentals=0)


def mm(a, b, ca, cb):
    return lax.dot_general(a, b, (((ca,), (cb,)), ((), ())), preferred_element_type=F32)


def number(rows, index):
    rows = rows.astype(F32)
    high = rows[2 * index : 2 * index + 1]
    return (high * DIGIT + rows[2 * index + 1 : 2 * index + 2]).astype(jnp.int32)


def swap(piece, axis, bits):
    size = lax.axis_size(axis)
    return lax.ppermute(piece, axis, [(j, j ^ bits) for j in range(size)])


def exchange(pieces, axis, unit=1):
    return [piece if k == 0 else swap(piece, axis, k * unit) for k, piece in enumerate(pieces)]


def tie(*values):
    return lax.optimization_barrier(values)


def pack_kernel(emb_ref, positive_ref, user_ref, item_ref, out_ref):
    rows = emb_ref.shape[0]
    down = lax.broadcasted_iota(jnp.int32, (rows, rows), 0)
    across = lax.broadcasted_iota(jnp.int32, (rows, rows), 1)

    def slots(expert):
        wide = jnp.broadcast_to(expert.astype(F32), (rows, rows))
        before = jnp.where((wide == wide.T) & (down < across), 1.0, 0.0)
        return expert * CAP + jnp.sum(before, axis=0, keepdims=True).astype(jnp.int32)

    user = slots(user_ref[...])
    item = slots(item_ref[...])
    line = lax.broadcasted_iota(jnp.int32, (EXTRA, rows), 0)
    block = jnp.zeros((EXTRA, rows), jnp.int32)
    for index, values in enumerate((positive_ref[...], user, item)):
        block = jnp.where(line == 2 * index, values // DIGIT, block)
        block = jnp.where(line == 2 * index + 1, values % DIGIT, block)
    out_ref[:rows, :] = emb_ref[...]
    out_ref[rows:, :] = block.astype(F32).astype(BF16)


def pack(emb, positive, user_expert, item_expert):
    rows, width = emb.shape
    return pl.pallas_call(
        pack_kernel,
        out_shape=jax.ShapeDtypeStruct((rows + EXTRA, width), BF16),
        cost_estimate=SMALL,
    )(emb, positive.reshape(1, rows), user_expert.reshape(1, rows), item_expert.reshape(1, rows))


def stats_kernel(first_ref, *refs, blocks, count, chunk):
    users_refs, items_refs = refs[:blocks], refs[blocks : blocks + count]
    out_ref, extra_ref, all_ref, col_ref, s_ref = refs[blocks + count :]
    own, emb = items_refs[0].shape
    rows = users_refs[0].shape[0] - EXTRA
    n_cols = own * count
    for k, ref in enumerate(users_refs):
        all_ref[k] = ref[...]
        extra_ref[k] = ref[rows:, :]
    for k, ref in enumerate(items_refs):
        col_ref[k * own : (k + 1) * own, :] = ref[...]

    def pair(step, carry):
        for half in range(2):
            block = step * 2 + half
            queries = all_ref[block, :rows, :] * jnp.asarray(SCALE, BF16)
            s_ref[half] = mm(col_ref[...], queries, 1, 1)
            positive = number(all_ref[block, rows:, :], 0)
            tops = jnp.full((8, rows), -jnp.inf, F32)
            for c in range(0, n_cols, chunk):
                part = s_ref[half, c : c + chunk, :]
                tops = jnp.maximum(tops, jnp.max(part.reshape(chunk // 8, 8, rows), axis=0))
            top = jnp.max(tops, axis=0, keepdims=True)
            total = jnp.zeros((8, rows), F32)
            picked = jnp.zeros((8, rows), F32)
            for c in range(0, n_cols, chunk):
                part = s_ref[half, c : c + chunk, :]
                probs = jnp.exp(part - top)
                total = total + jnp.sum(probs.reshape(chunk // 8, 8, rows), axis=0)
                wanted = positive - (first_ref[c // own] + c % own)
                hit = lax.broadcasted_iota(jnp.int32, (chunk, rows), 0) == wanted
                chosen = jnp.where(hit, part, 0.0)
                picked = picked + jnp.sum(chosen.reshape(chunk // 8, 8, rows), axis=0)
            out_ref[block, 0:1, :] = top
            out_ref[block, 1:2, :] = jnp.sum(total, axis=0, keepdims=True)
            out_ref[block, 2:3, :] = jnp.sum(picked, axis=0, keepdims=True)
        return carry

    lax.fori_loop(0, blocks // 2, pair, 0)


def stats(first, users, items):
    height, emb = users[0].shape
    rows = height - EXTRA
    own = items[0].shape[0]
    blocks, count = len(users), len(items)
    return pl.pallas_call(
        functools.partial(stats_kernel, blocks=blocks, count=count, chunk=64),
        in_specs=[SCALARS] + [WHOLE] * (blocks + count),
        out_specs=[WHOLE] * 2,
        out_shape=[
            jax.ShapeDtypeStruct((blocks, 3, rows), F32),
            jax.ShapeDtypeStruct((blocks, EXTRA, emb), BF16),
        ],
        scratch_shapes=[
            pltpu.VMEM((blocks, height, emb), BF16),
            pltpu.VMEM((own * count, emb), BF16),
            pltpu.VMEM((2, own * count, rows), F32),
        ],
        compiler_params=pltpu.CompilerParams(vmem_limit_bytes=40 * MIB),
        cost_estimate=SMALL,
    )(first, *users, *items)


def grad_kernel(first_ref, *refs, blocks, count, chunk):
    users_refs, items_refs = refs[:blocks], refs[blocks : blocks + count]
    refs = refs[blocks + count :]
    stats_refs, refs = refs[:blocks], refs[blocks:]
    loss_ref, near_ref, far_ref = refs[:3]
    user_refs, refs = refs[3 : 3 + blocks], refs[3 + blocks :]
    all_ref, col_ref, flip_ref, s_ref, g_ref, user_ref = refs
    own, emb = items_refs[0].shape
    rows = users_refs[0].shape[0] - EXTRA
    n_cols = own * count
    for k, ref in enumerate(users_refs):
        all_ref[k] = ref[...]
    for k, ref in enumerate(items_refs):
        col_ref[k * own : (k + 1) * own, :] = ref[...]
        flip_ref[:, k * own : (k + 1) * own] = ref[...].T

    def pair(step, carry):
        for half in range(2):
            block = step * 2 + half
            queries = all_ref[block, :rows, :] * jnp.asarray(SCALE, BF16)
            s_ref[half] = mm(col_ref[...], queries, 1, 1)
            positive = number(all_ref[block, rows:, :], 0)
            found = [ref[block ^ k] for k, ref in enumerate(stats_refs)]
            top = functools.reduce(jnp.maximum, [f[0:1] for f in found])
            total = sum(f[1:2] * jnp.exp(f[0:1] - top) for f in found)
            level = top + jnp.log(total)
            loss_ref[pl.ds(block, 1), :] = level - sum(f[2:3] for f in found)
            for c in range(0, n_cols, chunk):
                probs = jnp.exp(s_ref[half, c : c + chunk, :] - level)
                wanted = positive - (first_ref[c // own] + c % own)
                hit = lax.broadcasted_iota(jnp.int32, (chunk, rows), 0) == wanted
                g_ref[block, c : c + chunk, :] = jnp.where(hit, probs - 1.0, probs).astype(BF16)
            user_ref[block] = mm(flip_ref[...], g_ref[block], 1, 0).T * SCALE
        return carry

    lax.fori_loop(0, blocks // 2, pair, 0)
    for k, ref in enumerate(user_refs):
        ref[...] = user_ref[k]
    for k in range(count):
        left = jnp.concatenate([g_ref[b, k * own : (k + 1) * own, :] for b in range(blocks)], axis=1)
        right = jnp.concatenate([all_ref[b, :rows, :] for b in range(blocks)], axis=0)
        out_ref = near_ref if k < count // CORES else far_ref
        out_ref[k % (count // CORES)] = mm(left, right, 1, 0) * SCALE


def grads(first, users, items, gathered):
    height, emb = users[0].shape
    rows = height - EXTRA
    own = items[0].shape[0]
    blocks, count = len(users), len(items)
    results = pl.pallas_call(
        functools.partial(grad_kernel, blocks=blocks, count=count, chunk=64),
        in_specs=[SCALARS] + [WHOLE] * (2 * blocks + count),
        out_specs=[WHOLE] * (3 + blocks),
        out_shape=[jax.ShapeDtypeStruct((blocks, rows), F32)]
        + [jax.ShapeDtypeStruct((count // CORES, own, emb), F32)] * CORES
        + [jax.ShapeDtypeStruct((rows, emb), F32)] * blocks,
        scratch_shapes=[
            pltpu.VMEM((blocks, height, emb), BF16),
            pltpu.VMEM((own * count, emb), BF16),
            pltpu.VMEM((emb, own * count), BF16),
            pltpu.VMEM((2, own * count, rows), F32),
            pltpu.VMEM((blocks, own * count, rows), BF16),
            pltpu.VMEM((blocks, rows, emb), F32),
        ],
        compiler_params=pltpu.CompilerParams(vmem_limit_bytes=56 * MIB),
        cost_estimate=SMALL,
    )(first, *users, *items, *gathered)
    return results[0][0], results[1], results[2], results[3:]


def add_kernel(a_ref, b_ref, *out_refs):
    for k, out_ref in enumerate(out_refs):
        out_ref[...] = a_ref[k] + b_ref[k]


def add(a, b):
    return pl.pallas_call(
        add_kernel,
        in_specs=[WHOLE] * 2,
        out_specs=[WHOLE] * a.shape[0],
        out_shape=[jax.ShapeDtypeStruct(a.shape[1:], F32)] * a.shape[0],
        cost_estimate=SMALL,
    )(a, b)


def cut_kernel(in_ref, out_ref):
    width = out_ref.shape[2]
    for k in range(out_ref.shape[0]):
        out_ref[k] = in_ref[:, k * width : (k + 1) * width]


def cut(hidden, parts):
    rows, total = hidden.shape
    return pl.pallas_call(
        cut_kernel,
        in_specs=[WHOLE],
        out_specs=WHOLE,
        out_shape=jax.ShapeDtypeStruct((parts, rows, total // parts), hidden.dtype),
        cost_estimate=SMALL,
    )(hidden)


def onehot_of(target, me, groups):
    span = EXPERTS * CAP // groups
    place = lax.broadcasted_iota(jnp.int32, (EXPERTS * CAP, target.shape[1]), 0)
    place = (((place // span) ^ me) * span) + place % span
    return (place == target).astype(F32).astype(BF16)


def hidden_kernel(me_ref, near_ref, far_ref, hidden_ref, *out_refs, tower):
    pair, span = out_refs[0].shape[:2]
    for half in range(pair):
        apart = me_ref[1] ^ (pl.program_id(0) * pair + half)
        line = apart // CORES
        extra = jnp.where(apart % CORES == 0, near_ref[line].astype(F32), far_ref[line].astype(F32))
        onehot = onehot_of(number(extra, 1 + tower), me_ref[0], len(out_refs))
        moved = mm(onehot, hidden_ref[half], 1, 0).astype(BF16)
        for k, out_ref in enumerate(out_refs):
            out_ref[half] = moved[k * span : (k + 1) * span, :]


def slot_hidden(me, near, far, hidden, groups, tower):
    blocks, rows, width = hidden.shape
    span = EXPERTS * CAP // groups
    pair = 2
    return pl.pallas_call(
        functools.partial(hidden_kernel, tower=tower),
        grid=(blocks // pair,),
        in_specs=[
            SCALARS,
            pl.BlockSpec(near.shape, lambda b: (0, 0, 0)),
            pl.BlockSpec(far.shape, lambda b: (0, 0, 0)),
            pl.BlockSpec((pair, rows, width), lambda b: (b, 0, 0)),
        ],
        out_specs=[pl.BlockSpec((pair, span, width), lambda b: (b, 0, 0))] * groups,
        out_shape=[jax.ShapeDtypeStruct((blocks, span, width), BF16)] * groups,
        cost_estimate=SMALL,
    )(me, near, far, hidden)


def total_kernel(*refs):
    total = refs[0][...]
    for ref in refs[1:-1]:
        total = total + ref[...]
    refs[-1][...] = total.astype(BF16)


def total(pieces):
    shape = pieces[0].shape
    size = shape[0] * shape[1]
    return pl.pallas_call(
        total_kernel,
        in_specs=[WHOLE] * len(pieces),
        out_specs=WHOLE,
        out_shape=jax.ShapeDtypeStruct(shape, BF16),
        cost_estimate=SMALL,
    )(*pieces)


def select_kernel(me_ref, extra_ref, *refs, tower, lines):
    out_refs = refs[lines:]
    span = out_refs[0].shape[1]
    for j, grad_ref in enumerate(refs[:lines]):
        onehot = onehot_of(number(extra_ref[j], 1 + tower), me_ref[0], len(out_refs))
        moved = mm(onehot, grad_ref[...], 1, 0).astype(BF16)
        for k, out_ref in enumerate(out_refs):
            out_ref[j] = moved[k * span : (k + 1) * span, :]


def select(me, extra, grads, groups, tower):
    lines = len(grads)
    rows, emb = grads[0].shape
    span = EXPERTS * CAP // groups
    return pl.pallas_call(
        functools.partial(select_kernel, tower=tower, lines=lines),
        in_specs=[SCALARS] + [WHOLE] * (1 + lines),
        out_specs=[WHOLE] * groups,
        out_shape=[jax.ShapeDtypeStruct((lines, span, emb), BF16)] * groups,
        cost_estimate=SMALL,
    )(me, extra, *grads)


def outer_kernel(order_ref, *refs, groups):
    hidden_refs, grad_refs, out_ref = refs[:groups], refs[groups:-1], refs[-1]
    lines = grad_refs[0].shape[0]
    for e in range(out_ref.shape[0]):
        here = slice(e * CAP, (e + 1) * CAP)
        left, right = [], []
        for index, grad_ref in enumerate(grad_refs):
            for j in range(lines):
                block = order_ref[index // groups * lines + j]
                left.append(hidden_refs[index % groups][block, here, :])
                right.append(grad_ref[j, here, :])
        out_ref[e] = mm(jnp.concatenate(left), jnp.concatenate(right), 0, 0)


def outer(order, hidden, grad):
    blocks, span, width = hidden[0].shape
    groups, emb = len(hidden), grad[0].shape[-1]
    own = span // CAP
    return pl.pallas_call(
        functools.partial(outer_kernel, groups=groups),
        in_specs=[SCALARS] + [WHOLE] * (groups + len(grad)),
        out_specs=WHOLE,
        out_shape=jax.ShapeDtypeStruct((own, width, emb), F32),
        compiler_params=pltpu.CompilerParams(vmem_limit_bytes=40 * MIB),
        cost_estimate=SMALL,
    )(order, *hidden, *grad)


def shards(user_emb, item_emb, user_hidden, item_hidden, user_expert, item_expert, positive):
    rows, emb = user_emb.shape
    groups = lax.axis_size("user")
    parts = lax.axis_size("item")
    lines = parts // CORES
    me = lax.axis_index("user").astype(jnp.int32)
    part = lax.axis_index("item").astype(jnp.int32)
    others = me ^ jnp.arange(groups, dtype=jnp.int32)
    both = part ^ jnp.arange(CORES, dtype=jnp.int32)
    first = ((both[:, None] * groups + others[None, :]) * rows).reshape(-1)
    order = (both[:, None] ^ (CORES * jnp.arange(lines, dtype=jnp.int32))[None, :]).reshape(-1)
    me = jnp.stack([me, part])

    def by_part(hidden):
        return lax.all_to_all(cut(hidden, parts), "item", split_axis=0, concat_axis=0, tiled=True)

    def slots_of(cols, tower):
        return slot_hidden(me, extra_near, extra_far, cols, groups, tower)

    packed = pack(user_emb, positive, user_expert, item_expert)
    users = exchange([packed] * lines, "item", CORES)
    near = exchange([item_emb] * groups, "user")
    item_hidden, user_hidden, *near = tie(item_hidden, user_hidden, *near)
    item_cols = by_part(item_hidden)

    items = near + [swap(piece, "item", 1) for piece in near]
    found, extra_near = stats(first, users, items)
    gathered = exchange([found] * lines, "item", CORES)
    extra_far = swap(extra_near, "item", 1)

    row_loss, item_near, item_far, user_parts = grads(first, users, items, gathered)
    user_pieces = exchange(user_parts, "item", CORES)
    item_cols, user_hidden, item_far = tie(item_cols, user_hidden, item_far)
    user_cols = by_part(user_hidden)
    item_pieces = exchange(add(item_near, swap(item_far, "item", 1)), "user")
    item_rows = exchange(slots_of(item_cols, 1), "user")

    user_lines = exchange([total(user_pieces)] * lines, "item", CORES)
    item_lines = exchange([total(item_pieces)] * lines, "item", CORES)
    user_rows = exchange(slots_of(user_cols, 0), "user")

    def spread(grad_lines, tower):
        got = exchange(select(me, extra_near, grad_lines, groups, tower), "user")
        return got + [swap(piece, "item", 1) for piece in got]

    user_grad = spread(user_lines, 0)
    item_grad = spread(item_lines, 1)
    item_weight_grad = outer(order, item_rows, item_grad)
    user_weight_grad = outer(order, user_rows, user_grad)
    return (row_loss, user_weight_grad, item_weight_grad)


def solution(mesh):
    placed = (
        P(("user", "item"), None),
        P(("item", "user"), None),
        P(("user", "item"), None),
        P(("item", "user"), None),
        P(("user", "item"), None),
        P(("item", "user"), None),
        P(("user", "item")),
    )
    return jax.shard_map(
        shards,
        mesh=mesh,
        in_specs=placed,
        out_specs=(P(("user", "item")), P("user", "item", None), P("user", "item", None)),
        check_vma=False,
    )
```

```python
import functools
import math

import jax
import jax.numpy as jnp
from jax import lax
from jax.experimental import pallas as pl
from jax.experimental.pallas import tpu as pltpu
from jax.sharding import PartitionSpec as P

EMB = 256
EXPERTS = 32
CAP = 16
SCALE = 1.0 / math.sqrt(EMB)
EXTRA = 16
DIGIT = 128
CORES = 2
MIB = 1 << 20

F32 = jnp.float32
BF16 = jnp.bfloat16
SCALARS = pl.BlockSpec(memory_space=pltpu.SMEM)
WHOLE = pl.BlockSpec(memory_space=pltpu.VMEM)
SMALL = pl.CostEstimate(flops=1024, bytes_accessed=1024, transcendentals=0)


def mm(a, b, ca, cb):
    return lax.dot_general(a, b, (((ca,), (cb,)), ((), ())), preferred_element_type=F32)


def number(rows, index):
    rows = rows.astype(F32)
    high = rows[2 * index : 2 * index + 1]
    return (high * DIGIT + rows[2 * index + 1 : 2 * index + 2]).astype(jnp.int32)


def swap(piece, axis, bits):
    size = lax.axis_size(axis)
    return lax.ppermute(piece, axis, [(j, j ^ bits) for j in range(size)])


def exchange(pieces, axis, unit=1):
    return [piece if k == 0 else swap(piece, axis, k * unit) for k, piece in enumerate(pieces)]


def tie(*values):
    return lax.optimization_barrier(values)


def pack_kernel(emb_ref, positive_ref, user_ref, item_ref, out_ref):
    rows = emb_ref.shape[0]
    down = lax.broadcasted_iota(jnp.int32, (rows, rows), 0)
    across = lax.broadcasted_iota(jnp.int32, (rows, rows), 1)

    def slots(expert):
        wide = jnp.broadcast_to(expert.astype(F32), (rows, rows))
        before = jnp.where((wide == wide.T) & (down < across), 1.0, 0.0)
        return expert * CAP + jnp.sum(before, axis=0, keepdims=True).astype(jnp.int32)

    user = slots(user_ref[...])
    item = slots(item_ref[...])
    line = lax.broadcasted_iota(jnp.int32, (EXTRA, rows), 0)
    block = jnp.zeros((EXTRA, rows), jnp.int32)
    for index, values in enumerate((positive_ref[...], user, item)):
        block = jnp.where(line == 2 * index, values // DIGIT, block)
        block = jnp.where(line == 2 * index + 1, values % DIGIT, block)
    out_ref[:rows, :] = emb_ref[...]
    out_ref[rows:, :] = block.astype(F32).astype(BF16)


def pack(emb, positive, user_expert, item_expert):
    rows, width = emb.shape
    return pl.pallas_call(
        pack_kernel,
        out_shape=jax.ShapeDtypeStruct((rows + EXTRA, width), BF16),
        cost_estimate=SMALL,
    )(emb, positive.reshape(1, rows), user_expert.reshape(1, rows), item_expert.reshape(1, rows))


def gather_rows(refs, to_ref):
    height = to_ref.shape[1]
    for k, ref in enumerate(refs):
        to_ref[k] = ref[:height, :]


def hits(first_ref, positive, c, own, shape):
    wanted = positive - (first_ref[c // own] + c % own)
    return lax.broadcasted_iota(jnp.int32, shape, 0) == wanted


def stats_kernel(first_ref, *refs, blocks, count, chunk):
    users_refs, items_refs = refs[:blocks], refs[blocks : blocks + count]
    out_ref, all_ref, col_ref, s_ref = refs[blocks + count :]
    own, emb = items_refs[0].shape
    rows = users_refs[0].shape[0] - EXTRA
    n_cols = own * count
    gather_rows(users_refs, all_ref)
    for k, ref in enumerate(items_refs):
        col_ref[k * own : (k + 1) * own, :] = ref[...]

    def pair(step, carry):
        for half in range(2):
            block = step * 2 + half
            queries = all_ref[block, :rows, :] * jnp.asarray(SCALE, BF16)
            s_ref[half] = mm(col_ref[...], queries, 1, 1)
            positive = number(all_ref[block, rows:, :], 0)
            tops = jnp.full((8, rows), -jnp.inf, F32)
            for c in range(0, n_cols, chunk):
                part = s_ref[half, c : c + chunk, :]
                tops = jnp.maximum(tops, jnp.max(part.reshape(chunk // 8, 8, rows), axis=0))
            top = jnp.max(tops, axis=0, keepdims=True)
            total = jnp.zeros((8, rows), F32)
            picked = jnp.zeros((8, rows), F32)
            for c in range(0, n_cols, chunk):
                part = s_ref[half, c : c + chunk, :]
                probs = jnp.exp(part - top)
                total = total + jnp.sum(probs.reshape(chunk // 8, 8, rows), axis=0)
                chosen = jnp.where(hits(first_ref, positive, c, own, part.shape), part, 0.0)
                picked = picked + jnp.sum(chosen.reshape(chunk // 8, 8, rows), axis=0)
            out_ref[block, 0:1, :] = top
            out_ref[block, 1:2, :] = jnp.sum(total, axis=0, keepdims=True)
            out_ref[block, 2:3, :] = jnp.sum(picked, axis=0, keepdims=True)
        return carry

    lax.fori_loop(0, blocks // 2, pair, 0)


def stats(first, users, items):
    height, emb = users[0].shape
    rows = height - EXTRA
    own = items[0].shape[0]
    blocks, count = len(users), len(items)
    return pl.pallas_call(
        functools.partial(stats_kernel, blocks=blocks, count=count, chunk=64),
        in_specs=[SCALARS] + [WHOLE] * (blocks + count),
        out_specs=WHOLE,
        out_shape=jax.ShapeDtypeStruct((blocks, 3, rows), F32),
        scratch_shapes=[
            pltpu.VMEM((blocks, height, emb), BF16),
            pltpu.VMEM((own * count, emb), BF16),
            pltpu.VMEM((2, own * count, rows), F32),
        ],
        compiler_params=pltpu.CompilerParams(vmem_limit_bytes=40 * MIB),
        cost_estimate=SMALL,
    )(first, *users, *items)


def merge(refs, block):
    found = [ref[block ^ k] for k, ref in enumerate(refs)]
    top = functools.reduce(jnp.maximum, [f[0:1] for f in found])
    total = sum(f[1:2] * jnp.exp(f[0:1] - top) for f in found)
    return top + jnp.log(total), sum(f[2:3] for f in found)


def level_kernel(*refs):
    level, picked = merge(refs[:-2], 0)
    refs[-2][...] = level
    refs[-1][...] = level - picked


def levels(found):
    rows = found[0].shape[2]
    return pl.pallas_call(
        level_kernel,
        in_specs=[WHOLE] * len(found),
        out_specs=[WHOLE] * 2,
        out_shape=[jax.ShapeDtypeStruct((1, rows), F32)] * 2,
        cost_estimate=SMALL,
    )(*found)


def user_kernel(first_ref, *refs, blocks, count, chunk):
    users_refs, items_refs = refs[:blocks], refs[blocks : blocks + count]
    refs = refs[blocks + count :]
    stats_refs, out_refs, refs = refs[:blocks], refs[blocks : 2 * blocks], refs[2 * blocks :]
    all_ref, col_ref, flip_ref, s_ref, g_ref, sum_ref = refs
    own, emb = items_refs[0].shape
    rows = users_refs[0].shape[0] - EXTRA
    n_cols = own * count
    gather_rows(users_refs, all_ref)
    for k, ref in enumerate(items_refs):
        col_ref[k * own : (k + 1) * own, :] = ref[...]
        flip_ref[:, k * own : (k + 1) * own] = ref[...].T

    def pair(step, carry):
        for half in range(2):
            block = step * 2 + half
            queries = all_ref[block, :rows, :] * jnp.asarray(SCALE, BF16)
            s_ref[half] = mm(col_ref[...], queries, 1, 1)
            positive = number(all_ref[block, rows:, :], 0)
            level, _ = merge(stats_refs, block)
            for c in range(0, n_cols, chunk):
                probs = jnp.exp(s_ref[half, c : c + chunk, :] - level)
                hit = hits(first_ref, positive, c, own, probs.shape)
                g_ref[half, c : c + chunk, :] = jnp.where(hit, probs - 1.0, probs).astype(BF16)
            sum_ref[block] = mm(flip_ref[...], g_ref[half], 1, 0).T * SCALE
        return carry

    lax.fori_loop(0, blocks // 2, pair, 0)
    for k, ref in enumerate(out_refs):
        ref[...] = sum_ref[k]


def user_grads(first, users, items, found):
    height, emb = users[0].shape
    rows = height - EXTRA
    own = items[0].shape[0]
    blocks, count = len(users), len(items)
    return pl.pallas_call(
        functools.partial(user_kernel, blocks=blocks, count=count, chunk=64),
        in_specs=[SCALARS] + [WHOLE] * (2 * blocks + count),
        out_specs=[WHOLE] * blocks,
        out_shape=[jax.ShapeDtypeStruct((rows, emb), F32)] * blocks,
        scratch_shapes=[
            pltpu.VMEM((blocks, height, emb), BF16),
            pltpu.VMEM((own * count, emb), BF16),
            pltpu.VMEM((emb, own * count), BF16),
            pltpu.VMEM((2, own * count, rows), F32),
            pltpu.VMEM((2, own * count, rows), BF16),
            pltpu.VMEM((blocks, rows, emb), F32),
        ],
        compiler_params=pltpu.CompilerParams(vmem_limit_bytes=48 * MIB),
        cost_estimate=SMALL,
    )(first, *users, *items, *found)


def item_kernel(first_ref, *refs, blocks, count, chunk):
    users_refs, items_refs = refs[:blocks], refs[blocks : blocks + count]
    near_ref, far_ref, refs = refs[blocks + count], refs[blocks + count + 1], refs[blocks + count + 2 :]
    out_refs, refs = refs[:count], refs[count:]
    extra_ref, all_ref, row_ref, col_ref, level_ref, s_ref, g_ref = refs
    own, emb = items_refs[0].shape
    rows = users_refs[0].shape[0] - EXTRA
    n_cols = own * count
    gather_rows(users_refs, all_ref)
    level_ref[: blocks // 2] = near_ref[...]
    level_ref[blocks // 2 :] = far_ref[...]
    for k, ref in enumerate(users_refs):
        extra_ref[k] = ref[rows:, :]
        row_ref[k * rows : (k + 1) * rows, :] = ref[:rows, :]
    for k, ref in enumerate(items_refs):
        col_ref[k * own : (k + 1) * own, :] = ref[...]

    for block in range(blocks):
        half = block % 2
        queries = all_ref[block, :rows, :] * jnp.asarray(SCALE, BF16)
        s_ref[half] = mm(col_ref[...], queries, 1, 1)
        positive = number(all_ref[block, rows:, :], 0)
        level = level_ref[block]
        for c in range(0, n_cols, chunk):
            probs = jnp.exp(s_ref[half, c : c + chunk, :] - level)
            hit = hits(first_ref, positive, c, own, probs.shape)
            low = jnp.where(hit, probs - 1.0, probs).astype(BF16)
            g_ref[c : c + chunk, block * rows : (block + 1) * rows] = low

    for k, ref in enumerate(out_refs):
        ref[...] = mm(g_ref[k * own : (k + 1) * own, :], row_ref[...], 1, 0) * SCALE


def item_grads(first, users, items, near, far):
    height, emb = users[0].shape
    rows = height - EXTRA
    own = items[0].shape[0]
    blocks, count = len(users), len(items)
    results = pl.pallas_call(
        functools.partial(item_kernel, blocks=blocks, count=count, chunk=64),
        in_specs=[SCALARS] + [WHOLE] * (blocks + count + 2),
        out_specs=[WHOLE] * (count + 1),
        out_shape=[jax.ShapeDtypeStruct((own, emb), F32)] * count
        + [jax.ShapeDtypeStruct((blocks, EXTRA, emb), BF16)],
        scratch_shapes=[
            pltpu.VMEM((blocks, height, emb), BF16),
            pltpu.VMEM((blocks * rows, emb), BF16),
            pltpu.VMEM((own * count, emb), BF16),
            pltpu.VMEM((blocks, 1, rows), F32),
            pltpu.VMEM((2, own * count, rows), F32),
            pltpu.VMEM((own * count, blocks * rows), BF16),
        ],
        compiler_params=pltpu.CompilerParams(vmem_limit_bytes=48 * MIB),
        cost_estimate=SMALL,
    )(first, *users, *items, near, far)
    return results[:count], results[count]


def cut_kernel(in_ref, out_ref):
    width = out_ref.shape[2]
    for k in range(out_ref.shape[0]):
        out_ref[k] = in_ref[:, k * width : (k + 1) * width]


def cut(hidden, parts):
    rows, total = hidden.shape
    return pl.pallas_call(
        cut_kernel,
        in_specs=[WHOLE],
        out_specs=WHOLE,
        out_shape=jax.ShapeDtypeStruct((parts, rows, total // parts), hidden.dtype),
        cost_estimate=SMALL,
    )(hidden)


def onehot_of(target, me, groups):
    span = EXPERTS * CAP // groups
    place = lax.broadcasted_iota(jnp.int32, (EXPERTS * CAP, target.shape[1]), 0)
    place = (((place // span) ^ me) * span) + place % span
    return (place == target).astype(F32).astype(BF16)


def hidden_kernel(me_ref, extra_ref, hidden_ref, *out_refs, tower):
    pair, span = out_refs[0].shape[:2]
    for half in range(pair):
        apart = me_ref[1] ^ (pl.program_id(0) * pair + half)
        place = apart % CORES * (extra_ref.shape[0] // CORES) + apart // CORES
        onehot = onehot_of(number(extra_ref[place], 1 + tower), me_ref[0], len(out_refs))
        moved = mm(onehot, hidden_ref[half], 1, 0).astype(BF16)
        for k, out_ref in enumerate(out_refs):
            out_ref[half] = moved[k * span : (k + 1) * span, :]


def slot_hidden(me, extra, hidden, groups, tower):
    blocks, rows, width = hidden.shape
    span = EXPERTS * CAP // groups
    pair = 2
    return pl.pallas_call(
        functools.partial(hidden_kernel, tower=tower),
        grid=(blocks // pair,),
        in_specs=[
            SCALARS,
            pl.BlockSpec(extra.shape, lambda b: (0, 0, 0)),
            pl.BlockSpec((pair, rows, width), lambda b: (b, 0, 0)),
        ],
        out_specs=[pl.BlockSpec((pair, span, width), lambda b: (b, 0, 0))] * groups,
        out_shape=[jax.ShapeDtypeStruct((blocks, span, width), BF16)] * groups,
        cost_estimate=SMALL,
    )(me, extra, hidden)


def total_kernel(*refs):
    total = refs[0][...]
    for ref in refs[1:-1]:
        total = total + ref[...]
    refs[-1][...] = total.astype(BF16)


def total(pieces):
    shape = pieces[0].shape
    size = shape[0] * shape[1]
    return pl.pallas_call(
        total_kernel,
        in_specs=[WHOLE] * len(pieces),
        out_specs=WHOLE,
        out_shape=jax.ShapeDtypeStruct(shape, BF16),
        cost_estimate=SMALL,
    )(*pieces)


def select_kernel(me_ref, extra_ref, *refs, tower, lines):
    out_refs = refs[lines:]
    span = out_refs[0].shape[1]
    for j, grad_ref in enumerate(refs[:lines]):
        onehot = onehot_of(number(extra_ref[j], 1 + tower), me_ref[0], len(out_refs))
        moved = mm(onehot, grad_ref[...], 1, 0).astype(BF16)
        for k, out_ref in enumerate(out_refs):
            out_ref[j] = moved[k * span : (k + 1) * span, :]


def select(me, extra, grads, groups, tower):
    lines = len(grads)
    rows, emb = grads[0].shape
    span = EXPERTS * CAP // groups
    return pl.pallas_call(
        functools.partial(select_kernel, tower=tower, lines=lines),
        in_specs=[SCALARS] + [WHOLE] * (1 + lines),
        out_specs=[WHOLE] * groups,
        out_shape=[jax.ShapeDtypeStruct((lines, span, emb), BF16)] * groups,
        cost_estimate=SMALL,
    )(me, extra, *grads)


def outer_kernel(order_ref, *refs, groups):
    hidden_refs, grad_refs, out_ref = refs[:groups], refs[groups:-1], refs[-1]
    lines = grad_refs[0].shape[0]
    for e in range(out_ref.shape[0]):
        here = slice(e * CAP, (e + 1) * CAP)
        left, right = [], []
        for index, grad_ref in enumerate(grad_refs):
            for j in range(lines):
                block = order_ref[index // groups * lines + j]
                left.append(hidden_refs[index % groups][block, here, :])
                right.append(grad_ref[j, here, :])
        out_ref[e] = mm(jnp.concatenate(left), jnp.concatenate(right), 0, 0)


def outer(order, hidden, grad):
    blocks, span, width = hidden[0].shape
    groups, emb = len(hidden), grad[0].shape[-1]
    own = span // CAP
    return pl.pallas_call(
        functools.partial(outer_kernel, groups=groups),
        in_specs=[SCALARS] + [WHOLE] * (groups + len(grad)),
        out_specs=WHOLE,
        out_shape=jax.ShapeDtypeStruct((own, width, emb), F32),
        compiler_params=pltpu.CompilerParams(vmem_limit_bytes=40 * MIB),
        cost_estimate=SMALL,
    )(order, *hidden, *grad)


def shards(user_emb, item_emb, user_hidden, item_hidden, user_expert, item_expert, positive):
    rows, emb = user_emb.shape
    groups = lax.axis_size("user")
    parts = lax.axis_size("item")
    lines = parts // CORES
    me = lax.axis_index("user").astype(jnp.int32)
    part = lax.axis_index("item").astype(jnp.int32)
    others = me ^ jnp.arange(groups, dtype=jnp.int32)
    both = part ^ jnp.arange(CORES, dtype=jnp.int32)
    order = (both[:, None] ^ (CORES * jnp.arange(lines, dtype=jnp.int32))[None, :]).reshape(-1)
    first_cross = (order * groups + me) * rows
    first_plane = (part * groups + others) * rows
    me = jnp.stack([me, part])

    def by_part(hidden):
        return lax.all_to_all(cut(hidden, parts), "item", split_axis=0, concat_axis=0, tiled=True)

    item_line = exchange([item_emb] * lines, "item", CORES)
    packed = pack(user_emb, positive, user_expert, item_expert)
    user_plane = exchange([packed] * groups, "user")
    item_hidden, again, item_emb, *item_line = tie(item_hidden, packed, item_emb, *item_line)
    item_cross = item_line + [swap(piece, "item", 1) for piece in item_line]
    user_line = exchange([again] * lines, "item", CORES)
    item_cols = by_part(item_hidden)
    item_plane = exchange([item_emb] * groups, "user")
    user_cross = user_line + [swap(piece, "item", 1) for piece in user_line]

    found = exchange([stats(first_cross, user_plane, item_cross)] * groups, "user")
    level, loss = levels(found)
    level_near = jnp.stack(exchange([level] * lines, "item", CORES))
    level_far = swap(level_near, "item", 1)
    user_pieces = exchange(user_grads(first_cross, user_plane, item_cross, found), "user")
    item_parts, extra = item_grads(first_plane, user_cross, item_plane, level_near, level_far)
    item_cols, user_hidden, extra = tie(item_cols, user_hidden, extra)
    user_cols = by_part(user_hidden)
    item_pieces = exchange(item_parts, "user")
    user_pieces[0], *item_slots = tie(
        user_pieces[0], *slot_hidden(me, extra, item_cols, groups, 1)
    )
    item_rows = exchange(item_slots, "user")

    user_lines = exchange([total(user_pieces)] * lines, "item", CORES)
    item_lines = exchange([total(item_pieces)] * lines, "item", CORES)
    item_lines[0], *user_slots = tie(
        item_lines[0], *slot_hidden(me, extra, user_cols, groups, 0)
    )
    user_rows = exchange(user_slots, "user")

    def spread(grad_lines, tower):
        got = exchange(select(me, extra[:lines], grad_lines, groups, tower), "user")
        return got + [swap(piece, "item", 1) for piece in got]

    user_grad = spread(user_lines, 0)
    item_grad = spread(item_lines, 1)
    item_weight_grad = outer(order, item_rows, item_grad)
    user_weight_grad = outer(order, user_rows, user_grad)
    row_loss = loss[0]
    return (row_loss, user_weight_grad, item_weight_grad)


def solution(mesh):
    placed = (
        P(("user", "item"), None),
        P(("item", "user"), None),
        P(("user", "item"), None),
        P(("item", "user"), None),
        P(("user", "item"), None),
        P(("item", "user"), None),
        P(("user", "item")),
    )
    return jax.shard_map(
        shards,
        mesh=mesh,
        in_specs=placed,
        out_specs=(P(("user", "item")), P("user", "item", None), P("user", "item", None)),
        check_vma=False,
    )
```

```python
import functools
import math

import jax
import jax.numpy as jnp
from jax import lax
from jax.experimental import pallas as pl
from jax.experimental.pallas import tpu as pltpu
from jax.sharding import PartitionSpec as P

EMB = 256
EXPERTS = 32
CAP = 16
SCALE = 1.0 / math.sqrt(EMB)
EXTRA = 16
DIGIT = 128
CORES = 2
MIB = 1 << 20

F32 = jnp.float32
BF16 = jnp.bfloat16
SCALARS = pl.BlockSpec(memory_space=pltpu.SMEM)
WHOLE = pl.BlockSpec(memory_space=pltpu.VMEM)
SMALL = pl.CostEstimate(flops=1024, bytes_accessed=1024, transcendentals=0)


def mm(a, b, ca, cb):
    return lax.dot_general(a, b, (((ca,), (cb,)), ((), ())), preferred_element_type=F32)


def number(rows, index):
    rows = rows.astype(F32)
    high = rows[2 * index : 2 * index + 1]
    return (high * DIGIT + rows[2 * index + 1 : 2 * index + 2]).astype(jnp.int32)


def swap(piece, axis, bits):
    size = lax.axis_size(axis)
    return lax.ppermute(piece, axis, [(j, j ^ bits) for j in range(size)])


def exchange(pieces, axis, unit=1):
    return [piece if k == 0 else swap(piece, axis, k * unit) for k, piece in enumerate(pieces)]


def tie(*values):
    return lax.optimization_barrier(values)


def pack_kernel(emb_ref, other_ref, positive_ref, user_ref, item_ref, line_ref, plane_ref):
    rows = emb_ref.shape[0]
    down = lax.broadcasted_iota(jnp.int32, (rows, rows), 0)
    across = lax.broadcasted_iota(jnp.int32, (rows, rows), 1)

    def slots(expert):
        wide = jnp.broadcast_to(expert.astype(F32), (rows, rows))
        before = jnp.where((wide == wide.T) & (down < across), 1.0, 0.0)
        return expert * CAP + jnp.sum(before, axis=0, keepdims=True).astype(jnp.int32)

    line = lax.broadcasted_iota(jnp.int32, (EXTRA, rows), 0)
    block = jnp.zeros((EXTRA, rows), jnp.int32)
    numbers = (positive_ref[...], slots(user_ref[...]), slots(item_ref[...]))
    for index, values in enumerate(numbers):
        block = jnp.where(line == 2 * index, values // DIGIT, block)
        block = jnp.where(line == 2 * index + 1, values % DIGIT, block)
    extra = block.astype(F32).astype(BF16)
    for ref in (line_ref, plane_ref):
        ref[:rows, :] = emb_ref[...]
        ref[rows : rows + EXTRA, :] = extra
    plane_ref[rows + EXTRA :, :] = other_ref[...]


def pack(emb, other, positive, user_expert, item_expert):
    rows, width = emb.shape
    return pl.pallas_call(
        pack_kernel,
        out_shape=[
            jax.ShapeDtypeStruct((rows + EXTRA, width), BF16),
            jax.ShapeDtypeStruct((2 * rows + EXTRA, width), BF16),
        ],
        cost_estimate=SMALL,
    )(
        emb,
        other,
        positive.reshape(1, rows),
        user_expert.reshape(1, rows),
        item_expert.reshape(1, rows),
    )


def gather_rows(refs, to_ref):
    height = to_ref.shape[1]
    for k, ref in enumerate(refs):
        to_ref[k] = ref[:height, :]


def hits(first_ref, positive, c, own, shape):
    wanted = positive - (first_ref[c // own] + c % own)
    return lax.broadcasted_iota(jnp.int32, shape, 0) == wanted


def stats_kernel(first_ref, *refs, blocks, count, chunk):
    users_refs, items_refs = refs[:blocks], refs[blocks : blocks + count]
    out_ref, all_ref, col_ref, s_ref = refs[blocks + count :]
    own, emb = items_refs[0].shape
    rows = all_ref.shape[1] - EXTRA
    n_cols = own * count
    gather_rows(users_refs, all_ref)
    for k, ref in enumerate(items_refs):
        col_ref[k * own : (k + 1) * own, :] = ref[...]

    def pair(step, carry):
        for half in range(2):
            block = step * 2 + half
            queries = all_ref[block, :rows, :] * jnp.asarray(SCALE, BF16)
            s_ref[half] = mm(col_ref[...], queries, 1, 1)
            positive = number(all_ref[block, rows:, :], 0)
            tops = jnp.full((8, rows), -jnp.inf, F32)
            for c in range(0, n_cols, chunk):
                part = s_ref[half, c : c + chunk, :]
                tops = jnp.maximum(tops, jnp.max(part.reshape(chunk // 8, 8, rows), axis=0))
            top = jnp.max(tops, axis=0, keepdims=True)
            total = jnp.zeros((8, rows), F32)
            picked = jnp.zeros((8, rows), F32)
            for c in range(0, n_cols, chunk):
                part = s_ref[half, c : c + chunk, :]
                probs = jnp.exp(part - top)
                total = total + jnp.sum(probs.reshape(chunk // 8, 8, rows), axis=0)
                chosen = jnp.where(hits(first_ref, positive, c, own, part.shape), part, 0.0)
                picked = picked + jnp.sum(chosen.reshape(chunk // 8, 8, rows), axis=0)
            out_ref[block, 0:1, :] = top
            out_ref[block, 1:2, :] = jnp.sum(total, axis=0, keepdims=True)
            out_ref[block, 2:3, :] = jnp.sum(picked, axis=0, keepdims=True)
        return carry

    lax.fori_loop(0, blocks // 2, pair, 0)


def stats(first, users, items):
    own, emb = items[0].shape
    rows = (users[0].shape[0] - EXTRA) // 2
    height = rows + EXTRA
    blocks, count = len(users), len(items)
    return pl.pallas_call(
        functools.partial(stats_kernel, blocks=blocks, count=count, chunk=64),
        in_specs=[SCALARS] + [WHOLE] * (blocks + count),
        out_specs=WHOLE,
        out_shape=jax.ShapeDtypeStruct((blocks, 3, rows), F32),
        scratch_shapes=[
            pltpu.VMEM((blocks, height, emb), BF16),
            pltpu.VMEM((own * count, emb), BF16),
            pltpu.VMEM((2, own * count, rows), F32),
        ],
        compiler_params=pltpu.CompilerParams(vmem_limit_bytes=40 * MIB),
        cost_estimate=SMALL,
    )(first, *users, *items)


def merge(refs, block):
    found = [ref[block ^ k] for k, ref in enumerate(refs)]
    top = functools.reduce(jnp.maximum, [f[0:1] for f in found])
    total = sum(f[1:2] * jnp.exp(f[0:1] - top) for f in found)
    return top + jnp.log(total), sum(f[2:3] for f in found)


def level_kernel(*refs):
    level, picked = merge(refs[:-2], 0)
    refs[-2][...] = level
    refs[-1][...] = level - picked


def levels(found):
    rows = found[0].shape[2]
    return pl.pallas_call(
        level_kernel,
        in_specs=[WHOLE] * len(found),
        out_specs=[WHOLE] * 2,
        out_shape=[jax.ShapeDtypeStruct((1, rows), F32)] * 2,
        cost_estimate=SMALL,
    )(*found)


def user_kernel(first_ref, *refs, blocks, count, chunk):
    users_refs, items_refs = refs[:blocks], refs[blocks : blocks + count]
    refs = refs[blocks + count :]
    stats_refs, out_refs, refs = refs[:blocks], refs[blocks : 2 * blocks], refs[2 * blocks :]
    all_ref, col_ref, flip_ref, s_ref, g_ref, sum_ref = refs
    own, emb = items_refs[0].shape
    rows = all_ref.shape[1] - EXTRA
    n_cols = own * count
    gather_rows(users_refs, all_ref)
    for k, ref in enumerate(items_refs):
        col_ref[k * own : (k + 1) * own, :] = ref[...]
        flip_ref[:, k * own : (k + 1) * own] = ref[...].T

    def pair(step, carry):
        for half in range(2):
            block = step * 2 + half
            queries = all_ref[block, :rows, :] * jnp.asarray(SCALE, BF16)
            s_ref[half] = mm(col_ref[...], queries, 1, 1)
            positive = number(all_ref[block, rows:, :], 0)
            level, _ = merge(stats_refs, block)
            for c in range(0, n_cols, chunk):
                probs = jnp.exp(s_ref[half, c : c + chunk, :] - level)
                hit = hits(first_ref, positive, c, own, probs.shape)
                g_ref[half, c : c + chunk, :] = jnp.where(hit, probs - 1.0, probs).astype(BF16)
            sum_ref[block] = mm(flip_ref[...], g_ref[half], 1, 0).T * SCALE
        return carry

    lax.fori_loop(0, blocks // 2, pair, 0)
    for k, ref in enumerate(out_refs):
        ref[...] = sum_ref[k]


def user_grads(first, users, items, found):
    own, emb = items[0].shape
    rows = (users[0].shape[0] - EXTRA) // 2
    height = rows + EXTRA
    blocks, count = len(users), len(items)
    return pl.pallas_call(
        functools.partial(user_kernel, blocks=blocks, count=count, chunk=64),
        in_specs=[SCALARS] + [WHOLE] * (2 * blocks + count),
        out_specs=[WHOLE] * blocks,
        out_shape=[jax.ShapeDtypeStruct((rows, emb), F32)] * blocks,
        scratch_shapes=[
            pltpu.VMEM((blocks, height, emb), BF16),
            pltpu.VMEM((own * count, emb), BF16),
            pltpu.VMEM((emb, own * count), BF16),
            pltpu.VMEM((2, own * count, rows), F32),
            pltpu.VMEM((2, own * count, rows), BF16),
            pltpu.VMEM((blocks, rows, emb), F32),
        ],
        compiler_params=pltpu.CompilerParams(vmem_limit_bytes=48 * MIB),
        cost_estimate=SMALL,
    )(first, *users, *items, *found)


def item_kernel(first_ref, *refs, blocks, count, chunk):
    users_refs, plane_refs = refs[:blocks], refs[blocks : blocks + count]
    refs = refs[blocks + count :]
    level_refs, out_refs, refs = refs[:blocks], refs[blocks : blocks + count], refs[blocks + count :]
    extra_ref, row_ref, col_ref, s_ref, g_ref = refs
    own, emb = out_refs[0].shape
    rows = users_refs[0].shape[0] - EXTRA
    n_cols = own * count
    for k in range(blocks // CORES):
        extra_ref[k] = users_refs[k][rows:, :]
    for k, ref in enumerate(users_refs):
        row_ref[k * rows : (k + 1) * rows, :] = ref[:rows, :]
    for k, ref in enumerate(plane_refs):
        col_ref[k * own : (k + 1) * own, :] = ref[rows + EXTRA :, :]

    for block in range(blocks):
        half = block % 2
        queries = users_refs[block][:rows, :] * jnp.asarray(SCALE, BF16)
        s_ref[half] = mm(col_ref[...], queries, 1, 1)
        positive = number(users_refs[block][rows:, :], 0)
        level = level_refs[block][...]
        for c in range(0, n_cols, chunk):
            probs = jnp.exp(s_ref[half, c : c + chunk, :] - level)
            hit = hits(first_ref, positive, c, own, probs.shape)
            low = jnp.where(hit, probs - 1.0, probs).astype(BF16)
            g_ref[c : c + chunk, block * rows : (block + 1) * rows] = low

    for k, ref in enumerate(out_refs):
        ref[...] = mm(g_ref[k * own : (k + 1) * own, :], row_ref[...], 1, 0) * SCALE


def item_grads(first, users, planes, level):
    height, emb = users[0].shape
    rows = height - EXTRA
    own = planes[0].shape[0] - height
    blocks, count = len(users), len(planes)
    results = pl.pallas_call(
        functools.partial(item_kernel, blocks=blocks, count=count, chunk=64),
        in_specs=[SCALARS] + [WHOLE] * (2 * blocks + count),
        out_specs=[WHOLE] * (count + 1),
        out_shape=[jax.ShapeDtypeStruct((own, emb), F32)] * count
        + [jax.ShapeDtypeStruct((blocks // CORES, EXTRA, emb), BF16)],
        scratch_shapes=[
            pltpu.VMEM((blocks * rows, emb), BF16),
            pltpu.VMEM((own * count, emb), BF16),
            pltpu.VMEM((2, own * count, rows), F32),
            pltpu.VMEM((own * count, blocks * rows), BF16),
        ],
        compiler_params=pltpu.CompilerParams(vmem_limit_bytes=48 * MIB),
        cost_estimate=SMALL,
    )(first, *users, *planes, *level)
    return results[:count], results[count]


def cut_kernel(in_ref, line_ref, out_ref):
    rows = in_ref.shape[0]
    width = out_ref.shape[2]
    for k in range(out_ref.shape[0]):
        out_ref[k, :rows, :] = in_ref[:, k * width : (k + 1) * width]
        for cut_at in range(0, rows, width):
            place = rows + cut_at // width * EXTRA
            out_ref[k, place : place + EXTRA, :] = line_ref[rows:, cut_at : cut_at + width]


def cut(hidden, line, parts):
    rows, total = hidden.shape
    width = total // parts
    height = rows + EXTRA * max(1, rows // width)
    return pl.pallas_call(
        cut_kernel,
        in_specs=[WHOLE] * 2,
        out_specs=WHOLE,
        out_shape=jax.ShapeDtypeStruct((parts, height, width), hidden.dtype),
        cost_estimate=SMALL,
    )(hidden, line)


def onehot_of(target, me, groups):
    span = EXPERTS * CAP // groups
    place = lax.broadcasted_iota(jnp.int32, (EXPERTS * CAP, target.shape[1]), 0)
    place = (((place // span) ^ me) * span) + place % span
    return (place == target).astype(F32).astype(BF16)


def hidden_kernel(me_ref, hidden_ref, *out_refs, tower, rows):
    pair, span, width = out_refs[0].shape
    for half in range(pair):
        extra = [
            hidden_ref[half, place : place + EXTRA, :]
            for place in range(rows, hidden_ref.shape[1], EXTRA)
        ]
        extra = extra[0] if len(extra) == 1 else jnp.concatenate(extra, axis=1)
        onehot = onehot_of(number(extra, 1 + tower), me_ref[0], len(out_refs))
        moved = mm(onehot, hidden_ref[half, :rows, :], 1, 0).astype(BF16)
        for k, out_ref in enumerate(out_refs):
            out_ref[half] = moved[k * span : (k + 1) * span, :]


def slot_hidden(me, hidden, rows, groups, tower):
    blocks, height, width = hidden.shape
    span = EXPERTS * CAP // groups
    pair = 2
    return pl.pallas_call(
        functools.partial(hidden_kernel, tower=tower, rows=rows),
        grid=(blocks // pair,),
        in_specs=[SCALARS, pl.BlockSpec((pair, height, width), lambda b: (b, 0, 0))],
        out_specs=[pl.BlockSpec((pair, span, width), lambda b: (b, 0, 0))] * groups,
        out_shape=[jax.ShapeDtypeStruct((blocks, span, width), BF16)] * groups,
        cost_estimate=SMALL,
    )(me, hidden)


def total_kernel(*refs):
    total = refs[0][...]
    for ref in refs[1:-1]:
        total = total + ref[...]
    refs[-1][...] = total.astype(BF16)


def total(pieces):
    shape = pieces[0].shape
    size = shape[0] * shape[1]
    return pl.pallas_call(
        total_kernel,
        in_specs=[WHOLE] * len(pieces),
        out_specs=WHOLE,
        out_shape=jax.ShapeDtypeStruct(shape, BF16),
        cost_estimate=SMALL,
    )(*pieces)


def select_kernel(me_ref, extra_ref, *refs, tower, lines):
    out_refs = refs[lines:]
    span = out_refs[0].shape[1]
    for j, grad_ref in enumerate(refs[:lines]):
        onehot = onehot_of(number(extra_ref[j], 1 + tower), me_ref[0], len(out_refs))
        moved = mm(onehot, grad_ref[...], 1, 0).astype(BF16)
        for k, out_ref in enumerate(out_refs):
            out_ref[j] = moved[k * span : (k + 1) * span, :]


def select(me, extra, grads, groups, tower):
    lines = len(grads)
    rows, emb = grads[0].shape
    span = EXPERTS * CAP // groups
    return pl.pallas_call(
        functools.partial(select_kernel, tower=tower, lines=lines),
        in_specs=[SCALARS] + [WHOLE] * (1 + lines),
        out_specs=[WHOLE] * groups,
        out_shape=[jax.ShapeDtypeStruct((lines, span, emb), BF16)] * groups,
        cost_estimate=SMALL,
    )(me, extra, *grads)


def outer_kernel(order_ref, *refs, groups):
    hidden_refs, grad_refs, out_ref = refs[:groups], refs[groups:-1], refs[-1]
    lines = grad_refs[0].shape[0]
    for e in range(out_ref.shape[0]):
        here = slice(e * CAP, (e + 1) * CAP)
        left, right = [], []
        for index, grad_ref in enumerate(grad_refs):
            for j in range(lines):
                block = order_ref[index // groups * lines + j]
                left.append(hidden_refs[index % groups][block, here, :])
                right.append(grad_ref[j, here, :])
        out_ref[e] = mm(jnp.concatenate(left), jnp.concatenate(right), 0, 0)


def outer(order, hidden, grad):
    blocks, span, width = hidden[0].shape
    groups, emb = len(hidden), grad[0].shape[-1]
    own = span // CAP
    return pl.pallas_call(
        functools.partial(outer_kernel, groups=groups),
        in_specs=[SCALARS] + [WHOLE] * (groups + len(grad)),
        out_specs=WHOLE,
        out_shape=jax.ShapeDtypeStruct((own, width, emb), F32),
        compiler_params=pltpu.CompilerParams(vmem_limit_bytes=40 * MIB),
        cost_estimate=SMALL,
    )(order, *hidden, *grad)


def shards(user_emb, item_emb, user_hidden, item_hidden, user_expert, item_expert, positive):
    rows, emb = user_emb.shape
    groups = lax.axis_size("user")
    parts = lax.axis_size("item")
    lines = parts // CORES
    me = lax.axis_index("user").astype(jnp.int32)
    part = lax.axis_index("item").astype(jnp.int32)
    others = me ^ jnp.arange(groups, dtype=jnp.int32)
    both = part ^ jnp.arange(CORES, dtype=jnp.int32)
    order = (both[:, None] ^ (CORES * jnp.arange(lines, dtype=jnp.int32))[None, :]).reshape(-1)
    first_cross = (order * groups + me) * rows
    first_plane = (part * groups + others) * rows
    me = jnp.stack([me, part])

    def by_part(blocks):
        return lax.all_to_all(blocks, "item", split_axis=0, concat_axis=0, tiled=True)

    def across(pieces):
        return pieces + [swap(piece, "item", 1) for piece in pieces]

    item_line = exchange([item_emb] * lines, "item", CORES)
    line, plane = pack(user_emb, item_emb, positive, user_expert, item_expert)
    plane = exchange([plane] * groups, "user")
    item_blocks = cut(item_hidden, line, parts)
    user_blocks = cut(user_hidden, line, parts)
    again, *item_line = tie(line, *item_line)
    item_cross = across(item_line)
    user_line = exchange([again] * lines, "item", CORES)

    found = stats(first_cross, plane, item_cross)
    item_blocks, found = tie(item_blocks, found)
    found = exchange([found] * groups, "user")
    item_cols = by_part(item_blocks)
    level, loss = levels(found)
    level, *found = tie(level, *found)
    level = across(exchange([level] * lines, "item", CORES))
    user_parts = list(user_grads(first_cross, plane, item_cross, found))
    user_pieces = exchange(user_parts, "user")
    user_parts[0], *level = tie(user_parts[0], *level)
    item_parts, extra = item_grads(first_plane, across(user_line), plane, level)
    item_pieces = exchange(item_parts, "user")
    item_cols, user_blocks, extra = tie(item_cols, user_blocks, extra)
    user_cols = by_part(user_blocks)

    user_pieces[0], *item_slots = tie(
        user_parts[0], *slot_hidden(me, item_cols, rows, groups, 1)
    )
    early = groups // 2 + 1
    item_rows = exchange(item_slots[:early], "user")
    user_lines = exchange([total(user_pieces)] * lines, "item", CORES)
    item_lines = exchange([total(item_pieces)] * lines, "item", CORES)
    *user_lines, item_slots[-1] = tie(*user_lines, item_slots[-1])
    item_rows += [swap(item_slots[k], "user", k) for k in range(early, groups)]

    def spread(chosen):
        return across(exchange(chosen, "user"))

    user_chosen = select(me, extra, user_lines, groups, 0)
    user_cols, *user_chosen = tie(user_cols, *user_chosen)
    user_grad = spread(user_chosen)
    user_slots = list(slot_hidden(me, user_cols, rows, groups, 0))
    user_rows = exchange(user_slots[:early], "user")
    item_grad = spread(select(me, extra, item_lines, groups, 1))
    *user_grad, user_slots[-1] = tie(*user_grad, user_slots[-1])
    user_rows += [swap(user_slots[k], "user", k) for k in range(early, groups)]
    item_weight_grad = outer(order, item_rows, item_grad)
    user_weight_grad = outer(order, user_rows, user_grad)
    row_loss = loss[0]
    return (row_loss, user_weight_grad, item_weight_grad)


def solution(mesh):
    placed = (
        P(("user", "item"), None),
        P(("item", "user"), None),
        P(("user", "item"), None),
        P(("item", "user"), None),
        P(("user", "item"), None),
        P(("item", "user"), None),
        P(("user", "item")),
    )
    return jax.shard_map(
        shards,
        mesh=mesh,
        in_specs=placed,
        out_specs=(P(("user", "item")), P("user", "item", None), P("user", "item", None)),
        check_vma=False,
    )
```

```python
import functools
import math

import jax
import jax.numpy as jnp
from jax import lax
from jax.experimental import pallas as pl
from jax.experimental.pallas import tpu as pltpu
from jax.sharding import PartitionSpec as P

EMB = 256
EXPERTS = 32
CAP = 16
SCALE = 1.0 / math.sqrt(EMB)
EXTRA = 16
DIGIT = 128
CORES = 2
MIB = 1 << 20

F32 = jnp.float32
BF16 = jnp.bfloat16
SCALARS = pl.BlockSpec(memory_space=pltpu.SMEM)
WHOLE = pl.BlockSpec(memory_space=pltpu.VMEM)
SMALL = pl.CostEstimate(flops=1024, bytes_accessed=1024, transcendentals=0)


def mm(a, b, ca, cb):
    return lax.dot_general(a, b, (((ca,), (cb,)), ((), ())), preferred_element_type=F32)


def number(rows, index):
    rows = rows.astype(F32)
    high = rows[2 * index : 2 * index + 1]
    return (high * DIGIT + rows[2 * index + 1 : 2 * index + 2]).astype(jnp.int32)


def swap(piece, axis, bits):
    size = lax.axis_size(axis)
    return lax.ppermute(piece, axis, [(j, j ^ bits) for j in range(size)])


def exchange(pieces, axis, unit=1):
    return [piece if k == 0 else swap(piece, axis, k * unit) for k, piece in enumerate(pieces)]


def tie(*lists):
    flat = iter(lax.optimization_barrier([value for values in lists for value in values]))
    return [[next(flat) for _ in values] for values in lists]


def pack_kernel(emb_ref, other_ref, positive_ref, user_ref, item_ref, out_ref):
    rows = emb_ref.shape[0]
    down = lax.broadcasted_iota(jnp.int32, (rows, rows), 0)
    across = lax.broadcasted_iota(jnp.int32, (rows, rows), 1)

    def slots(expert):
        wide = jnp.broadcast_to(expert.astype(F32), (rows, rows))
        before = jnp.where((wide == wide.T) & (down < across), 1.0, 0.0)
        return expert * CAP + jnp.sum(before, axis=0, keepdims=True).astype(jnp.int32)

    line = lax.broadcasted_iota(jnp.int32, (EXTRA, rows), 0)
    block = jnp.zeros((EXTRA, rows), jnp.int32)
    numbers = (positive_ref[...], slots(user_ref[...]), slots(item_ref[...]))
    for index, values in enumerate(numbers):
        block = jnp.where(line == 2 * index, values // DIGIT, block)
        block = jnp.where(line == 2 * index + 1, values % DIGIT, block)
    out_ref[:rows, :] = emb_ref[...]
    out_ref[rows : rows + EXTRA, :] = block.astype(F32).astype(BF16)
    out_ref[rows + EXTRA :, :] = other_ref[...]


def pack(emb, other, positive, user_expert, item_expert):
    rows, width = emb.shape
    return pl.pallas_call(
        pack_kernel,
        out_shape=jax.ShapeDtypeStruct((2 * rows + EXTRA, width), BF16),
        cost_estimate=SMALL,
    )(
        emb,
        other,
        positive.reshape(1, rows),
        user_expert.reshape(1, rows),
        item_expert.reshape(1, rows),
    )


def gather_rows(refs, to_ref):
    height = to_ref.shape[1]
    for k, ref in enumerate(refs):
        to_ref[k] = ref[:height, :]


def hits(first_ref, positive, c, own, shape):
    wanted = positive - (first_ref[c // own] + c % own)
    return lax.broadcasted_iota(jnp.int32, shape, 0) == wanted


def stats_kernel(first_ref, *refs, blocks, count, chunk):
    users_refs, items_refs = refs[:blocks], refs[blocks : blocks + count]
    out_ref, all_ref, col_ref, s_ref = refs[blocks + count :]
    rows, emb = all_ref.shape[1] - EXTRA, all_ref.shape[2]
    own = col_ref.shape[0] // count
    n_cols = own * count
    gather_rows(users_refs, all_ref)
    for k, ref in enumerate(items_refs):
        col_ref[k * own : (k + 1) * own, :] = ref[rows + EXTRA :, :]

    def pair(step, carry):
        for half in range(2):
            block = step * 2 + half
            queries = all_ref[block, :rows, :] * jnp.asarray(SCALE, BF16)
            s_ref[half] = mm(col_ref[...], queries, 1, 1)
            positive = number(all_ref[block, rows:, :], 0)
            tops = jnp.full((8, rows), -jnp.inf, F32)
            for c in range(0, n_cols, chunk):
                part = s_ref[half, c : c + chunk, :]
                tops = jnp.maximum(tops, jnp.max(part.reshape(chunk // 8, 8, rows), axis=0))
            top = jnp.max(tops, axis=0, keepdims=True)
            total = jnp.zeros((8, rows), F32)
            picked = jnp.zeros((8, rows), F32)
            for c in range(0, n_cols, chunk):
                part = s_ref[half, c : c + chunk, :]
                probs = jnp.exp(part - top)
                total = total + jnp.sum(probs.reshape(chunk // 8, 8, rows), axis=0)
                chosen = jnp.where(hits(first_ref, positive, c, own, part.shape), part, 0.0)
                picked = picked + jnp.sum(chosen.reshape(chunk // 8, 8, rows), axis=0)
            out_ref[block, 0:1, :] = top
            out_ref[block, 1:2, :] = jnp.sum(total, axis=0, keepdims=True)
            out_ref[block, 2:3, :] = jnp.sum(picked, axis=0, keepdims=True)
        return carry

    lax.fori_loop(0, blocks // 2, pair, 0)


def stats(first, users, items):
    emb = users[0].shape[1]
    rows = own = (users[0].shape[0] - EXTRA) // 2
    height = rows + EXTRA
    blocks, count = len(users), len(items)
    return pl.pallas_call(
        functools.partial(stats_kernel, blocks=blocks, count=count, chunk=64),
        in_specs=[SCALARS] + [WHOLE] * (blocks + count),
        out_specs=WHOLE,
        out_shape=jax.ShapeDtypeStruct((blocks, 3, rows), F32),
        scratch_shapes=[
            pltpu.VMEM((blocks, height, emb), BF16),
            pltpu.VMEM((own * count, emb), BF16),
            pltpu.VMEM((2, own * count, rows), F32),
        ],
        compiler_params=pltpu.CompilerParams(vmem_limit_bytes=40 * MIB),
        cost_estimate=SMALL,
    )(first, *users, *items)


def merge(refs, block):
    found = [ref[block ^ k] for k, ref in enumerate(refs)]
    top = functools.reduce(jnp.maximum, [f[0:1] for f in found])
    total = sum(f[1:2] * jnp.exp(f[0:1] - top) for f in found)
    return top + jnp.log(total), sum(f[2:3] for f in found)


def level_kernel(*refs):
    level, picked = merge(refs[:-2], 0)
    refs[-2][...] = level
    refs[-1][...] = level - picked


def levels(found):
    rows = found[0].shape[2]
    return pl.pallas_call(
        level_kernel,
        in_specs=[WHOLE] * len(found),
        out_specs=[WHOLE] * 2,
        out_shape=[jax.ShapeDtypeStruct((1, rows), F32)] * 2,
        cost_estimate=SMALL,
    )(*found)


def user_kernel(first_ref, *refs, blocks, count, chunk):
    users_refs, items_refs = refs[:blocks], refs[blocks : blocks + count]
    refs = refs[blocks + count :]
    stats_refs, out_refs, refs = refs[:blocks], refs[blocks : 2 * blocks], refs[2 * blocks :]
    all_ref, col_ref, flip_ref, s_ref, g_ref, sum_ref = refs
    rows, emb = all_ref.shape[1] - EXTRA, all_ref.shape[2]
    own = col_ref.shape[0] // count
    n_cols = own * count
    gather_rows(users_refs, all_ref)
    for k, ref in enumerate(items_refs):
        col_ref[k * own : (k + 1) * own, :] = ref[rows + EXTRA :, :]
        flip_ref[:, k * own : (k + 1) * own] = ref[rows + EXTRA :, :].T

    def pair(step, carry):
        for half in range(2):
            block = step * 2 + half
            queries = all_ref[block, :rows, :] * jnp.asarray(SCALE, BF16)
            s_ref[half] = mm(col_ref[...], queries, 1, 1)
            positive = number(all_ref[block, rows:, :], 0)
            level, _ = merge(stats_refs, block)
            for c in range(0, n_cols, chunk):
                probs = jnp.exp(s_ref[half, c : c + chunk, :] - level)
                hit = hits(first_ref, positive, c, own, probs.shape)
                g_ref[half, c : c + chunk, :] = jnp.where(hit, probs - 1.0, probs).astype(BF16)
            sum_ref[block] = mm(flip_ref[...], g_ref[half], 1, 0).T * SCALE
        return carry

    lax.fori_loop(0, blocks // 2, pair, 0)
    for k, ref in enumerate(out_refs):
        ref[...] = sum_ref[k]


def user_grads(first, users, items, found):
    emb = users[0].shape[1]
    rows = own = (users[0].shape[0] - EXTRA) // 2
    height = rows + EXTRA
    blocks, count = len(users), len(items)
    return pl.pallas_call(
        functools.partial(user_kernel, blocks=blocks, count=count, chunk=64),
        in_specs=[SCALARS] + [WHOLE] * (2 * blocks + count),
        out_specs=[WHOLE] * blocks,
        out_shape=[jax.ShapeDtypeStruct((rows, emb), F32)] * blocks,
        scratch_shapes=[
            pltpu.VMEM((blocks, height, emb), BF16),
            pltpu.VMEM((own * count, emb), BF16),
            pltpu.VMEM((emb, own * count), BF16),
            pltpu.VMEM((2, own * count, rows), F32),
            pltpu.VMEM((2, own * count, rows), BF16),
            pltpu.VMEM((blocks, rows, emb), F32),
        ],
        compiler_params=pltpu.CompilerParams(vmem_limit_bytes=48 * MIB),
        cost_estimate=SMALL,
    )(first, *users, *items, *found)


def item_kernel(first_ref, *refs, blocks, count, chunk):
    users_refs, plane_refs = refs[:blocks], refs[blocks : blocks + count]
    refs = refs[blocks + count :]
    level_refs, out_refs, refs = refs[:blocks], refs[blocks : blocks + count], refs[blocks + count :]
    extra_ref, row_ref, col_ref, s_ref, g_ref = refs
    own, emb = out_refs[0].shape
    rows = row_ref.shape[0] // blocks
    n_cols = own * count
    for k in range(blocks // CORES):
        extra_ref[k] = users_refs[k][rows : rows + EXTRA, :]
    for k, ref in enumerate(users_refs):
        row_ref[k * rows : (k + 1) * rows, :] = ref[:rows, :]
    for k, ref in enumerate(plane_refs):
        col_ref[k * own : (k + 1) * own, :] = ref[rows + EXTRA :, :]

    for block in range(blocks):
        half = block % 2
        queries = users_refs[block][:rows, :] * jnp.asarray(SCALE, BF16)
        s_ref[half] = mm(col_ref[...], queries, 1, 1)
        positive = number(users_refs[block][rows : rows + EXTRA, :], 0)
        level = level_refs[block][...]
        for c in range(0, n_cols, chunk):
            probs = jnp.exp(s_ref[half, c : c + chunk, :] - level)
            hit = hits(first_ref, positive, c, own, probs.shape)
            low = jnp.where(hit, probs - 1.0, probs).astype(BF16)
            g_ref[c : c + chunk, block * rows : (block + 1) * rows] = low

    for k, ref in enumerate(out_refs):
        ref[...] = mm(g_ref[k * own : (k + 1) * own, :], row_ref[...], 1, 0) * SCALE


def item_grads(first, users, planes, level):
    emb = users[0].shape[1]
    rows = own = (users[0].shape[0] - EXTRA) // 2
    blocks, count = len(users), len(planes)
    results = pl.pallas_call(
        functools.partial(item_kernel, blocks=blocks, count=count, chunk=64),
        in_specs=[SCALARS] + [WHOLE] * (2 * blocks + count),
        out_specs=[WHOLE] * (count + 1),
        out_shape=[jax.ShapeDtypeStruct((own, emb), F32)] * count
        + [jax.ShapeDtypeStruct((blocks // CORES, EXTRA, emb), BF16)],
        scratch_shapes=[
            pltpu.VMEM((blocks * rows, emb), BF16),
            pltpu.VMEM((own * count, emb), BF16),
            pltpu.VMEM((2, own * count, rows), F32),
            pltpu.VMEM((own * count, blocks * rows), BF16),
        ],
        compiler_params=pltpu.CompilerParams(vmem_limit_bytes=48 * MIB),
        cost_estimate=SMALL,
    )(first, *users, *planes, *level)
    return results[:count], results[count]


def cut_kernel(in_ref, line_ref, out_ref):
    rows = in_ref.shape[0]
    width = out_ref.shape[2]
    for k in range(out_ref.shape[0]):
        out_ref[k, :rows, :] = in_ref[:, k * width : (k + 1) * width]
        for cut_at in range(0, rows, width):
            place = rows + cut_at // width * EXTRA
            out_ref[k, place : place + EXTRA, :] = line_ref[rows : rows + EXTRA, cut_at : cut_at + width]


def cut(hidden, line, parts):
    rows, total = hidden.shape
    width = total // parts
    height = rows + EXTRA * max(1, rows // width)
    return pl.pallas_call(
        cut_kernel,
        in_specs=[WHOLE] * 2,
        out_specs=WHOLE,
        out_shape=jax.ShapeDtypeStruct((parts, height, width), hidden.dtype),
        cost_estimate=SMALL,
    )(hidden, line)


def onehot_of(target, me, groups):
    span = EXPERTS * CAP // groups
    place = lax.broadcasted_iota(jnp.int32, (EXPERTS * CAP, target.shape[1]), 0)
    place = (((place // span) ^ me) * span) + place % span
    return (place == target).astype(F32).astype(BF16)


def hidden_kernel(me_ref, hidden_ref, *out_refs, tower, rows):
    pair, span, width = out_refs[0].shape
    for half in range(pair):
        extra = [
            hidden_ref[half, place : place + EXTRA, :]
            for place in range(rows, hidden_ref.shape[1], EXTRA)
        ]
        extra = extra[0] if len(extra) == 1 else jnp.concatenate(extra, axis=1)
        onehot = onehot_of(number(extra, 1 + tower), me_ref[0], len(out_refs))
        moved = mm(onehot, hidden_ref[half, :rows, :], 1, 0).astype(BF16)
        for k, out_ref in enumerate(out_refs):
            out_ref[half] = moved[k * span : (k + 1) * span, :]


def slot_hidden(me, hidden, rows, groups, tower):
    blocks, height, width = hidden.shape
    span = EXPERTS * CAP // groups
    pair = 2
    return pl.pallas_call(
        functools.partial(hidden_kernel, tower=tower, rows=rows),
        grid=(blocks // pair,),
        in_specs=[SCALARS, pl.BlockSpec((pair, height, width), lambda b: (b, 0, 0))],
        out_specs=[pl.BlockSpec((pair, span, width), lambda b: (b, 0, 0))] * groups,
        out_shape=[jax.ShapeDtypeStruct((blocks, span, width), BF16)] * groups,
        cost_estimate=SMALL,
    )(me, hidden)


def total_kernel(*refs):
    *in_refs, out_ref = refs
    count = len(in_refs) // 2
    rows = in_refs[0].shape[0]
    for tower in range(2):
        pieces = [ref[...] for ref in in_refs[tower * count : (tower + 1) * count]]
        out_ref[tower * rows : (tower + 1) * rows, :] = sum(pieces[1:], pieces[0]).astype(BF16)


def total(user_pieces, item_pieces):
    rows, emb = user_pieces[0].shape
    return pl.pallas_call(
        total_kernel,
        in_specs=[WHOLE] * (2 * len(user_pieces)),
        out_specs=WHOLE,
        out_shape=jax.ShapeDtypeStruct((2 * rows, emb), BF16),
        cost_estimate=SMALL,
    )(*user_pieces, *item_pieces)


def select_kernel(me_ref, extra_ref, *refs, lines):
    out_refs = refs[lines:]
    span = out_refs[0].shape[2]
    rows = refs[0].shape[0] // 2
    for j, grad_ref in enumerate(refs[:lines]):
        for tower in range(2):
            onehot = onehot_of(number(extra_ref[j], 1 + tower), me_ref[0], len(out_refs))
            values = grad_ref[tower * rows : (tower + 1) * rows, :]
            moved = mm(onehot, values, 1, 0).astype(BF16)
            for k, out_ref in enumerate(out_refs):
                out_ref[tower, j] = moved[k * span : (k + 1) * span, :]


def select(me, extra, grads, groups):
    lines = len(grads)
    emb = grads[0].shape[1]
    span = EXPERTS * CAP // groups
    return pl.pallas_call(
        functools.partial(select_kernel, lines=lines),
        in_specs=[SCALARS] + [WHOLE] * (1 + lines),
        out_specs=[WHOLE] * groups,
        out_shape=[jax.ShapeDtypeStruct((2, lines, span, emb), BF16)] * groups,
        cost_estimate=SMALL,
    )(me, extra, *grads)


def outer_kernel(order_ref, *refs, groups):
    hidden_refs, grad_refs, out_ref = refs[:groups], refs[groups:-1], refs[-1]
    lines = grad_refs[0].shape[1]
    for e in range(out_ref.shape[0]):
        here = slice(e * CAP, (e + 1) * CAP)
        left, right = [], []
        for index, grad_ref in enumerate(grad_refs):
            for j in range(lines):
                block = order_ref[index // groups * lines + j]
                left.append(hidden_refs[index % groups][block, here, :])
                right.append(grad_ref[0, j, here, :])
        out_ref[e] = mm(jnp.concatenate(left), jnp.concatenate(right), 0, 0)


def outer(order, hidden, grad, tower):
    blocks, span, width = hidden[0].shape
    _, lines, _, emb = grad[0].shape
    groups, own = len(hidden), span // CAP
    one = pl.BlockSpec((1, lines, span, emb), lambda _: (tower, 0, 0, 0))
    return pl.pallas_call(
        functools.partial(outer_kernel, groups=groups),
        grid=(1,),
        in_specs=[SCALARS]
        + [pl.BlockSpec((blocks, span, width), lambda _: (0, 0, 0))] * groups
        + [one] * len(grad),
        out_specs=pl.BlockSpec((own, width, emb), lambda _: (0, 0, 0)),
        out_shape=jax.ShapeDtypeStruct((own, width, emb), F32),
        compiler_params=pltpu.CompilerParams(vmem_limit_bytes=40 * MIB),
        cost_estimate=SMALL,
    )(order, *hidden, *grad)


def shards(user_emb, item_emb, user_hidden, item_hidden, user_expert, item_expert, positive):
    rows, emb = user_emb.shape
    groups = lax.axis_size("user")
    parts = lax.axis_size("item")
    lines = parts // CORES
    me = lax.axis_index("user").astype(jnp.int32)
    part = lax.axis_index("item").astype(jnp.int32)
    others = me ^ jnp.arange(groups, dtype=jnp.int32)
    both = part ^ jnp.arange(CORES, dtype=jnp.int32)
    order = (both[:, None] ^ (CORES * jnp.arange(lines, dtype=jnp.int32))[None, :]).reshape(-1)
    first_cross = (order * groups + me) * rows
    first_plane = (part * groups + others) * rows
    me = jnp.stack([me, part])

    def by_part(blocks):
        return lax.all_to_all(blocks, "item", split_axis=0, concat_axis=0, tiled=True)

    def across(pieces):
        return pieces + [swap(piece, "item", 1) for piece in pieces]

    early = groups // 2 + 1

    def late(pieces):
        return [swap(piece, "user", early + k) for k, piece in enumerate(pieces)]

    packed = pack(user_emb, item_emb, positive, user_expert, item_expert)
    line = exchange([packed] * lines, "item", CORES)
    plane = exchange([packed] * early, "user")
    item_blocks = cut(item_hidden, packed, parts)
    user_blocks = cut(user_hidden, packed, parts)
    (item_blocks, again), plane = tie([item_blocks, packed], plane)
    plane += late([again] * (groups - early))
    item_cols = by_part(item_blocks)
    (line,) = tie(line)
    plane, cross = tie(plane, across(line))

    found = exchange([stats(first_cross, plane, cross)] * groups, "user")
    level, loss = levels(found)
    (level,), found = tie([level], found)
    level = exchange([level] * lines, "item", CORES)
    user_parts = user_grads(first_cross, plane, cross, found)
    user_parts, level = tie(user_parts, level)
    (level,) = tie(across(level))
    user_pieces = exchange(user_parts, "user")
    item_parts, extra = item_grads(first_plane, cross, plane, level)
    item_pieces = exchange(item_parts[:early], "user")
    (item_cols, user_blocks, extra), = tie([item_cols, user_blocks, extra])
    user_cols = by_part(user_blocks)
    item_slots = slot_hidden(me, item_cols, rows, groups, 1)
    user_pieces, item_parts, item_slots = tie(user_pieces, item_parts[early:], item_slots)
    item_pieces, item_slots = tie(item_pieces + late(item_parts), item_slots)

    both = exchange([total(user_pieces, item_pieces)] * lines, "item", CORES)
    item_rows = exchange(item_slots[:early], "user")
    (user_cols,), item_slots, item_rows = tie([user_cols], item_slots[early:], item_rows)
    item_rows += late(item_slots)
    user_slots = slot_hidden(me, user_cols, rows, groups, 0)
    user_rows = exchange(user_slots[:2], "user")
    both, user_slots, item_rows = tie(both, user_slots, item_rows)

    chosen = exchange(select(me, extra, both, groups), "user")
    user_rows += [swap(user_slots[k], "user", k) for k in range(2, early)]
    open_rows, user_slots = tie(user_rows[1:2], user_slots[early:])
    user_rows[1:2] = open_rows
    user_rows += late(user_slots)
    (chosen,) = tie(chosen)
    grad = across(chosen)
    item_weight_grad = outer(order, item_rows, grad, 1)
    user_weight_grad = outer(order, user_rows, grad, 0)
    row_loss = loss[0]
    return (row_loss, user_weight_grad, item_weight_grad)


def solution(mesh):
    placed = (
        P(("user", "item"), None),
        P(("item", "user"), None),
        P(("user", "item"), None),
        P(("item", "user"), None),
        P(("user", "item"), None),
        P(("item", "user"), None),
        P(("user", "item")),
    )
    return jax.shard_map(
        shards,
        mesh=mesh,
        in_specs=placed,
        out_specs=(P(("user", "item")), P("user", "item", None), P("user", "item", None)),
        check_vma=False,
    )
```

```python
import functools
import math

import jax
import jax.numpy as jnp
from jax import lax
from jax.experimental import pallas as pl
from jax.experimental.pallas import tpu as pltpu
from jax.sharding import PartitionSpec as P

EMB = 256
EXPERTS = 32
CAP = 16
SCALE = 1.0 / math.sqrt(EMB)
EXTRA = 16
DIGIT = 128
MIB = 1 << 20

F32 = jnp.float32
BF16 = jnp.bfloat16
CORES = 2
SCALARS = pl.BlockSpec(memory_space=pltpu.SMEM)
WHOLE = pl.BlockSpec(memory_space=pltpu.VMEM)
ANYWHERE = pl.BlockSpec(memory_space=pl.ANY)
SMALL = pl.CostEstimate(flops=1024, bytes_accessed=1024, transcendentals=0)


def mm(a, b, ca, cb):
    return lax.dot_general(a, b, (((ca,), (cb,)), ((), ())), preferred_element_type=F32)


def number(rows, index):
    rows = rows.astype(F32)
    high = rows[2 * index : 2 * index + 1]
    return (high * DIGIT + rows[2 * index + 1 : 2 * index + 2]).astype(jnp.int32)


def swap(piece, axis, bits):
    size = lax.axis_size(axis)
    return lax.ppermute(piece, axis, [(j, j ^ bits) for j in range(size)])


def exchange(pieces, axis, unit=1):
    return [piece if k == 0 else swap(piece, axis, k * unit) for k, piece in enumerate(pieces)]


def pack_kernel(emb_ref, positive_ref, user_ref, item_ref, out_ref, target_ref):
    rows = emb_ref.shape[0]
    down = lax.broadcasted_iota(jnp.int32, (rows, rows), 0)
    across = lax.broadcasted_iota(jnp.int32, (rows, rows), 1)

    def slots(expert):
        wide = jnp.broadcast_to(expert.astype(F32), (rows, rows))
        before = jnp.where((wide == wide.T) & (down < across), 1.0, 0.0)
        return expert * CAP + jnp.sum(before, axis=0, keepdims=True).astype(jnp.int32)

    user = slots(user_ref[...])
    item = slots(item_ref[...])
    target_ref[0:1, :] = user
    target_ref[1:2, :] = item
    line = lax.broadcasted_iota(jnp.int32, (EXTRA, rows), 0)
    block = jnp.zeros((EXTRA, rows), jnp.int32)
    for index, values in enumerate((positive_ref[...], user, item)):
        block = jnp.where(line == 2 * index, values // DIGIT, block)
        block = jnp.where(line == 2 * index + 1, values % DIGIT, block)
    out_ref[:rows, :] = emb_ref[...]
    out_ref[rows:, :] = block.astype(F32).astype(BF16)


def pack(emb, positive, user_expert, item_expert):
    rows, width = emb.shape
    return pl.pallas_call(
        pack_kernel,
        out_shape=[
            jax.ShapeDtypeStruct((rows + EXTRA, width), BF16),
            jax.ShapeDtypeStruct((2, rows), jnp.int32),
        ],
        cost_estimate=SMALL,
    )(emb, positive.reshape(1, rows), user_expert.reshape(1, rows), item_expert.reshape(1, rows))


def stats_kernel(first_ref, users_ref, *refs, rows, chunk):
    *items_refs, _, out_ref, s_ref = refs
    own = items_refs[0].shape[0]
    n_cols = own * len(items_refs)
    for half in range(users_ref.shape[0]):
        queries = users_ref[half, :rows, :] * jnp.asarray(SCALE, BF16)
        for k, items_ref in enumerate(items_refs):
            s_ref[half, k * own : (k + 1) * own, :] = mm(items_ref[...], queries, 1, 1)
        positive = number(users_ref[half, rows:, :], 0)
        tops = jnp.full((8, rows), -jnp.inf, F32)
        for c in range(0, n_cols, chunk):
            part = s_ref[half, c : c + chunk, :]
            tops = jnp.maximum(tops, jnp.max(part.reshape(chunk // 8, 8, rows), axis=0))
        top = jnp.max(tops, axis=0, keepdims=True)
        total = jnp.zeros((8, rows), F32)
        picked = jnp.zeros((8, rows), F32)
        for c in range(0, n_cols, chunk):
            part = s_ref[half, c : c + chunk, :]
            probs = jnp.exp(part - top)
            total = total + jnp.sum(probs.reshape(chunk // 8, 8, rows), axis=0)
            wanted = positive - (first_ref[c // own] + c % own)
            hit = lax.broadcasted_iota(jnp.int32, (chunk, rows), 0) == wanted
            chosen = jnp.where(hit, part, 0.0)
            picked = picked + jnp.sum(chosen.reshape(chunk // 8, 8, rows), axis=0)
        here = pl.ds(half * rows, rows)
        out_ref[0:1, here] = top
        out_ref[1:2, here] = jnp.sum(total, axis=0, keepdims=True)
        out_ref[2:3, here] = jnp.sum(picked, axis=0, keepdims=True)


def stats(first, users, items, rows, after):
    blocks, height, emb = users.shape
    own = items[0].shape[0]
    n_cols = own * len(items)
    pair = 2
    return pl.pallas_call(
        functools.partial(stats_kernel, rows=rows, chunk=64),
        grid=(blocks // pair,),
        in_specs=[SCALARS, pl.BlockSpec((pair, height, emb), lambda b: (b, 0, 0))]
        + [pl.BlockSpec((own, emb), lambda b: (0, 0))] * len(items)
        + [ANYWHERE],
        out_specs=pl.BlockSpec((3, pair * rows), lambda b: (0, b)),
        out_shape=jax.ShapeDtypeStruct((3, blocks * rows), F32),
        scratch_shapes=[pltpu.VMEM((pair, n_cols, rows), F32)],
        compiler_params=pltpu.CompilerParams(vmem_limit_bytes=40 * MIB),
        cost_estimate=SMALL,
    )(first, users, *items, after)


def grad_kernel(first_ref, users_ref, *refs, rows, chunk, count, groups):
    stats_refs, refs = refs[:groups], refs[groups:]
    items_refs, refs = refs[:count], refs[count + 1 :]
    loss_ref, user_ref = refs[:2]
    part_refs = refs[2 : count + 2]
    s_ref, g_ref, flip_ref = refs[count + 2 :]
    own = items_refs[0].shape[0]
    n_cols = own * count
    step = pl.program_id(0)

    @pl.when(step == 0)
    def _():
        for k in range(count):
            flip_ref[:, k * own : (k + 1) * own] = items_refs[k][...].T
            part_refs[k][...] = jnp.zeros_like(part_refs[k])

    for half in range(users_ref.shape[0]):
        here = pl.ds(half * rows, rows)
        queries = users_ref[half, :rows, :]
        scaled = queries * jnp.asarray(SCALE, BF16)
        for k in range(count):
            s_ref[half, k * own : (k + 1) * own, :] = mm(items_refs[k][...], scaled, 1, 1)
        positive = number(users_ref[half, rows:, :], 0)
        top = functools.reduce(jnp.maximum, [ref[0:1, here] for ref in stats_refs])
        total = sum(ref[1:2, here] * jnp.exp(ref[0:1, here] - top) for ref in stats_refs)
        level = top + jnp.log(total)
        loss_ref[0:1, here] = level - sum(ref[2:3, here] for ref in stats_refs)
        for c in range(0, n_cols, chunk):
            probs = jnp.exp(s_ref[half, c : c + chunk, :] - level)
            wanted = positive - (first_ref[c // own] + c % own)
            hit = lax.broadcasted_iota(jnp.int32, (chunk, rows), 0) == wanted
            g_ref[half, c : c + chunk, :] = jnp.where(hit, probs - 1.0, probs).astype(BF16)
        for k in range(count):
            part_refs[k][...] += mm(g_ref[half, k * own : (k + 1) * own, :], queries, 1, 0)
        user_ref[here, :] = mm(flip_ref[...], g_ref[half], 1, 0).T * SCALE

    @pl.when(step == pl.num_programs(0) - 1)
    def _():
        for k in range(count):
            part_refs[k][...] = part_refs[k][...] * SCALE


def grads(first, users, items, gathered, rows, after):
    blocks, height, emb = users.shape
    count = len(items)
    own = items[0].shape[0]
    n_cols = own * count
    pair = 2
    groups = len(gathered)
    results = pl.pallas_call(
        functools.partial(grad_kernel, rows=rows, chunk=64, count=count, groups=groups),
        grid=(blocks // pair,),
        in_specs=[
            SCALARS,
            pl.BlockSpec((pair, height, emb), lambda b: (b, 0, 0)),
        ]
        + [pl.BlockSpec((3, pair * rows), lambda b: (0, b))] * groups
        + [pl.BlockSpec((own, emb), lambda b: (0, 0))] * count
        + [ANYWHERE],
        out_specs=[
            pl.BlockSpec((1, pair * rows), lambda b: (0, b)),
            pl.BlockSpec((pair * rows, emb), lambda b: (b, 0)),
        ]
        + [pl.BlockSpec((own, emb), lambda b: (0, 0))] * count,
        out_shape=[
            jax.ShapeDtypeStruct((1, blocks * rows), F32),
            jax.ShapeDtypeStruct((blocks * rows, emb), F32),
        ]
        + [jax.ShapeDtypeStruct((own, emb), F32)] * count,
        scratch_shapes=[
            pltpu.VMEM((pair, n_cols, rows), F32),
            pltpu.VMEM((pair, n_cols, rows), BF16),
            pltpu.VMEM((emb, n_cols), BF16),
        ],
        compiler_params=pltpu.CompilerParams(vmem_limit_bytes=48 * MIB),
        cost_estimate=SMALL,
    )(first, users, *gathered, *items, after)
    return results[0], results[1], results[2:]


def cut_kernel(user_ref, item_ref, _, out_ref):
    rows = user_ref.shape[0]
    width = out_ref.shape[2]
    for k in range(out_ref.shape[0]):
        out_ref[k, :rows, :] = user_ref[:, k * width : (k + 1) * width]
        out_ref[k, rows:, :] = item_ref[:, k * width : (k + 1) * width]


def cut(user_hidden, item_hidden, parts, after):
    rows, total = user_hidden.shape
    return pl.pallas_call(
        cut_kernel,
        in_specs=[WHOLE] * 2 + [ANYWHERE],
        out_specs=WHOLE,
        out_shape=jax.ShapeDtypeStruct((parts, 2 * rows, total // parts), BF16),
        compiler_params=pltpu.CompilerParams(vmem_limit_bytes=24 * MIB),
        cost_estimate=SMALL,
    )(user_hidden, item_hidden, after)


def onehot_of(target, me, groups):
    span = EXPERTS * CAP // groups
    place = lax.broadcasted_iota(jnp.int32, (EXPERTS * CAP, target.shape[1]), 0)
    place = (((place // span) ^ me) * span) + place % span
    return (place == target).astype(F32).astype(BF16)


def hidden_kernel(me_ref, users_ref, hidden_ref, _, *out_refs):
    rows = users_ref.shape[2]
    _, pair, span, _ = out_refs[0].shape
    for half in range(pair):
        for tower in range(2):
            onehot = onehot_of(number(users_ref[half], 1 + tower), me_ref[0], len(out_refs))
            values = hidden_ref[half, tower * rows : (tower + 1) * rows, :]
            moved = mm(onehot, values, 1, 0).astype(BF16)
            for k, out_ref in enumerate(out_refs):
                out_ref[tower, half] = moved[k * span : (k + 1) * span, :]


def slot_hidden(me, users, hidden, groups, after):
    blocks, height, rows = users.shape
    width = hidden.shape[2]
    span = EXPERTS * CAP // groups
    pair = 2
    return pl.pallas_call(
        hidden_kernel,
        grid=(blocks // pair,),
        in_specs=[
            SCALARS,
            pl.BlockSpec((pair, EXTRA, rows), lambda b: (b, rows // EXTRA, 0)),
            pl.BlockSpec((pair, 2 * rows, width), lambda b: (b, 0, 0)),
            ANYWHERE,
        ],
        out_specs=[pl.BlockSpec((2, pair, span, width), lambda b: (0, b, 0, 0))] * groups,
        out_shape=[jax.ShapeDtypeStruct((2, blocks, span, width), BF16)] * groups,
        cost_estimate=SMALL,
    )(me, users, hidden, after)


def route_kernel(me_ref, target_ref, *refs, tower, count):
    total = refs[0][...]
    for ref in refs[1:count]:
        total = total + ref[...]
    low = total.astype(BF16)
    out_refs = refs[count + 1 :]
    span = out_refs[0].shape[0]
    onehot = onehot_of(target_ref[tower : tower + 1, :], me_ref[0], len(out_refs))
    moved = mm(onehot, low, 1, 0).astype(BF16)
    for k, out_ref in enumerate(out_refs):
        out_ref[...] = moved[k * span : (k + 1) * span, :]


def route(me, targets, pieces, tower, groups, after):
    rows, emb = pieces[0].shape
    span = EXPERTS * CAP // groups
    return pl.pallas_call(
        functools.partial(route_kernel, tower=tower, count=len(pieces)),
        in_specs=[SCALARS] + [WHOLE] * (1 + len(pieces)) + [ANYWHERE],
        out_specs=[WHOLE] * groups,
        out_shape=[jax.ShapeDtypeStruct((span, emb), BF16)] * groups,
        cost_estimate=SMALL,
    )(me, targets, *pieces, after)


def outer_kernel(order_ref, *refs, groups):
    hidden_refs, grad_refs, out_ref = refs[:groups], refs[groups:-1], refs[-1]
    _, blocks, span, width = hidden_refs[0].shape
    for e in range(span // CAP):
        here = slice(e * CAP, (e + 1) * CAP)
        left, right = [], []
        for j in range(blocks):
            for k, hidden_ref in enumerate(hidden_refs):
                if len(grad_refs) == 1:
                    left.append(hidden_ref[0, j, here, :])
                    right.append(grad_refs[0][j, k, here, :])
                else:
                    left.append(hidden_ref[0, order_ref[j], here, :])
                    right.append(grad_refs[j][k, here, :])
        out_ref[e] = mm(jnp.concatenate(left), jnp.concatenate(right), 0, 0)


def outer(order, hidden, grads, tower):
    _, blocks, span, width = hidden[0].shape
    emb = grads[0].shape[-1]
    own = span // CAP
    return pl.pallas_call(
        functools.partial(outer_kernel, groups=len(hidden)),
        grid=(1,),
        in_specs=[SCALARS]
        + [pl.BlockSpec((1, blocks, span, width), lambda _: (tower, 0, 0, 0))] * len(hidden)
        + [pl.BlockSpec(g.shape, lambda _, d=g.ndim: (0,) * d) for g in grads],
        out_specs=pl.BlockSpec((own, width, emb), lambda _: (0, 0, 0)),
        out_shape=jax.ShapeDtypeStruct((own, width, emb), F32),
        compiler_params=pltpu.CompilerParams(vmem_limit_bytes=40 * MIB),
        cost_estimate=SMALL,
    )(order, *hidden, *grads)


def shards(user_emb, item_emb, user_hidden, item_hidden, user_expert, item_expert, positive):
    rows, emb = user_emb.shape
    groups = lax.axis_size("user")
    parts = lax.axis_size("item")
    width = user_hidden.shape[1] // parts
    lines = parts // CORES
    me = lax.axis_index("user").astype(jnp.int32)
    part = lax.axis_index("item").astype(jnp.int32)
    others = me ^ jnp.arange(groups, dtype=jnp.int32)
    both = part ^ jnp.arange(CORES, dtype=jnp.int32)
    order = (both[:, None] ^ (CORES * jnp.arange(lines, dtype=jnp.int32))[None, :]).reshape(-1)
    first = (part * groups + others) * rows
    me = me.reshape(1)

    packed, targets = pack(user_emb, positive, user_expert, item_expert)
    users = lax.all_gather(packed, "item", axis=0)
    items = exchange([item_emb] * groups, "user")
    cols = lax.all_to_all(
        cut(user_hidden, item_hidden, parts, packed), "item", split_axis=0, concat_axis=0, tiled=True
    )

    gathered = exchange([stats(first, users, items, rows, packed)] * parts, "item")
    losses, user_part, item_parts = grads(first, users, items, gathered, rows, cols)
    row_loss = lax.dynamic_slice_in_dim(losses[0], part * rows, rows)
    user_grad = lax.psum_scatter(user_part, "item", scatter_dimension=0, tiled=True)
    item_pieces = exchange(item_parts, "user")

    item_routed = route(me, targets, item_pieces, 1, groups, packed)
    hidden_rows = exchange(slot_hidden(me, users, cols, groups, item_routed[0]), "user")
    item_sent = jnp.stack(exchange(item_routed, "user"))
    user_routed = route(me, targets, [user_grad], 0, groups, item_sent)
    user_sent = jnp.stack(exchange(user_routed, "user"))
    item_line = exchange([item_sent] * lines, "item", CORES)
    item_cross = item_line + [swap(piece, "item", 1) for piece in item_line]
    user_all = lax.all_gather(user_sent, "item", axis=0)
    item_weight_grad = outer(order, hidden_rows, item_cross, 1)
    user_weight_grad = outer(order, hidden_rows, [user_all], 0)
    return (row_loss, user_weight_grad, item_weight_grad)


def solution(mesh):
    placed = (
        P(("user", "item"), None),
        P(("item", "user"), None),
        P(("user", "item"), None),
        P(("item", "user"), None),
        P(("user", "item"), None),
        P(("item", "user"), None),
        P(("user", "item")),
    )
    return jax.shard_map(
        shards,
        mesh=mesh,
        in_specs=placed,
        out_specs=(P(("user", "item")), P("user", "item", None), P("user", "item", None)),
        check_vma=False,
    )
```

```python
import functools
import math

import jax
import jax.numpy as jnp
from jax import lax
from jax.experimental import pallas as pl
from jax.experimental.pallas import tpu as pltpu
from jax.sharding import PartitionSpec as P

EMB = 256
EXPERTS = 32
CAP = 16
SCALE = 1.0 / math.sqrt(EMB)
EXTRA = 16
DIGIT = 128
MIB = 1 << 20

F32 = jnp.float32
BF16 = jnp.bfloat16
CORES = 2
SCALARS = pl.BlockSpec(memory_space=pltpu.SMEM)
WHOLE = pl.BlockSpec(memory_space=pltpu.VMEM)
ANYWHERE = pl.BlockSpec(memory_space=pl.ANY)
SMALL = pl.CostEstimate(flops=1024, bytes_accessed=1024, transcendentals=0)


def mm(a, b, ca, cb):
    return lax.dot_general(a, b, (((ca,), (cb,)), ((), ())), preferred_element_type=F32)


def number(rows, index):
    rows = rows.astype(F32)
    high = rows[2 * index : 2 * index + 1]
    return (high * DIGIT + rows[2 * index + 1 : 2 * index + 2]).astype(jnp.int32)


def swap(piece, axis, bits):
    size = lax.axis_size(axis)
    return lax.ppermute(piece, axis, [(j, j ^ bits) for j in range(size)])


def exchange(pieces, axis, unit=1):
    return [piece if k == 0 else swap(piece, axis, k * unit) for k, piece in enumerate(pieces)]


def pack_kernel(emb_ref, positive_ref, user_ref, item_ref, out_ref, target_ref):
    rows = emb_ref.shape[0]
    down = lax.broadcasted_iota(jnp.int32, (rows, rows), 0)
    across = lax.broadcasted_iota(jnp.int32, (rows, rows), 1)

    def slots(expert):
        wide = jnp.broadcast_to(expert.astype(F32), (rows, rows))
        before = jnp.where((wide == wide.T) & (down < across), 1.0, 0.0)
        return expert * CAP + jnp.sum(before, axis=0, keepdims=True).astype(jnp.int32)

    user = slots(user_ref[...])
    item = slots(item_ref[...])
    target_ref[0:1, :] = user
    target_ref[1:2, :] = item
    line = lax.broadcasted_iota(jnp.int32, (EXTRA, rows), 0)
    block = jnp.zeros((EXTRA, rows), jnp.int32)
    for index, values in enumerate((positive_ref[...], user, item)):
        block = jnp.where(line == 2 * index, values // DIGIT, block)
        block = jnp.where(line == 2 * index + 1, values % DIGIT, block)
    out_ref[:rows, :] = emb_ref[...]
    out_ref[rows:, :] = block.astype(F32).astype(BF16)


def pack(emb, positive, user_expert, item_expert):
    rows, width = emb.shape
    return pl.pallas_call(
        pack_kernel,
        out_shape=[
            jax.ShapeDtypeStruct((rows + EXTRA, width), BF16),
            jax.ShapeDtypeStruct((2, rows), jnp.int32),
        ],
        cost_estimate=SMALL,
    )(emb, positive.reshape(1, rows), user_expert.reshape(1, rows), item_expert.reshape(1, rows))


def stats_kernel(first_ref, users_ref, *refs, rows, chunk):
    *items_refs, _, out_ref, s_ref = refs
    own = items_refs[0].shape[0]
    n_cols = own * len(items_refs)
    for half in range(users_ref.shape[0]):
        queries = users_ref[half, :rows, :] * jnp.asarray(SCALE, BF16)
        for k, items_ref in enumerate(items_refs):
            s_ref[half, k * own : (k + 1) * own, :] = mm(items_ref[...], queries, 1, 1)
        positive = number(users_ref[half, rows:, :], 0)
        tops = jnp.full((8, rows), -jnp.inf, F32)
        for c in range(0, n_cols, chunk):
            part = s_ref[half, c : c + chunk, :]
            tops = jnp.maximum(tops, jnp.max(part.reshape(chunk // 8, 8, rows), axis=0))
        top = jnp.max(tops, axis=0, keepdims=True)
        total = jnp.zeros((8, rows), F32)
        picked = jnp.zeros((8, rows), F32)
        for c in range(0, n_cols, chunk):
            part = s_ref[half, c : c + chunk, :]
            probs = jnp.exp(part - top)
            total = total + jnp.sum(probs.reshape(chunk // 8, 8, rows), axis=0)
            wanted = positive - (first_ref[c // own] + c % own)
            hit = lax.broadcasted_iota(jnp.int32, (chunk, rows), 0) == wanted
            chosen = jnp.where(hit, part, 0.0)
            picked = picked + jnp.sum(chosen.reshape(chunk // 8, 8, rows), axis=0)
        here = pl.ds(half * rows, rows)
        out_ref[0:1, here] = top
        out_ref[1:2, here] = jnp.sum(total, axis=0, keepdims=True)
        out_ref[2:3, here] = jnp.sum(picked, axis=0, keepdims=True)


def stats(first, users, items, rows, after):
    blocks, height, emb = users.shape
    own = items[0].shape[0]
    n_cols = own * len(items)
    pair = 2
    return pl.pallas_call(
        functools.partial(stats_kernel, rows=rows, chunk=64),
        grid=(blocks // pair,),
        in_specs=[SCALARS, pl.BlockSpec((pair, height, emb), lambda b: (b, 0, 0))]
        + [pl.BlockSpec((own, emb), lambda b: (0, 0))] * len(items)
        + [ANYWHERE],
        out_specs=pl.BlockSpec((3, pair * rows), lambda b: (0, b)),
        out_shape=jax.ShapeDtypeStruct((3, blocks * rows), F32),
        scratch_shapes=[pltpu.VMEM((pair, n_cols, rows), F32)],
        compiler_params=pltpu.CompilerParams(vmem_limit_bytes=40 * MIB),
        cost_estimate=SMALL,
    )(first, users, *items, after)


def grad_kernel(first_ref, users_ref, *refs, rows, chunk, count, groups):
    stats_refs, refs = refs[:groups], refs[groups:]
    items_refs, refs = refs[:count], refs[count + 1 :]
    loss_ref, user_ref = refs[:2]
    part_refs = refs[2 : count + 2]
    s_ref, g_ref, flip_ref = refs[count + 2 :]
    own = items_refs[0].shape[0]
    n_cols = own * count
    step = pl.program_id(0)

    @pl.when(step == 0)
    def _():
        for k in range(count):
            flip_ref[:, k * own : (k + 1) * own] = items_refs[k][...].T
            part_refs[k][...] = jnp.zeros_like(part_refs[k])

    for half in range(users_ref.shape[0]):
        here = pl.ds(half * rows, rows)
        queries = users_ref[half, :rows, :]
        scaled = queries * jnp.asarray(SCALE, BF16)
        for k in range(count):
            s_ref[half, k * own : (k + 1) * own, :] = mm(items_refs[k][...], scaled, 1, 1)
        positive = number(users_ref[half, rows:, :], 0)
        top = functools.reduce(jnp.maximum, [ref[0:1, here] for ref in stats_refs])
        total = sum(ref[1:2, here] * jnp.exp(ref[0:1, here] - top) for ref in stats_refs)
        level = top + jnp.log(total)
        loss_ref[0:1, here] = level - sum(ref[2:3, here] for ref in stats_refs)
        for c in range(0, n_cols, chunk):
            probs = jnp.exp(s_ref[half, c : c + chunk, :] - level)
            wanted = positive - (first_ref[c // own] + c % own)
            hit = lax.broadcasted_iota(jnp.int32, (chunk, rows), 0) == wanted
            g_ref[half, c : c + chunk, :] = jnp.where(hit, probs - 1.0, probs).astype(BF16)
        for k in range(count):
            part_refs[k][...] += mm(g_ref[half, k * own : (k + 1) * own, :], queries, 1, 0)
        user_ref[here, :] = mm(flip_ref[...], g_ref[half], 1, 0).T * SCALE

    @pl.when(step == pl.num_programs(0) - 1)
    def _():
        for k in range(count):
            part_refs[k][...] = part_refs[k][...] * SCALE


def grads(first, users, items, gathered, rows, after):
    blocks, height, emb = users.shape
    count = len(items)
    own = items[0].shape[0]
    n_cols = own * count
    pair = 2
    groups = len(gathered)
    results = pl.pallas_call(
        functools.partial(grad_kernel, rows=rows, chunk=64, count=count, groups=groups),
        grid=(blocks // pair,),
        in_specs=[
            SCALARS,
            pl.BlockSpec((pair, height, emb), lambda b: (b, 0, 0)),
        ]
        + [pl.BlockSpec((3, pair * rows), lambda b: (0, b))] * groups
        + [pl.BlockSpec((own, emb), lambda b: (0, 0))] * count
        + [ANYWHERE],
        out_specs=[
            pl.BlockSpec((1, pair * rows), lambda b: (0, b)),
            pl.BlockSpec((pair * rows, emb), lambda b: (b, 0)),
        ]
        + [pl.BlockSpec((own, emb), lambda b: (0, 0))] * count,
        out_shape=[
            jax.ShapeDtypeStruct((1, blocks * rows), F32),
            jax.ShapeDtypeStruct((blocks * rows, emb), F32),
        ]
        + [jax.ShapeDtypeStruct((own, emb), F32)] * count,
        scratch_shapes=[
            pltpu.VMEM((pair, n_cols, rows), F32),
            pltpu.VMEM((pair, n_cols, rows), BF16),
            pltpu.VMEM((emb, n_cols), BF16),
        ],
        compiler_params=pltpu.CompilerParams(vmem_limit_bytes=48 * MIB),
        cost_estimate=SMALL,
    )(first, users, *gathered, *items, after)
    return results[0], results[1], results[2:]


def cut_kernel(user_ref, item_ref, _, out_ref):
    rows = user_ref.shape[0]
    width = out_ref.shape[2]
    for k in range(out_ref.shape[0]):
        out_ref[k, :rows, :] = user_ref[:, k * width : (k + 1) * width]
        out_ref[k, rows:, :] = item_ref[:, k * width : (k + 1) * width]


def cut(user_hidden, item_hidden, parts, after):
    rows, total = user_hidden.shape
    return pl.pallas_call(
        cut_kernel,
        in_specs=[WHOLE] * 2 + [ANYWHERE],
        out_specs=WHOLE,
        out_shape=jax.ShapeDtypeStruct((parts, 2 * rows, total // parts), BF16),
        compiler_params=pltpu.CompilerParams(vmem_limit_bytes=24 * MIB),
        cost_estimate=SMALL,
    )(user_hidden, item_hidden, after)


def onehot_of(target, me, groups):
    span = EXPERTS * CAP // groups
    place = lax.broadcasted_iota(jnp.int32, (EXPERTS * CAP, target.shape[1]), 0)
    place = (((place // span) ^ me) * span) + place % span
    return (place == target).astype(F32).astype(BF16)


def hidden_kernel(me_ref, users_ref, hidden_ref, _, *out_refs):
    rows = users_ref.shape[2]
    _, pair, span, _ = out_refs[0].shape
    for half in range(pair):
        for tower in range(2):
            onehot = onehot_of(number(users_ref[half], 1 + tower), me_ref[0], len(out_refs))
            values = hidden_ref[half, tower * rows : (tower + 1) * rows, :]
            moved = mm(onehot, values, 1, 0).astype(BF16)
            for k, out_ref in enumerate(out_refs):
                out_ref[tower, half] = moved[k * span : (k + 1) * span, :]


def slot_hidden(me, users, hidden, groups, after):
    blocks, height, rows = users.shape
    width = hidden.shape[2]
    span = EXPERTS * CAP // groups
    pair = 2
    return pl.pallas_call(
        hidden_kernel,
        grid=(blocks // pair,),
        in_specs=[
            SCALARS,
            pl.BlockSpec((pair, EXTRA, rows), lambda b: (b, rows // EXTRA, 0)),
            pl.BlockSpec((pair, 2 * rows, width), lambda b: (b, 0, 0)),
            ANYWHERE,
        ],
        out_specs=[pl.BlockSpec((2, pair, span, width), lambda b: (0, b, 0, 0))] * groups,
        out_shape=[jax.ShapeDtypeStruct((2, blocks, span, width), BF16)] * groups,
        cost_estimate=SMALL,
    )(me, users, hidden, after)


def route_kernel(me_ref, target_ref, *refs, tower, count, order):
    total = refs[0][...]
    for ref in refs[1:count]:
        total = total + ref[...]
    low = total.astype(BF16)
    out_refs = refs[count + order :]
    span = out_refs[0].shape[0]
    onehot = onehot_of(target_ref[tower : tower + 1, :], me_ref[0], len(out_refs))
    moved = mm(onehot, low, 1, 0).astype(BF16)
    for k, out_ref in enumerate(out_refs):
        out_ref[...] = moved[k * span : (k + 1) * span, :]


def route(me, targets, pieces, tower, groups, after):
    rows, emb = pieces[0].shape
    span = EXPERTS * CAP // groups
    return pl.pallas_call(
        functools.partial(route_kernel, tower=tower, count=len(pieces), order=len(after)),
        in_specs=[SCALARS] + [WHOLE] * (1 + len(pieces)) + [ANYWHERE] * len(after),
        out_specs=[WHOLE] * groups,
        out_shape=[jax.ShapeDtypeStruct((span, emb), BF16)] * groups,
        cost_estimate=SMALL,
    )(me, targets, *pieces, *after)


def stack_kernel(*refs, count):
    for k in range(count):
        refs[-1][k] = refs[k][...]


def stack(pieces, after=()):
    return pl.pallas_call(
        functools.partial(stack_kernel, count=len(pieces)),
        in_specs=[WHOLE] * len(pieces) + [ANYWHERE] * len(after),
        out_specs=WHOLE,
        out_shape=jax.ShapeDtypeStruct((len(pieces),) + pieces[0].shape, pieces[0].dtype),
        cost_estimate=SMALL,
    )(*pieces, *after)


def outer_kernel(order_ref, *refs, groups):
    hidden_refs, grad_refs, out_ref = refs[:groups], refs[groups:-1], refs[-1]
    _, blocks, span, width = hidden_refs[0].shape
    for e in range(span // CAP):
        here = slice(e * CAP, (e + 1) * CAP)
        left, right = [], []
        for j in range(blocks):
            for k, hidden_ref in enumerate(hidden_refs):
                if len(grad_refs) == 1:
                    left.append(hidden_ref[0, j, here, :])
                    right.append(grad_refs[0][j, k, here, :])
                else:
                    left.append(hidden_ref[0, order_ref[j], here, :])
                    right.append(grad_refs[j][k, here, :])
        out_ref[e] = mm(jnp.concatenate(left), jnp.concatenate(right), 0, 0)


def outer(order, hidden, grads, tower):
    _, blocks, span, width = hidden[0].shape
    emb = grads[0].shape[-1]
    own = span // CAP
    return pl.pallas_call(
        functools.partial(outer_kernel, groups=len(hidden)),
        grid=(1,),
        in_specs=[SCALARS]
        + [pl.BlockSpec((1, blocks, span, width), lambda _: (tower, 0, 0, 0))] * len(hidden)
        + [pl.BlockSpec(g.shape, lambda _, d=g.ndim: (0,) * d) for g in grads],
        out_specs=pl.BlockSpec((own, width, emb), lambda _: (0, 0, 0)),
        out_shape=jax.ShapeDtypeStruct((own, width, emb), F32),
        compiler_params=pltpu.CompilerParams(vmem_limit_bytes=40 * MIB),
        cost_estimate=SMALL,
    )(order, *hidden, *grads)


def shards(user_emb, item_emb, user_hidden, item_hidden, user_expert, item_expert, positive):
    rows, emb = user_emb.shape
    groups = lax.axis_size("user")
    parts = lax.axis_size("item")
    width = user_hidden.shape[1] // parts
    lines = parts // CORES
    me = lax.axis_index("user").astype(jnp.int32)
    part = lax.axis_index("item").astype(jnp.int32)
    others = me ^ jnp.arange(groups, dtype=jnp.int32)
    both = part ^ jnp.arange(CORES, dtype=jnp.int32)
    order = (both[:, None] ^ (CORES * jnp.arange(lines, dtype=jnp.int32))[None, :]).reshape(-1)
    first = (part * groups + others) * rows
    me = me.reshape(1)

    packed, targets = pack(user_emb, positive, user_expert, item_expert)
    users = lax.all_gather(packed, "item", axis=0)
    items = exchange([item_emb] * groups, "user")
    cols = lax.all_to_all(
        cut(user_hidden, item_hidden, parts, packed), "item", split_axis=0, concat_axis=0, tiled=True
    )

    gathered = exchange([stats(first, users, items, rows, packed)] * parts, "item")
    losses, user_part, item_parts = grads(first, users, items, gathered, rows, cols)
    row_loss = lax.dynamic_slice_in_dim(losses[0], part * rows, rows)
    user_grad = lax.psum_scatter(user_part, "item", scatter_dimension=0, tiled=True)
    item_pieces = exchange(item_parts, "user")

    hidden_slots = slot_hidden(me, users, cols, groups, item_parts[0])
    hidden_rows = exchange(hidden_slots, "user")
    item_routed = route(me, targets, item_pieces, 1, groups, hidden_slots[:1])
    item_sent = stack(exchange(item_routed, "user"))
    item_line = exchange([item_sent] * lines, "item", CORES)
    user_routed = route(me, targets, [user_grad], 0, groups, [item_sent] + hidden_rows[1:3])
    user_sent = stack(exchange(user_routed, "user"), item_line[1:3])
    item_cross = item_line + [swap(piece, "item", 1) for piece in item_line]
    user_all = lax.all_gather(user_sent, "item", axis=0)
    item_weight_grad = outer(order, hidden_rows, item_cross, 1)
    user_weight_grad = outer(order, hidden_rows, [user_all], 0)
    return (row_loss, user_weight_grad, item_weight_grad)


def solution(mesh):
    placed = (
        P(("user", "item"), None),
        P(("item", "user"), None),
        P(("user", "item"), None),
        P(("item", "user"), None),
        P(("user", "item"), None),
        P(("item", "user"), None),
        P(("user", "item")),
    )
    return jax.shard_map(
        shards,
        mesh=mesh,
        in_specs=placed,
        out_specs=(P(("user", "item")), P("user", "item", None), P("user", "item", None)),
        check_vma=False,
    )
```

```python
import functools
import math

import jax
import jax.numpy as jnp
from jax import lax
from jax.experimental import pallas as pl
from jax.experimental.pallas import tpu as pltpu
from jax.sharding import PartitionSpec as P

EMB = 256
EXPERTS = 32
CAP = 16
SCALE = 1.0 / math.sqrt(EMB)
EXTRA = 16
DIGIT = 128
MIB = 1 << 20

F32 = jnp.float32
BF16 = jnp.bfloat16
CORES = 2
SCALARS = pl.BlockSpec(memory_space=pltpu.SMEM)
WHOLE = pl.BlockSpec(memory_space=pltpu.VMEM)
ANYWHERE = pl.BlockSpec(memory_space=pl.ANY)
SMALL = pl.CostEstimate(flops=1024, bytes_accessed=1024, transcendentals=0)


def mm(a, b, ca, cb):
    return lax.dot_general(a, b, (((ca,), (cb,)), ((), ())), preferred_element_type=F32)


def number(rows, index):
    rows = rows.astype(F32)
    high = rows[2 * index : 2 * index + 1]
    return (high * DIGIT + rows[2 * index + 1 : 2 * index + 2]).astype(jnp.int32)


def swap(piece, axis, bits):
    size = lax.axis_size(axis)
    return lax.ppermute(piece, axis, [(j, j ^ bits) for j in range(size)])


def exchange(pieces, axis, unit=1):
    return [piece if k == 0 else swap(piece, axis, k * unit) for k, piece in enumerate(pieces)]


def pack_kernel(emb_ref, positive_ref, user_ref, item_ref, out_ref, target_ref):
    rows = emb_ref.shape[0]
    down = lax.broadcasted_iota(jnp.int32, (rows, rows), 0)
    across = lax.broadcasted_iota(jnp.int32, (rows, rows), 1)

    def slots(expert):
        wide = jnp.broadcast_to(expert.astype(F32), (rows, rows))
        before = jnp.where((wide == wide.T) & (down < across), 1.0, 0.0)
        return expert * CAP + jnp.sum(before, axis=0, keepdims=True).astype(jnp.int32)

    user = slots(user_ref[...])
    item = slots(item_ref[...])
    target_ref[0:1, :] = user
    target_ref[1:2, :] = item
    line = lax.broadcasted_iota(jnp.int32, (EXTRA, rows), 0)
    block = jnp.zeros((EXTRA, rows), jnp.int32)
    for index, values in enumerate((positive_ref[...], user, item)):
        block = jnp.where(line == 2 * index, values // DIGIT, block)
        block = jnp.where(line == 2 * index + 1, values % DIGIT, block)
    out_ref[:rows, :] = emb_ref[...]
    out_ref[rows:, :] = block.astype(F32).astype(BF16)


def pack(emb, positive, user_expert, item_expert):
    rows, width = emb.shape
    return pl.pallas_call(
        pack_kernel,
        out_shape=[
            jax.ShapeDtypeStruct((rows + EXTRA, width), BF16),
            jax.ShapeDtypeStruct((2, rows), jnp.int32),
        ],
        cost_estimate=SMALL,
    )(emb, positive.reshape(1, rows), user_expert.reshape(1, rows), item_expert.reshape(1, rows))


def stats_kernel(first_ref, users_ref, *refs, rows, chunk):
    *items_refs, _, out_ref, s_ref = refs
    own = items_refs[0].shape[0]
    n_cols = own * len(items_refs)
    for half in range(users_ref.shape[0]):
        queries = users_ref[half, :rows, :] * jnp.asarray(SCALE, BF16)
        for k, items_ref in enumerate(items_refs):
            s_ref[half, k * own : (k + 1) * own, :] = mm(items_ref[...], queries, 1, 1)
        positive = number(users_ref[half, rows:, :], 0)
        tops = jnp.full((8, rows), -jnp.inf, F32)
        for c in range(0, n_cols, chunk):
            part = s_ref[half, c : c + chunk, :]
            tops = jnp.maximum(tops, jnp.max(part.reshape(chunk // 8, 8, rows), axis=0))
        top = jnp.max(tops, axis=0, keepdims=True)
        total = jnp.zeros((8, rows), F32)
        picked = jnp.zeros((8, rows), F32)
        for c in range(0, n_cols, chunk):
            part = s_ref[half, c : c + chunk, :]
            probs = jnp.exp(part - top)
            total = total + jnp.sum(probs.reshape(chunk // 8, 8, rows), axis=0)
            wanted = positive - (first_ref[c // own] + c % own)
            hit = lax.broadcasted_iota(jnp.int32, (chunk, rows), 0) == wanted
            chosen = jnp.where(hit, part, 0.0)
            picked = picked + jnp.sum(chosen.reshape(chunk // 8, 8, rows), axis=0)
        here = pl.ds(half * rows, rows)
        out_ref[0:1, here] = top
        out_ref[1:2, here] = jnp.sum(total, axis=0, keepdims=True)
        out_ref[2:3, here] = jnp.sum(picked, axis=0, keepdims=True)


def stats(first, users, items, rows, after):
    blocks, height, emb = users.shape
    own = items[0].shape[0]
    n_cols = own * len(items)
    pair = 2
    return pl.pallas_call(
        functools.partial(stats_kernel, rows=rows, chunk=64),
        grid=(blocks // pair,),
        in_specs=[SCALARS, pl.BlockSpec((pair, height, emb), lambda b: (b, 0, 0))]
        + [pl.BlockSpec((own, emb), lambda b: (0, 0))] * len(items)
        + [ANYWHERE],
        out_specs=pl.BlockSpec((3, pair * rows), lambda b: (0, b)),
        out_shape=jax.ShapeDtypeStruct((3, blocks * rows), F32),
        scratch_shapes=[pltpu.VMEM((pair, n_cols, rows), F32)],
        compiler_params=pltpu.CompilerParams(vmem_limit_bytes=40 * MIB),
        cost_estimate=SMALL,
    )(first, users, *items, after)


def grad_kernel(first_ref, users_ref, *refs, rows, chunk, count, groups):
    stats_refs, refs = refs[:groups], refs[groups:]
    items_refs, refs = refs[:count], refs[count + 1 :]
    loss_ref, user_ref = refs[:2]
    part_refs = refs[2 : count + 2]
    s_ref, g_ref, flip_ref = refs[count + 2 :]
    own = items_refs[0].shape[0]
    n_cols = own * count
    step = pl.program_id(0)

    @pl.when(step == 0)
    def _():
        for k in range(count):
            flip_ref[:, k * own : (k + 1) * own] = items_refs[k][...].T
            part_refs[k][...] = jnp.zeros_like(part_refs[k])

    for half in range(users_ref.shape[0]):
        here = pl.ds(half * rows, rows)
        queries = users_ref[half, :rows, :]
        scaled = queries * jnp.asarray(SCALE, BF16)
        for k in range(count):
            s_ref[half, k * own : (k + 1) * own, :] = mm(items_refs[k][...], scaled, 1, 1)
        positive = number(users_ref[half, rows:, :], 0)
        top = functools.reduce(jnp.maximum, [ref[0:1, here] for ref in stats_refs])
        total = sum(ref[1:2, here] * jnp.exp(ref[0:1, here] - top) for ref in stats_refs)
        level = top + jnp.log(total)
        loss_ref[0:1, here] = level - sum(ref[2:3, here] for ref in stats_refs)
        for c in range(0, n_cols, chunk):
            probs = jnp.exp(s_ref[half, c : c + chunk, :] - level)
            wanted = positive - (first_ref[c // own] + c % own)
            hit = lax.broadcasted_iota(jnp.int32, (chunk, rows), 0) == wanted
            g_ref[half, c : c + chunk, :] = jnp.where(hit, probs - 1.0, probs).astype(BF16)
        for k in range(count):
            part_refs[k][...] += mm(g_ref[half, k * own : (k + 1) * own, :], queries, 1, 0)
        user_ref[here, :] = mm(flip_ref[...], g_ref[half], 1, 0).T * SCALE

    @pl.when(step == pl.num_programs(0) - 1)
    def _():
        for k in range(count):
            part_refs[k][...] = part_refs[k][...] * SCALE


def grads(first, users, items, gathered, rows, after):
    blocks, height, emb = users.shape
    count = len(items)
    own = items[0].shape[0]
    n_cols = own * count
    pair = 2
    groups = len(gathered)
    results = pl.pallas_call(
        functools.partial(grad_kernel, rows=rows, chunk=64, count=count, groups=groups),
        grid=(blocks // pair,),
        in_specs=[
            SCALARS,
            pl.BlockSpec((pair, height, emb), lambda b: (b, 0, 0)),
        ]
        + [pl.BlockSpec((3, pair * rows), lambda b: (0, b))] * groups
        + [pl.BlockSpec((own, emb), lambda b: (0, 0))] * count
        + [ANYWHERE],
        out_specs=[
            pl.BlockSpec((1, pair * rows), lambda b: (0, b)),
            pl.BlockSpec((pair * rows, emb), lambda b: (b, 0)),
        ]
        + [pl.BlockSpec((own, emb), lambda b: (0, 0))] * count,
        out_shape=[
            jax.ShapeDtypeStruct((1, blocks * rows), F32),
            jax.ShapeDtypeStruct((blocks * rows, emb), F32),
        ]
        + [jax.ShapeDtypeStruct((own, emb), F32)] * count,
        scratch_shapes=[
            pltpu.VMEM((pair, n_cols, rows), F32),
            pltpu.VMEM((pair, n_cols, rows), BF16),
            pltpu.VMEM((emb, n_cols), BF16),
        ],
        compiler_params=pltpu.CompilerParams(vmem_limit_bytes=48 * MIB),
        cost_estimate=SMALL,
    )(first, users, *gathered, *items, after)
    return results[0], results[1], results[2:]


def cut_kernel(in_ref, _, out_ref):
    width = out_ref.shape[2]
    for k in range(out_ref.shape[0]):
        out_ref[k] = in_ref[:, k * width : (k + 1) * width]


def cut(hidden, parts, after):
    rows, total = hidden.shape
    return pl.pallas_call(
        cut_kernel,
        in_specs=[WHOLE, ANYWHERE],
        out_specs=WHOLE,
        out_shape=jax.ShapeDtypeStruct((parts, rows, total // parts), BF16),
        compiler_params=pltpu.CompilerParams(vmem_limit_bytes=24 * MIB),
        cost_estimate=SMALL,
    )(hidden, after)


def onehot_of(target, me, groups):
    span = EXPERTS * CAP // groups
    place = lax.broadcasted_iota(jnp.int32, (EXPERTS * CAP, target.shape[1]), 0)
    place = (((place // span) ^ me) * span) + place % span
    return (place == target).astype(F32).astype(BF16)


def hidden_kernel(users_ref, user_ref, item_ref, _, out_ref):
    groups, _, pair, span, _ = out_ref.shape
    for half in range(pair):
        for tower, hidden_ref in enumerate((user_ref, item_ref)):
            onehot = onehot_of(number(users_ref[half], 1 + tower), 0, groups)
            moved = mm(onehot, hidden_ref[half], 1, 0).astype(BF16)
            for k in range(groups):
                out_ref[k, tower, half] = moved[k * span : (k + 1) * span, :]


def slot_hidden(users, user_hidden, item_hidden, groups, after):
    blocks, rows, width = user_hidden.shape
    span = EXPERTS * CAP // groups
    pair = 2
    half = pl.BlockSpec((pair, rows, width), lambda b: (b, 0, 0))
    return pl.pallas_call(
        hidden_kernel,
        grid=(blocks // pair,),
        in_specs=[
            pl.BlockSpec((pair, EXTRA, rows), lambda b: (b, rows // EXTRA, 0)),
            half,
            half,
            ANYWHERE,
        ],
        out_specs=pl.BlockSpec((groups, 2, pair, span, width), lambda b: (0, 0, b, 0, 0)),
        out_shape=jax.ShapeDtypeStruct((groups, 2, blocks, span, width), BF16),
        cost_estimate=SMALL,
    )(users, user_hidden, item_hidden, after)


def route_kernel(me_ref, target_ref, *refs, tower, count, order):
    total = refs[0][...]
    for ref in refs[1:count]:
        total = total + ref[...]
    low = total.astype(BF16)
    out_refs = refs[count + order :]
    span = out_refs[0].shape[0]
    onehot = onehot_of(target_ref[tower : tower + 1, :], me_ref[0], len(out_refs))
    moved = mm(onehot, low, 1, 0).astype(BF16)
    for k, out_ref in enumerate(out_refs):
        out_ref[...] = moved[k * span : (k + 1) * span, :]


def route(me, targets, pieces, tower, groups, after):
    rows, emb = pieces[0].shape
    span = EXPERTS * CAP // groups
    return pl.pallas_call(
        functools.partial(route_kernel, tower=tower, count=len(pieces), order=len(after)),
        in_specs=[SCALARS] + [WHOLE] * (1 + len(pieces)) + [ANYWHERE] * len(after),
        out_specs=[WHOLE] * groups,
        out_shape=[jax.ShapeDtypeStruct((span, emb), BF16)] * groups,
        cost_estimate=SMALL,
    )(me, targets, *pieces, *after)


def stack_kernel(*refs, count):
    for k in range(count):
        refs[-1][k] = refs[k][...]


def stack(pieces, after=()):
    return pl.pallas_call(
        functools.partial(stack_kernel, count=len(pieces)),
        in_specs=[WHOLE] * len(pieces) + [ANYWHERE] * len(after),
        out_specs=WHOLE,
        out_shape=jax.ShapeDtypeStruct((len(pieces),) + pieces[0].shape, pieces[0].dtype),
        cost_estimate=SMALL,
    )(*pieces, *after)


def outer_kernel(order_ref, me_ref, hidden_ref, *refs):
    grad_refs, out_ref = refs[:-1], refs[-1]
    groups, _, blocks, span, _ = hidden_ref.shape
    for e in range(span // CAP):
        here = slice(e * CAP, (e + 1) * CAP)
        left, right = [], []
        for j in range(blocks):
            for k in range(groups):
                if len(grad_refs) == 1:
                    left.append(hidden_ref[me_ref[0] ^ k, 0, j, here, :])
                    right.append(grad_refs[0][j, k, here, :])
                else:
                    left.append(hidden_ref[me_ref[0] ^ k, 0, order_ref[j], here, :])
                    right.append(grad_refs[j][k, here, :])
        out_ref[e] = mm(jnp.concatenate(left), jnp.concatenate(right), 0, 0)


def outer(order, me, hidden, grads, tower):
    groups, _, blocks, span, width = hidden.shape
    emb = grads[0].shape[-1]
    own = span // CAP
    return pl.pallas_call(
        outer_kernel,
        grid=(1,),
        in_specs=[SCALARS, SCALARS]
        + [pl.BlockSpec((groups, 1, blocks, span, width), lambda _: (0, tower, 0, 0, 0))]
        + [pl.BlockSpec(g.shape, lambda _, d=g.ndim: (0,) * d) for g in grads],
        out_specs=pl.BlockSpec((own, width, emb), lambda _: (0, 0, 0)),
        out_shape=jax.ShapeDtypeStruct((own, width, emb), F32),
        compiler_params=pltpu.CompilerParams(vmem_limit_bytes=56 * MIB),
        cost_estimate=SMALL,
    )(order, me, hidden, *grads)


def shards(user_emb, item_emb, user_hidden, item_hidden, user_expert, item_expert, positive):
    rows, emb = user_emb.shape
    groups = lax.axis_size("user")
    parts = lax.axis_size("item")
    width = user_hidden.shape[1] // parts
    lines = parts // CORES
    me = lax.axis_index("user").astype(jnp.int32)
    part = lax.axis_index("item").astype(jnp.int32)
    others = me ^ jnp.arange(groups, dtype=jnp.int32)
    both = part ^ jnp.arange(CORES, dtype=jnp.int32)
    order = (both[:, None] ^ (CORES * jnp.arange(lines, dtype=jnp.int32))[None, :]).reshape(-1)
    first = (part * groups + others) * rows
    me = me.reshape(1)

    packed, targets = pack(user_emb, positive, user_expert, item_expert)
    users = lax.all_gather(packed, "item", axis=0)
    items = exchange([item_emb] * groups, "user")

    def scatter(pieces, axis):
        return lax.all_to_all(pieces, axis, split_axis=0, concat_axis=0, tiled=True)

    user_cols = scatter(cut(user_hidden, parts, items[1]), "item")
    found = stats(first, users, items, rows, packed)
    item_cols = scatter(cut(item_hidden, parts, found), "item")
    gathered = exchange([found] * parts, "item")
    losses, user_part, item_parts = grads(first, users, items, gathered, rows, user_cols)
    row_loss = lax.dynamic_slice_in_dim(losses[0], part * rows, rows)
    user_grad = lax.psum_scatter(user_part, "item", scatter_dimension=0, tiled=True)
    item_pieces = exchange(item_parts, "user")

    item_routed = route(me, targets, item_pieces, 1, groups, [])
    item_sent = stack(exchange(item_routed, "user"))
    item_line = exchange([item_sent] * lines, "item", CORES)
    hidden_slots = slot_hidden(users, user_cols, item_cols, groups, item_sent)
    hidden_rows = scatter(hidden_slots, "user")
    user_routed = route(me, targets, [user_grad], 0, groups, [hidden_slots])
    user_sent = stack(exchange(user_routed, "user"))
    item_cross = item_line + [swap(piece, "item", 1) for piece in item_line]
    user_all = lax.all_gather(user_sent, "item", axis=0)
    item_weight_grad = outer(order, me, hidden_rows, item_cross, 1)
    user_weight_grad = outer(order, me, hidden_rows, [user_all], 0)
    return (row_loss, user_weight_grad, item_weight_grad)


def solution(mesh):
    placed = (
        P(("user", "item"), None),
        P(("item", "user"), None),
        P(("user", "item"), None),
        P(("item", "user"), None),
        P(("user", "item"), None),
        P(("item", "user"), None),
        P(("user", "item")),
    )
    return jax.shard_map(
        shards,
        mesh=mesh,
        in_specs=placed,
        out_specs=(P(("user", "item")), P("user", "item", None), P("user", "item", None)),
        check_vma=False,
    )
```

```python
import functools
import math

import jax
import jax.numpy as jnp
from jax import lax
from jax.experimental import pallas as pl
from jax.experimental.pallas import tpu as pltpu
from jax.sharding import PartitionSpec as P

EMB = 256
EXPERTS = 32
CAP = 16
SCALE = 1.0 / math.sqrt(EMB)
EXTRA = 16
DIGIT = 128
MIB = 1 << 20

F32 = jnp.float32
BF16 = jnp.bfloat16
CORES = 2
SCALARS = pl.BlockSpec(memory_space=pltpu.SMEM)
WHOLE = pl.BlockSpec(memory_space=pltpu.VMEM)
ANYWHERE = pl.BlockSpec(memory_space=pl.ANY)
VMEM = 60 * MIB
LARGE = pl.CostEstimate(flops=1 << 36, bytes_accessed=1 << 28, transcendentals=0)
SMALL = pl.CostEstimate(flops=1024, bytes_accessed=1024, transcendentals=0)


def mm(a, b, ca, cb):
    return lax.dot_general(a, b, (((ca,), (cb,)), ((), ())), preferred_element_type=F32)


def number(rows, index):
    rows = rows.astype(F32)
    high = rows[2 * index : 2 * index + 1]
    return (high * DIGIT + rows[2 * index + 1 : 2 * index + 2]).astype(jnp.int32)


def swap(piece, axis, bits):
    size = lax.axis_size(axis)
    return lax.ppermute(piece, axis, [(j, j ^ bits) for j in range(size)])


def exchange(pieces, axis, unit=1):
    return [piece if k == 0 else swap(piece, axis, k * unit) for k, piece in enumerate(pieces)]


def pack_kernel(emb_ref, positive_ref, user_ref, item_ref, out_ref, target_ref):
    rows = emb_ref.shape[0]
    down = lax.broadcasted_iota(jnp.int32, (rows, rows), 0)
    across = lax.broadcasted_iota(jnp.int32, (rows, rows), 1)

    def slots(expert):
        wide = jnp.broadcast_to(expert.astype(F32), (rows, rows))
        before = jnp.where((wide == wide.T) & (down < across), 1.0, 0.0)
        return expert * CAP + jnp.sum(before, axis=0, keepdims=True).astype(jnp.int32)

    user = slots(user_ref[...])
    item = slots(item_ref[...])
    target_ref[0:1, :] = user
    target_ref[1:2, :] = item
    line = lax.broadcasted_iota(jnp.int32, (EXTRA, rows), 0)
    block = jnp.zeros((EXTRA, rows), jnp.int32)
    for index, values in enumerate((positive_ref[...], user, item)):
        block = jnp.where(line == 2 * index, values // DIGIT, block)
        block = jnp.where(line == 2 * index + 1, values % DIGIT, block)
    out_ref[:rows, :] = emb_ref[...]
    out_ref[rows:, :] = block.astype(F32).astype(BF16)


def pack(emb, positive, user_expert, item_expert):
    rows, width = emb.shape
    return pl.pallas_call(
        pack_kernel,
        out_shape=[
            jax.ShapeDtypeStruct((rows + EXTRA, width), BF16),
            jax.ShapeDtypeStruct((2, rows), jnp.int32),
        ],
        compiler_params=pltpu.CompilerParams(vmem_limit_bytes=VMEM),
        cost_estimate=SMALL,
    )(emb, positive.reshape(1, rows), user_expert.reshape(1, rows), item_expert.reshape(1, rows))


def stats_kernel(first_ref, users_ref, *refs, rows, chunk):
    *items_refs, _, out_ref, s_ref = refs
    own = items_refs[0].shape[0]
    n_cols = own * len(items_refs)
    for half in range(users_ref.shape[0]):
        queries = users_ref[half, :rows, :] * jnp.asarray(SCALE, BF16)
        for k, items_ref in enumerate(items_refs):
            s_ref[half, k * own : (k + 1) * own, :] = mm(items_ref[...], queries, 1, 1)
        positive = number(users_ref[half, rows:, :], 0)
        tops = jnp.full((8, rows), -jnp.inf, F32)
        for c in range(0, n_cols, chunk):
            part = s_ref[half, c : c + chunk, :]
            tops = jnp.maximum(tops, jnp.max(part.reshape(chunk // 8, 8, rows), axis=0))
        top = jnp.max(tops, axis=0, keepdims=True)
        total = jnp.zeros((8, rows), F32)
        picked = jnp.zeros((8, rows), F32)
        for c in range(0, n_cols, chunk):
            part = s_ref[half, c : c + chunk, :]
            probs = jnp.exp(part - top)
            total = total + jnp.sum(probs.reshape(chunk // 8, 8, rows), axis=0)
            wanted = positive - (first_ref[c // own] + c % own)
            hit = lax.broadcasted_iota(jnp.int32, (chunk, rows), 0) == wanted
            chosen = jnp.where(hit, part, 0.0)
            picked = picked + jnp.sum(chosen.reshape(chunk // 8, 8, rows), axis=0)
        here = pl.ds(half * rows, rows)
        out_ref[0:1, here] = top
        out_ref[1:2, here] = jnp.sum(total, axis=0, keepdims=True)
        out_ref[2:3, here] = jnp.sum(picked, axis=0, keepdims=True)


def stats(first, users, items, rows, after):
    blocks, height, emb = users.shape
    own = items[0].shape[0]
    n_cols = own * len(items)
    pair = 2
    return pl.pallas_call(
        functools.partial(stats_kernel, rows=rows, chunk=64),
        grid=(blocks // pair,),
        in_specs=[SCALARS, pl.BlockSpec((pair, height, emb), lambda b: (b, 0, 0))]
        + [pl.BlockSpec((own, emb), lambda b: (0, 0))] * len(items)
        + [ANYWHERE],
        out_specs=pl.BlockSpec((3, pair * rows), lambda b: (0, b)),
        out_shape=jax.ShapeDtypeStruct((3, blocks * rows), F32),
        scratch_shapes=[pltpu.VMEM((pair, n_cols, rows), F32)],
        compiler_params=pltpu.CompilerParams(vmem_limit_bytes=VMEM),
        cost_estimate=SMALL,
    )(first, users, *items, after)


def grad_kernel(first_ref, users_ref, *refs, rows, chunk, count, groups):
    stats_refs, refs = refs[:groups], refs[groups:]
    items_refs, refs = refs[:count], refs[count + 1 :]
    loss_ref, user_ref = refs[:2]
    part_refs = refs[2 : count + 2]
    s_ref, g_ref, flip_ref = refs[count + 2 :]
    own = items_refs[0].shape[0]
    n_cols = own * count
    step = pl.program_id(0)

    @pl.when(step == 0)
    def _():
        for k in range(count):
            flip_ref[:, k * own : (k + 1) * own] = items_refs[k][...].T
            part_refs[k][...] = jnp.zeros_like(part_refs[k])

    for half in range(users_ref.shape[0]):
        here = pl.ds(half * rows, rows)
        queries = users_ref[half, :rows, :]
        scaled = queries * jnp.asarray(SCALE, BF16)
        for k in range(count):
            s_ref[half, k * own : (k + 1) * own, :] = mm(items_refs[k][...], scaled, 1, 1)
        positive = number(users_ref[half, rows:, :], 0)
        top = functools.reduce(jnp.maximum, [ref[0:1, here] for ref in stats_refs])
        total = sum(ref[1:2, here] * jnp.exp(ref[0:1, here] - top) for ref in stats_refs)
        level = top + jnp.log(total)
        loss_ref[0:1, here] = level - sum(ref[2:3, here] for ref in stats_refs)
        for c in range(0, n_cols, chunk):
            probs = jnp.exp(s_ref[half, c : c + chunk, :] - level)
            wanted = positive - (first_ref[c // own] + c % own)
            hit = lax.broadcasted_iota(jnp.int32, (chunk, rows), 0) == wanted
            g_ref[half, c : c + chunk, :] = jnp.where(hit, probs - 1.0, probs).astype(BF16)
        for k in range(count):
            part_refs[k][...] += mm(g_ref[half, k * own : (k + 1) * own, :], queries, 1, 0)
        user_ref[here, :] = mm(flip_ref[...], g_ref[half], 1, 0).T * SCALE

    @pl.when(step == pl.num_programs(0) - 1)
    def _():
        for k in range(count):
            part_refs[k][...] = part_refs[k][...] * SCALE


def grads(first, users, items, gathered, rows, after):
    blocks, height, emb = users.shape
    count = len(items)
    own = items[0].shape[0]
    n_cols = own * count
    pair = 2
    groups = len(gathered)
    results = pl.pallas_call(
        functools.partial(grad_kernel, rows=rows, chunk=64, count=count, groups=groups),
        grid=(blocks // pair,),
        in_specs=[
            SCALARS,
            pl.BlockSpec((pair, height, emb), lambda b: (b, 0, 0)),
        ]
        + [pl.BlockSpec((3, pair * rows), lambda b: (0, b))] * groups
        + [pl.BlockSpec((own, emb), lambda b: (0, 0))] * count
        + [ANYWHERE],
        out_specs=[
            pl.BlockSpec((1, pair * rows), lambda b: (0, b)),
            pl.BlockSpec((pair * rows, emb), lambda b: (b, 0)),
        ]
        + [pl.BlockSpec((own, emb), lambda b: (0, 0))] * count,
        out_shape=[
            jax.ShapeDtypeStruct((1, blocks * rows), F32),
            jax.ShapeDtypeStruct((blocks * rows, emb), F32),
        ]
        + [jax.ShapeDtypeStruct((own, emb), F32)] * count,
        scratch_shapes=[
            pltpu.VMEM((pair, n_cols, rows), F32),
            pltpu.VMEM((pair, n_cols, rows), BF16),
            pltpu.VMEM((emb, n_cols), BF16),
        ],
        compiler_params=pltpu.CompilerParams(vmem_limit_bytes=VMEM),
        cost_estimate=SMALL,
    )(first, users, *gathered, *items, after)
    return results[0], results[1], results[2:]


def cut_kernel(in_ref, _, out_ref):
    width = out_ref.shape[2]
    for k in range(out_ref.shape[0]):
        out_ref[k] = in_ref[:, k * width : (k + 1) * width]


def cut(hidden, parts, after):
    rows, total = hidden.shape
    return pl.pallas_call(
        cut_kernel,
        in_specs=[WHOLE, ANYWHERE],
        out_specs=WHOLE,
        out_shape=jax.ShapeDtypeStruct((parts, rows, total // parts), BF16),
        compiler_params=pltpu.CompilerParams(vmem_limit_bytes=VMEM),
        cost_estimate=SMALL,
    )(hidden, after)


def onehot_of(target, me, groups):
    span = EXPERTS * CAP // groups
    place = lax.broadcasted_iota(jnp.int32, (EXPERTS * CAP, target.shape[1]), 0)
    place = (((place // span) ^ me) * span) + place % span
    return (place == target).astype(F32).astype(BF16)


def hidden_kernel(me_ref, users_ref, hidden_ref, _, *out_refs, tower):
    count, (pair, span, _) = len(out_refs), out_refs[0].shape[-3:]
    groups = out_refs[0].shape[0] if count == 1 else count
    me = 0 if count == 1 else me_ref[0]
    for half in range(pair):
        onehot = onehot_of(number(users_ref[half], 1 + tower), me, groups)
        moved = mm(onehot, hidden_ref[half], 1, 0).astype(BF16)
        for k in range(groups):
            part = moved[k * span : (k + 1) * span, :]
            if count == 1:
                out_refs[0][k, half] = part
            else:
                out_refs[k][half] = part


def slot_hidden(me, users, hidden, groups, tower, apart, after):
    blocks, rows, width = hidden.shape
    span = EXPERTS * CAP // groups
    pair = 2
    if apart:
        out_specs = [pl.BlockSpec((pair, span, width), lambda b: (b, 0, 0))] * groups
        out_shape = [jax.ShapeDtypeStruct((blocks, span, width), BF16)] * groups
    else:
        out_specs = [pl.BlockSpec((groups, pair, span, width), lambda b: (0, b, 0, 0))]
        out_shape = [jax.ShapeDtypeStruct((groups, blocks, span, width), BF16)]
    return pl.pallas_call(
        functools.partial(hidden_kernel, tower=tower),
        grid=(blocks // pair,),
        in_specs=[
            SCALARS,
            pl.BlockSpec((pair, EXTRA, rows), lambda b: (b, rows // EXTRA, 0)),
            pl.BlockSpec((pair, rows, width), lambda b: (b, 0, 0)),
            ANYWHERE,
        ],
        out_specs=out_specs,
        out_shape=out_shape,
        compiler_params=pltpu.CompilerParams(vmem_limit_bytes=VMEM),
        cost_estimate=SMALL,
    )(me, users, hidden, after)


def route_kernel(me_ref, target_ref, *refs, tower, count, order):
    total = refs[0][...]
    for ref in refs[1:count]:
        total = total + ref[...]
    low = total.astype(BF16)
    out_refs = refs[count + order :]
    span = out_refs[0].shape[0]
    onehot = onehot_of(target_ref[tower : tower + 1, :], me_ref[0], len(out_refs))
    moved = mm(onehot, low, 1, 0).astype(BF16)
    for k, out_ref in enumerate(out_refs):
        out_ref[...] = moved[k * span : (k + 1) * span, :]


def route(me, targets, pieces, tower, groups, after):
    rows, emb = pieces[0].shape
    span = EXPERTS * CAP // groups
    return pl.pallas_call(
        functools.partial(route_kernel, tower=tower, count=len(pieces), order=len(after)),
        in_specs=[SCALARS] + [WHOLE] * (1 + len(pieces)) + [ANYWHERE] * len(after),
        out_specs=[WHOLE] * groups,
        out_shape=[jax.ShapeDtypeStruct((span, emb), BF16)] * groups,
        compiler_params=pltpu.CompilerParams(vmem_limit_bytes=VMEM),
        cost_estimate=SMALL,
    )(me, targets, *pieces, *after)


def stack_kernel(*refs, count):
    for k in range(count):
        refs[-1][k] = refs[k][...]


def stack(pieces, after=()):
    return pl.pallas_call(
        functools.partial(stack_kernel, count=len(pieces)),
        in_specs=[WHOLE] * len(pieces) + [ANYWHERE] * len(after),
        out_specs=WHOLE,
        out_shape=jax.ShapeDtypeStruct((len(pieces),) + pieces[0].shape, pieces[0].dtype),
        compiler_params=pltpu.CompilerParams(vmem_limit_bytes=VMEM),
        cost_estimate=SMALL,
    )(*pieces, *after)


def outer_kernel(order_ref, me_ref, *refs, count):
    hidden_refs, grad_refs, out_ref = refs[:count], refs[count:-1], refs[-1]
    blocks, span, _ = hidden_refs[0].shape[-3:]
    groups = hidden_refs[0].shape[0] if count == 1 else count
    for e in range(span // CAP):
        here = slice(e * CAP, (e + 1) * CAP)
        left, right = [], []
        for j in range(blocks):
            block = j if len(grad_refs) == 1 else order_ref[j]
            for k in range(groups):
                if count == 1:
                    left.append(hidden_refs[0][me_ref[0] ^ k, block, here, :])
                else:
                    left.append(hidden_refs[k][block, here, :])
                if len(grad_refs) == 1:
                    right.append(grad_refs[0][j, k, here, :])
                else:
                    right.append(grad_refs[j][k, here, :])
        out_ref[e] = mm(jnp.concatenate(left), jnp.concatenate(right), 0, 0)


def outer(order, me, hidden, grads, cost):
    span, width = hidden[0].shape[-2:]
    emb = grads[0].shape[-1]
    own = span // CAP
    return pl.pallas_call(
        functools.partial(outer_kernel, count=len(hidden)),
        grid=(1,),
        in_specs=[SCALARS, SCALARS]
        + [pl.BlockSpec(g.shape, lambda _, d=g.ndim: (0,) * d) for g in hidden + grads],
        out_specs=pl.BlockSpec((own, width, emb), lambda _: (0, 0, 0)),
        out_shape=jax.ShapeDtypeStruct((own, width, emb), F32),
        compiler_params=pltpu.CompilerParams(vmem_limit_bytes=VMEM),
        cost_estimate=cost,
    )(order, me, *hidden, *grads)


def shards(user_emb, item_emb, user_hidden, item_hidden, user_expert, item_expert, positive):
    rows, emb = user_emb.shape
    groups = lax.axis_size("user")
    parts = lax.axis_size("item")
    width = user_hidden.shape[1] // parts
    lines = parts // CORES
    me = lax.axis_index("user").astype(jnp.int32)
    part = lax.axis_index("item").astype(jnp.int32)
    others = me ^ jnp.arange(groups, dtype=jnp.int32)
    both = part ^ jnp.arange(CORES, dtype=jnp.int32)
    order = (both[:, None] ^ (CORES * jnp.arange(lines, dtype=jnp.int32))[None, :]).reshape(-1)
    first = (part * groups + others) * rows
    me = me.reshape(1)

    packed, targets = pack(user_emb, positive, user_expert, item_expert)
    users = lax.all_gather(packed, "item", axis=0)
    items = exchange([item_emb] * groups, "user")

    def scatter(pieces, axis):
        return lax.all_to_all(pieces, axis, split_axis=0, concat_axis=0, tiled=True)

    user_cols = scatter(cut(user_hidden, parts, items[1]), "item")
    found = stats(first, users, items, rows, packed)
    item_cols = scatter(cut(item_hidden, parts, found), "item")
    gathered = exchange([found] * parts, "item")
    losses, user_part, item_parts = grads(first, users, items, gathered, rows, user_cols)
    row_loss = lax.dynamic_slice_in_dim(losses[0], part * rows, rows)
    user_grad = lax.psum_scatter(user_part, "item", scatter_dimension=0, tiled=True)
    item_pieces = exchange(item_parts, "user")

    item_routed = route(me, targets, item_pieces, 1, groups, [])
    item_sent = stack(exchange(item_routed, "user"))
    item_line = exchange([item_sent] * lines, "item", CORES)
    user_slots = slot_hidden(me, users, user_cols, groups, 0, True, item_routed[0])
    user_rows = exchange(user_slots, "user")
    item_slots = slot_hidden(me, users, item_cols, groups, 1, False, item_sent)
    item_rows = [scatter(item_slots[0], "user")]
    user_routed = route(me, targets, [user_grad], 0, groups, [item_slots[0]] + user_rows[1:])
    user_sent = stack(exchange(user_routed, "user"))
    item_cross = item_line + [swap(piece, "item", 1) for piece in item_line]
    user_all = lax.all_gather(user_sent, "item", axis=0)
    item_weight_grad = outer(order, me, item_rows, item_cross, LARGE)
    user_weight_grad = outer(order, me, user_rows, [user_all], SMALL)
    return (row_loss, user_weight_grad, item_weight_grad)


def solution(mesh):
    placed = (
        P(("user", "item"), None),
        P(("item", "user"), None),
        P(("user", "item"), None),
        P(("item", "user"), None),
        P(("user", "item"), None),
        P(("item", "user"), None),
        P(("user", "item")),
    )
    return jax.shard_map(
        shards,
        mesh=mesh,
        in_specs=placed,
        out_specs=(P(("user", "item")), P("user", "item", None), P("user", "item", None)),
        check_vma=False,
    )
```

```python
import functools
import math

import jax
import jax.numpy as jnp
from jax import lax
from jax.experimental import pallas as pl
from jax.experimental.pallas import tpu as pltpu
from jax.sharding import PartitionSpec as P

EMB = 256
EXPERTS = 32
CAP = 16
SCALE = 1.0 / math.sqrt(EMB)
EXTRA = 16
DIGIT = 128
MIB = 1 << 20

F32 = jnp.float32
BF16 = jnp.bfloat16
CORES = 2
SCALARS = pl.BlockSpec(memory_space=pltpu.SMEM)
WHOLE = pl.BlockSpec(memory_space=pltpu.VMEM)
ANYWHERE = pl.BlockSpec(memory_space=pl.ANY)
VMEM = 60 * MIB
SMALL = pl.CostEstimate(flops=1024, bytes_accessed=1024, transcendentals=0)


def mm(a, b, ca, cb):
    return lax.dot_general(a, b, (((ca,), (cb,)), ((), ())), preferred_element_type=F32)


def number(rows, index):
    rows = rows.astype(F32)
    high = rows[2 * index : 2 * index + 1]
    return (high * DIGIT + rows[2 * index + 1 : 2 * index + 2]).astype(jnp.int32)


def swap(piece, axis, bits):
    size = lax.axis_size(axis)
    return lax.ppermute(piece, axis, [(j, j ^ bits) for j in range(size)])


def exchange(pieces, axis, unit=1):
    return [piece if k == 0 else swap(piece, axis, k * unit) for k, piece in enumerate(pieces)]


def pack_kernel(emb_ref, positive_ref, user_ref, item_ref, out_ref, target_ref):
    rows = emb_ref.shape[0]
    down = lax.broadcasted_iota(jnp.int32, (rows, rows), 0)
    across = lax.broadcasted_iota(jnp.int32, (rows, rows), 1)

    def slots(expert):
        wide = jnp.broadcast_to(expert.astype(F32), (rows, rows))
        before = jnp.where((wide == wide.T) & (down < across), 1.0, 0.0)
        return expert * CAP + jnp.sum(before, axis=0, keepdims=True).astype(jnp.int32)

    user = slots(user_ref[...])
    item = slots(item_ref[...])
    target_ref[0:1, :] = user
    target_ref[1:2, :] = item
    line = lax.broadcasted_iota(jnp.int32, (EXTRA, rows), 0)
    block = jnp.zeros((EXTRA, rows), jnp.int32)
    for index, values in enumerate((positive_ref[...], user, item)):
        block = jnp.where(line == 2 * index, values // DIGIT, block)
        block = jnp.where(line == 2 * index + 1, values % DIGIT, block)
    out_ref[:rows, :] = emb_ref[...]
    out_ref[rows:, :] = block.astype(F32).astype(BF16)


def pack(emb, positive, user_expert, item_expert):
    rows, width = emb.shape
    return pl.pallas_call(
        pack_kernel,
        out_shape=[
            jax.ShapeDtypeStruct((rows + EXTRA, width), BF16),
            jax.ShapeDtypeStruct((2, rows), jnp.int32),
        ],
        compiler_params=pltpu.CompilerParams(vmem_limit_bytes=VMEM),
        cost_estimate=SMALL,
    )(emb, positive.reshape(1, rows), user_expert.reshape(1, rows), item_expert.reshape(1, rows))


def stats_kernel(first_ref, users_ref, *refs, rows, chunk):
    *items_refs, _, out_ref, s_ref = refs
    own = items_refs[0].shape[0]
    n_cols = own * len(items_refs)
    for half in range(users_ref.shape[0]):
        queries = users_ref[half, :rows, :] * jnp.asarray(SCALE, BF16)
        for k, items_ref in enumerate(items_refs):
            s_ref[half, k * own : (k + 1) * own, :] = mm(items_ref[...], queries, 1, 1)
        positive = number(users_ref[half, rows:, :], 0)
        tops = jnp.full((8, rows), -jnp.inf, F32)
        for c in range(0, n_cols, chunk):
            part = s_ref[half, c : c + chunk, :]
            tops = jnp.maximum(tops, jnp.max(part.reshape(chunk // 8, 8, rows), axis=0))
        top = jnp.max(tops, axis=0, keepdims=True)
        total = jnp.zeros((8, rows), F32)
        picked = jnp.zeros((8, rows), F32)
        for c in range(0, n_cols, chunk):
            part = s_ref[half, c : c + chunk, :]
            probs = jnp.exp(part - top)
            total = total + jnp.sum(probs.reshape(chunk // 8, 8, rows), axis=0)
            wanted = positive - (first_ref[c // own] + c % own)
            hit = lax.broadcasted_iota(jnp.int32, (chunk, rows), 0) == wanted
            chosen = jnp.where(hit, part, 0.0)
            picked = picked + jnp.sum(chosen.reshape(chunk // 8, 8, rows), axis=0)
        here = pl.ds(half * rows, rows)
        out_ref[0:1, here] = top
        out_ref[1:2, here] = jnp.sum(total, axis=0, keepdims=True)
        out_ref[2:3, here] = jnp.sum(picked, axis=0, keepdims=True)


def stats(first, users, items, rows, after):
    blocks, height, emb = users.shape
    own = items[0].shape[0]
    n_cols = own * len(items)
    pair = 2
    return pl.pallas_call(
        functools.partial(stats_kernel, rows=rows, chunk=64),
        grid=(blocks // pair,),
        in_specs=[SCALARS, pl.BlockSpec((pair, height, emb), lambda b: (b, 0, 0))]
        + [pl.BlockSpec((own, emb), lambda b: (0, 0))] * len(items)
        + [ANYWHERE],
        out_specs=pl.BlockSpec((3, pair * rows), lambda b: (0, b)),
        out_shape=jax.ShapeDtypeStruct((3, blocks * rows), F32),
        scratch_shapes=[pltpu.VMEM((pair, n_cols, rows), F32)],
        compiler_params=pltpu.CompilerParams(vmem_limit_bytes=VMEM),
        cost_estimate=SMALL,
    )(first, users, *items, after)


def grad_kernel(first_ref, users_ref, *refs, rows, chunk, count, groups):
    stats_refs, refs = refs[:groups], refs[groups:]
    items_refs, refs = refs[:count], refs[count + 1 :]
    loss_ref, user_ref = refs[:2]
    part_refs = refs[2 : count + 2]
    s_ref, g_ref, flip_ref = refs[count + 2 :]
    own = items_refs[0].shape[0]
    n_cols = own * count
    step = pl.program_id(0)

    @pl.when(step == 0)
    def _():
        for k in range(count):
            flip_ref[:, k * own : (k + 1) * own] = items_refs[k][...].T
            part_refs[k][...] = jnp.zeros_like(part_refs[k])

    for half in range(users_ref.shape[0]):
        here = pl.ds(half * rows, rows)
        queries = users_ref[half, :rows, :]
        scaled = queries * jnp.asarray(SCALE, BF16)
        for k in range(count):
            s_ref[half, k * own : (k + 1) * own, :] = mm(items_refs[k][...], scaled, 1, 1)
        positive = number(users_ref[half, rows:, :], 0)
        top = functools.reduce(jnp.maximum, [ref[0:1, here] for ref in stats_refs])
        total = sum(ref[1:2, here] * jnp.exp(ref[0:1, here] - top) for ref in stats_refs)
        level = top + jnp.log(total)
        loss_ref[0:1, here] = level - sum(ref[2:3, here] for ref in stats_refs)
        for c in range(0, n_cols, chunk):
            probs = jnp.exp(s_ref[half, c : c + chunk, :] - level)
            wanted = positive - (first_ref[c // own] + c % own)
            hit = lax.broadcasted_iota(jnp.int32, (chunk, rows), 0) == wanted
            g_ref[half, c : c + chunk, :] = jnp.where(hit, probs - 1.0, probs).astype(BF16)
        for k in range(count):
            part_refs[k][...] += mm(g_ref[half, k * own : (k + 1) * own, :], queries, 1, 0)
        user_ref[here, :] = mm(flip_ref[...], g_ref[half], 1, 0).T * SCALE

    @pl.when(step == pl.num_programs(0) - 1)
    def _():
        for k in range(count):
            part_refs[k][...] = part_refs[k][...] * SCALE


def grads(first, users, items, gathered, rows, after):
    blocks, height, emb = users.shape
    count = len(items)
    own = items[0].shape[0]
    n_cols = own * count
    pair = 2
    groups = len(gathered)
    results = pl.pallas_call(
        functools.partial(grad_kernel, rows=rows, chunk=64, count=count, groups=groups),
        grid=(blocks // pair,),
        in_specs=[
            SCALARS,
            pl.BlockSpec((pair, height, emb), lambda b: (b, 0, 0)),
        ]
        + [pl.BlockSpec((3, pair * rows), lambda b: (0, b))] * groups
        + [pl.BlockSpec((own, emb), lambda b: (0, 0))] * count
        + [ANYWHERE],
        out_specs=[
            pl.BlockSpec((1, pair * rows), lambda b: (0, b)),
            pl.BlockSpec((pair * rows, emb), lambda b: (b, 0)),
        ]
        + [pl.BlockSpec((own, emb), lambda b: (0, 0))] * count,
        out_shape=[
            jax.ShapeDtypeStruct((1, blocks * rows), F32),
            jax.ShapeDtypeStruct((blocks * rows, emb), F32),
        ]
        + [jax.ShapeDtypeStruct((own, emb), F32)] * count,
        scratch_shapes=[
            pltpu.VMEM((pair, n_cols, rows), F32),
            pltpu.VMEM((pair, n_cols, rows), BF16),
            pltpu.VMEM((emb, n_cols), BF16),
        ],
        compiler_params=pltpu.CompilerParams(vmem_limit_bytes=VMEM),
        cost_estimate=SMALL,
    )(first, users, *gathered, *items, after)
    return results[0], results[1], results[2:]


def cut_kernel(in_ref, _, out_ref):
    width = out_ref.shape[2]
    for k in range(out_ref.shape[0]):
        out_ref[k] = in_ref[:, k * width : (k + 1) * width]


def cut(hidden, parts, after):
    rows, total = hidden.shape
    return pl.pallas_call(
        cut_kernel,
        in_specs=[WHOLE, ANYWHERE],
        out_specs=WHOLE,
        out_shape=jax.ShapeDtypeStruct((parts, rows, total // parts), BF16),
        compiler_params=pltpu.CompilerParams(vmem_limit_bytes=VMEM),
        cost_estimate=SMALL,
    )(hidden, after)


def onehot_of(target, me, groups):
    span = EXPERTS * CAP // groups
    place = lax.broadcasted_iota(jnp.int32, (EXPERTS * CAP, target.shape[1]), 0)
    place = (((place // span) ^ me) * span) + place % span
    return (place == target).astype(F32).astype(BF16)


def hidden_kernel(me_ref, users_ref, hidden_ref, _, *out_refs, tower):
    count, (pair, span, _) = len(out_refs), out_refs[0].shape[-3:]
    groups = out_refs[0].shape[0] if count == 1 else count
    me = 0 if count == 1 else me_ref[0]
    for half in range(pair):
        onehot = onehot_of(number(users_ref[half], 1 + tower), me, groups)
        moved = mm(onehot, hidden_ref[half], 1, 0).astype(BF16)
        for k in range(groups):
            part = moved[k * span : (k + 1) * span, :]
            if count == 1:
                out_refs[0][k, half] = part
            else:
                out_refs[k][half] = part


def slot_hidden(me, users, hidden, groups, tower, apart, after):
    blocks, rows, width = hidden.shape
    span = EXPERTS * CAP // groups
    pair = 2
    if apart:
        out_specs = [pl.BlockSpec((pair, span, width), lambda b: (b, 0, 0))] * groups
        out_shape = [jax.ShapeDtypeStruct((blocks, span, width), BF16)] * groups
    else:
        out_specs = [pl.BlockSpec((groups, pair, span, width), lambda b: (0, b, 0, 0))]
        out_shape = [jax.ShapeDtypeStruct((groups, blocks, span, width), BF16)]
    return pl.pallas_call(
        functools.partial(hidden_kernel, tower=tower),
        grid=(blocks // pair,),
        in_specs=[
            SCALARS,
            pl.BlockSpec((pair, EXTRA, rows), lambda b: (b, rows // EXTRA, 0)),
            pl.BlockSpec((pair, rows, width), lambda b: (b, 0, 0)),
            ANYWHERE,
        ],
        out_specs=out_specs,
        out_shape=out_shape,
        compiler_params=pltpu.CompilerParams(vmem_limit_bytes=VMEM),
        cost_estimate=SMALL,
    )(me, users, hidden, after)


def route_kernel(me_ref, target_ref, *refs, tower, count, order):
    total = refs[0][...]
    for ref in refs[1:count]:
        total = total + ref[...]
    low = total.astype(BF16)
    out_refs = refs[count + order :]
    span = out_refs[0].shape[0]
    onehot = onehot_of(target_ref[tower : tower + 1, :], me_ref[0], len(out_refs))
    moved = mm(onehot, low, 1, 0).astype(BF16)
    for k, out_ref in enumerate(out_refs):
        out_ref[...] = moved[k * span : (k + 1) * span, :]


def route(me, targets, pieces, tower, groups, after):
    rows, emb = pieces[0].shape
    span = EXPERTS * CAP // groups
    return pl.pallas_call(
        functools.partial(route_kernel, tower=tower, count=len(pieces), order=len(after)),
        in_specs=[SCALARS] + [WHOLE] * (1 + len(pieces)) + [ANYWHERE] * len(after),
        out_specs=[WHOLE] * groups,
        out_shape=[jax.ShapeDtypeStruct((span, emb), BF16)] * groups,
        compiler_params=pltpu.CompilerParams(vmem_limit_bytes=VMEM),
        cost_estimate=SMALL,
    )(me, targets, *pieces, *after)


def stack_kernel(*refs, count):
    for k in range(count):
        refs[-1][k] = refs[k][...]


def stack(pieces, after=()):
    return pl.pallas_call(
        functools.partial(stack_kernel, count=len(pieces)),
        in_specs=[WHOLE] * len(pieces) + [ANYWHERE] * len(after),
        out_specs=WHOLE,
        out_shape=jax.ShapeDtypeStruct((len(pieces),) + pieces[0].shape, pieces[0].dtype),
        compiler_params=pltpu.CompilerParams(vmem_limit_bytes=VMEM),
        cost_estimate=SMALL,
    )(*pieces, *after)


def outer_kernel(order_ref, me_ref, *refs, count):
    hidden_refs, grad_refs, out_ref = refs[:count], refs[count:-1], refs[-1]
    blocks, span, _ = hidden_refs[0].shape[-3:]
    groups = hidden_refs[0].shape[0] if count == 1 else count
    for e in range(span // CAP):
        here = slice(e * CAP, (e + 1) * CAP)
        left, right = [], []
        for j in range(blocks):
            block = j if len(grad_refs) == 1 else order_ref[j]
            for k in range(groups):
                if count == 1:
                    left.append(hidden_refs[0][me_ref[0] ^ k, block, here, :])
                else:
                    left.append(hidden_refs[k][block, here, :])
                if len(grad_refs) == 1:
                    right.append(grad_refs[0][j, k, here, :])
                else:
                    right.append(grad_refs[j][k, here, :])
        out_ref[e] = mm(jnp.concatenate(left), jnp.concatenate(right), 0, 0)


def outer(order, me, hidden, grads, cost):
    span, width = hidden[0].shape[-2:]
    emb = grads[0].shape[-1]
    own = span // CAP
    return pl.pallas_call(
        functools.partial(outer_kernel, count=len(hidden)),
        grid=(1,),
        in_specs=[SCALARS, SCALARS]
        + [pl.BlockSpec(g.shape, lambda _, d=g.ndim: (0,) * d) for g in hidden + grads],
        out_specs=pl.BlockSpec((own, width, emb), lambda _: (0, 0, 0)),
        out_shape=jax.ShapeDtypeStruct((own, width, emb), F32),
        compiler_params=pltpu.CompilerParams(vmem_limit_bytes=VMEM),
        cost_estimate=cost,
    )(order, me, *hidden, *grads)


def shards(user_emb, item_emb, user_hidden, item_hidden, user_expert, item_expert, positive):
    rows, emb = user_emb.shape
    groups = lax.axis_size("user")
    parts = lax.axis_size("item")
    width = user_hidden.shape[1] // parts
    lines = parts // CORES
    me = lax.axis_index("user").astype(jnp.int32)
    part = lax.axis_index("item").astype(jnp.int32)
    others = me ^ jnp.arange(groups, dtype=jnp.int32)
    both = part ^ jnp.arange(CORES, dtype=jnp.int32)
    order = (both[:, None] ^ (CORES * jnp.arange(lines, dtype=jnp.int32))[None, :]).reshape(-1)
    first = (part * groups + others) * rows
    me = me.reshape(1)

    packed, targets = pack(user_emb, positive, user_expert, item_expert)
    users = lax.all_gather(packed, "item", axis=0)
    items = exchange([item_emb] * groups, "user")

    def scatter(pieces, axis):
        return lax.all_to_all(pieces, axis, split_axis=0, concat_axis=0, tiled=True)

    user_cols = scatter(cut(user_hidden, parts, items[1]), "item")
    found = stats(first, users, items, rows, packed)
    item_cols = scatter(cut(item_hidden, parts, found), "item")
    gathered = exchange([found] * parts, "item")
    losses, user_part, item_parts = grads(first, users, items, gathered, rows, user_cols)
    row_loss = lax.dynamic_slice_in_dim(losses[0], part * rows, rows)
    user_grad = lax.psum_scatter(user_part, "item", scatter_dimension=0, tiled=True)
    item_pieces = exchange(item_parts, "user")

    item_routed = route(me, targets, item_pieces, 1, groups, [])
    user_slots = slot_hidden(me, users, user_cols, groups, 0, True, item_routed[0])
    item_sent = stack(exchange(item_routed, "user"), user_slots[:1])
    item_line = exchange([item_sent] * lines, "item", CORES)
    user_rows = exchange(user_slots, "user")
    user_routed = route(me, targets, [user_grad], 0, groups, [item_sent] + user_rows[1:])
    item_slots = slot_hidden(me, users, item_cols, groups, 1, False, user_routed[0])
    user_sent = stack(exchange(user_routed, "user"), item_line[1:3] + [item_slots[0]])
    item_rows = [scatter(item_slots[0], "user")]
    item_cross = item_line + [swap(piece, "item", 1) for piece in item_line]
    user_all = lax.all_gather(user_sent, "item", axis=0)
    item_weight_grad = outer(order, me, item_rows, item_cross, SMALL)
    user_weight_grad = outer(order, me, user_rows, [user_all], SMALL)
    return (row_loss, user_weight_grad, item_weight_grad)


def solution(mesh):
    placed = (
        P(("user", "item"), None),
        P(("item", "user"), None),
        P(("user", "item"), None),
        P(("item", "user"), None),
        P(("user", "item"), None),
        P(("item", "user"), None),
        P(("user", "item")),
    )
    return jax.shard_map(
        shards,
        mesh=mesh,
        in_specs=placed,
        out_specs=(P(("user", "item")), P("user", "item", None), P("user", "item", None)),
        check_vma=False,
    )
```

```python
import functools
import math

import jax
import jax.numpy as jnp
from jax import lax
from jax.experimental import pallas as pl
from jax.experimental.pallas import tpu as pltpu
from jax.sharding import PartitionSpec as P

EMB = 256
EXPERTS = 32
CAP = 16
SCALE = 1.0 / math.sqrt(EMB)
EXTRA = 16
DIGIT = 128
MIB = 1 << 20

F32 = jnp.float32
BF16 = jnp.bfloat16
CORES = 2
SCALARS = pl.BlockSpec(memory_space=pltpu.SMEM)
WHOLE = pl.BlockSpec(memory_space=pltpu.VMEM)
ANYWHERE = pl.BlockSpec(memory_space=pl.ANY)
VMEM = 60 * MIB
SMALL = pl.CostEstimate(flops=1024, bytes_accessed=1024, transcendentals=0)


def mm(a, b, ca, cb):
    return lax.dot_general(a, b, (((ca,), (cb,)), ((), ())), preferred_element_type=F32)


def number(rows, index):
    rows = rows.astype(F32)
    high = rows[2 * index : 2 * index + 1]
    return (high * DIGIT + rows[2 * index + 1 : 2 * index + 2]).astype(jnp.int32)


def swap(piece, axis, bits):
    size = lax.axis_size(axis)
    return lax.ppermute(piece, axis, [(j, j ^ bits) for j in range(size)])


def exchange(pieces, axis, unit=1):
    return [piece if k == 0 else swap(piece, axis, k * unit) for k, piece in enumerate(pieces)]


def pack_kernel(emb_ref, positive_ref, user_ref, item_ref, out_ref, target_ref):
    rows = emb_ref.shape[0]
    down = lax.broadcasted_iota(jnp.int32, (rows, rows), 0)
    across = lax.broadcasted_iota(jnp.int32, (rows, rows), 1)

    def slots(expert):
        wide = jnp.broadcast_to(expert.astype(F32), (rows, rows))
        before = jnp.where((wide == wide.T) & (down < across), 1.0, 0.0)
        return expert * CAP + jnp.sum(before, axis=0, keepdims=True).astype(jnp.int32)

    user = slots(user_ref[...])
    item = slots(item_ref[...])
    target_ref[0:1, :] = user
    target_ref[1:2, :] = item
    line = lax.broadcasted_iota(jnp.int32, (EXTRA, rows), 0)
    block = jnp.zeros((EXTRA, rows), jnp.int32)
    for index, values in enumerate((positive_ref[...], user, item)):
        block = jnp.where(line == 2 * index, values // DIGIT, block)
        block = jnp.where(line == 2 * index + 1, values % DIGIT, block)
    out_ref[:rows, :] = emb_ref[...]
    out_ref[rows:, :] = block.astype(F32).astype(BF16)


def pack(emb, positive, user_expert, item_expert):
    rows, width = emb.shape
    return pl.pallas_call(
        pack_kernel,
        out_shape=[
            jax.ShapeDtypeStruct((rows + EXTRA, width), BF16),
            jax.ShapeDtypeStruct((2, rows), jnp.int32),
        ],
        compiler_params=pltpu.CompilerParams(vmem_limit_bytes=VMEM),
        cost_estimate=SMALL,
    )(emb, positive.reshape(1, rows), user_expert.reshape(1, rows), item_expert.reshape(1, rows))


def stats_kernel(first_ref, users_ref, *refs, rows, chunk):
    *items_refs, _, out_ref, s_ref = refs
    own = items_refs[0].shape[0]
    n_cols = own * len(items_refs)
    for half in range(users_ref.shape[0]):
        queries = users_ref[half, :rows, :] * jnp.asarray(SCALE, BF16)
        for k, items_ref in enumerate(items_refs):
            s_ref[half, k * own : (k + 1) * own, :] = mm(items_ref[...], queries, 1, 1)
        positive = number(users_ref[half, rows:, :], 0)
        tops = jnp.full((8, rows), -jnp.inf, F32)
        for c in range(0, n_cols, chunk):
            part = s_ref[half, c : c + chunk, :]
            tops = jnp.maximum(tops, jnp.max(part.reshape(chunk // 8, 8, rows), axis=0))
        top = jnp.max(tops, axis=0, keepdims=True)
        total = jnp.zeros((8, rows), F32)
        picked = jnp.zeros((8, rows), F32)
        for c in range(0, n_cols, chunk):
            part = s_ref[half, c : c + chunk, :]
            probs = jnp.exp(part - top)
            total = total + jnp.sum(probs.reshape(chunk // 8, 8, rows), axis=0)
            wanted = positive - (first_ref[c // own] + c % own)
            hit = lax.broadcasted_iota(jnp.int32, (chunk, rows), 0) == wanted
            chosen = jnp.where(hit, part, 0.0)
            picked = picked + jnp.sum(chosen.reshape(chunk // 8, 8, rows), axis=0)
        here = pl.ds(half * rows, rows)
        out_ref[0:1, here] = top
        out_ref[1:2, here] = jnp.sum(total, axis=0, keepdims=True)
        out_ref[2:3, here] = jnp.sum(picked, axis=0, keepdims=True)


def stats(first, users, items, rows, after):
    blocks, height, emb = users.shape
    own = items[0].shape[0]
    n_cols = own * len(items)
    pair = 2
    return pl.pallas_call(
        functools.partial(stats_kernel, rows=rows, chunk=64),
        grid=(blocks // pair,),
        in_specs=[SCALARS, pl.BlockSpec((pair, height, emb), lambda b: (b, 0, 0))]
        + [pl.BlockSpec((own, emb), lambda b: (0, 0))] * len(items)
        + [ANYWHERE],
        out_specs=pl.BlockSpec((3, pair * rows), lambda b: (0, b)),
        out_shape=jax.ShapeDtypeStruct((3, blocks * rows), F32),
        scratch_shapes=[pltpu.VMEM((pair, n_cols, rows), F32)],
        compiler_params=pltpu.CompilerParams(vmem_limit_bytes=VMEM),
        cost_estimate=SMALL,
    )(first, users, *items, after)


def grad_kernel(first_ref, users_ref, *refs, rows, chunk, count, groups):
    stats_refs, refs = refs[:groups], refs[groups:]
    items_refs, refs = refs[:count], refs[count + 1 :]
    loss_ref, user_ref = refs[:2]
    part_refs = refs[2 : count + 2]
    s_ref, g_ref, flip_ref = refs[count + 2 :]
    own = items_refs[0].shape[0]
    n_cols = own * count
    step = pl.program_id(0)

    @pl.when(step == 0)
    def _():
        for k in range(count):
            flip_ref[:, k * own : (k + 1) * own] = items_refs[k][...].T
            part_refs[k][...] = jnp.zeros_like(part_refs[k])

    for half in range(users_ref.shape[0]):
        here = pl.ds(half * rows, rows)
        queries = users_ref[half, :rows, :]
        scaled = queries * jnp.asarray(SCALE, BF16)
        for k in range(count):
            s_ref[half, k * own : (k + 1) * own, :] = mm(items_refs[k][...], scaled, 1, 1)
        positive = number(users_ref[half, rows:, :], 0)
        top = functools.reduce(jnp.maximum, [ref[0:1, here] for ref in stats_refs])
        total = sum(ref[1:2, here] * jnp.exp(ref[0:1, here] - top) for ref in stats_refs)
        level = top + jnp.log(total)
        loss_ref[0:1, here] = level - sum(ref[2:3, here] for ref in stats_refs)
        for c in range(0, n_cols, chunk):
            probs = jnp.exp(s_ref[half, c : c + chunk, :] - level)
            wanted = positive - (first_ref[c // own] + c % own)
            hit = lax.broadcasted_iota(jnp.int32, (chunk, rows), 0) == wanted
            g_ref[half, c : c + chunk, :] = jnp.where(hit, probs - 1.0, probs).astype(BF16)
        for k in range(count):
            part_refs[k][...] += mm(g_ref[half, k * own : (k + 1) * own, :], queries, 1, 0)
        user_ref[here, :] = mm(flip_ref[...], g_ref[half], 1, 0).T * SCALE

    @pl.when(step == pl.num_programs(0) - 1)
    def _():
        for k in range(count):
            part_refs[k][...] = part_refs[k][...] * SCALE


def grads(first, users, items, gathered, rows, after):
    blocks, height, emb = users.shape
    count = len(items)
    own = items[0].shape[0]
    n_cols = own * count
    pair = 2
    groups = len(gathered)
    results = pl.pallas_call(
        functools.partial(grad_kernel, rows=rows, chunk=64, count=count, groups=groups),
        grid=(blocks // pair,),
        in_specs=[
            SCALARS,
            pl.BlockSpec((pair, height, emb), lambda b: (b, 0, 0)),
        ]
        + [pl.BlockSpec((3, pair * rows), lambda b: (0, b))] * groups
        + [pl.BlockSpec((own, emb), lambda b: (0, 0))] * count
        + [ANYWHERE],
        out_specs=[
            pl.BlockSpec((1, pair * rows), lambda b: (0, b)),
            pl.BlockSpec((pair * rows, emb), lambda b: (b, 0)),
        ]
        + [pl.BlockSpec((own, emb), lambda b: (0, 0))] * count,
        out_shape=[
            jax.ShapeDtypeStruct((1, blocks * rows), F32),
            jax.ShapeDtypeStruct((blocks * rows, emb), F32),
        ]
        + [jax.ShapeDtypeStruct((own, emb), F32)] * count,
        scratch_shapes=[
            pltpu.VMEM((pair, n_cols, rows), F32),
            pltpu.VMEM((pair, n_cols, rows), BF16),
            pltpu.VMEM((emb, n_cols), BF16),
        ],
        compiler_params=pltpu.CompilerParams(vmem_limit_bytes=VMEM),
        cost_estimate=SMALL,
    )(first, users, *gathered, *items, after)
    return results[0], results[1], results[2:]


def cut_kernel(in_ref, _, out_ref):
    width = out_ref.shape[2]
    for k in range(out_ref.shape[0]):
        out_ref[k] = in_ref[:, k * width : (k + 1) * width]


def cut(hidden, parts, after):
    rows, total = hidden.shape
    return pl.pallas_call(
        cut_kernel,
        in_specs=[WHOLE, ANYWHERE],
        out_specs=WHOLE,
        out_shape=jax.ShapeDtypeStruct((parts, rows, total // parts), BF16),
        compiler_params=pltpu.CompilerParams(vmem_limit_bytes=VMEM),
        cost_estimate=SMALL,
    )(hidden, after)


def onehot_of(target, me, groups):
    span = EXPERTS * CAP // groups
    place = lax.broadcasted_iota(jnp.int32, (EXPERTS * CAP, target.shape[1]), 0)
    place = (((place // span) ^ me) * span) + place % span
    return (place == target).astype(F32).astype(BF16)


def hidden_kernel(me_ref, users_ref, hidden_ref, _, *out_refs, tower):
    count, (pair, span, _) = len(out_refs), out_refs[0].shape[-3:]
    groups = out_refs[0].shape[0] if count == 1 else count
    me = 0 if count == 1 else me_ref[0]
    for half in range(pair):
        onehot = onehot_of(number(users_ref[half], 1 + tower), me, groups)
        moved = mm(onehot, hidden_ref[half], 1, 0).astype(BF16)
        for k in range(groups):
            part = moved[k * span : (k + 1) * span, :]
            if count == 1:
                out_refs[0][k, half] = part
            else:
                out_refs[k][half] = part


def slot_hidden(me, users, hidden, groups, tower, apart, after):
    blocks, rows, width = hidden.shape
    span = EXPERTS * CAP // groups
    pair = 2
    if apart:
        out_specs = [pl.BlockSpec((pair, span, width), lambda b: (b, 0, 0))] * groups
        out_shape = [jax.ShapeDtypeStruct((blocks, span, width), BF16)] * groups
    else:
        out_specs = [pl.BlockSpec((groups, pair, span, width), lambda b: (0, b, 0, 0))]
        out_shape = [jax.ShapeDtypeStruct((groups, blocks, span, width), BF16)]
    return pl.pallas_call(
        functools.partial(hidden_kernel, tower=tower),
        grid=(blocks // pair,),
        in_specs=[
            SCALARS,
            pl.BlockSpec((pair, EXTRA, rows), lambda b: (b, rows // EXTRA, 0)),
            pl.BlockSpec((pair, rows, width), lambda b: (b, 0, 0)),
            ANYWHERE,
        ],
        out_specs=out_specs,
        out_shape=out_shape,
        compiler_params=pltpu.CompilerParams(vmem_limit_bytes=VMEM),
        cost_estimate=SMALL,
    )(me, users, hidden, after)


def route_kernel(me_ref, target_ref, *refs, tower, count, order):
    total = refs[0][...]
    for ref in refs[1:count]:
        total = total + ref[...]
    low = total.astype(BF16)
    out_refs = refs[count + order :]
    span = out_refs[0].shape[0]
    onehot = onehot_of(target_ref[tower : tower + 1, :], me_ref[0], len(out_refs))
    moved = mm(onehot, low, 1, 0).astype(BF16)
    for k, out_ref in enumerate(out_refs):
        out_ref[...] = moved[k * span : (k + 1) * span, :]


def route(me, targets, pieces, tower, groups, after):
    rows, emb = pieces[0].shape
    span = EXPERTS * CAP // groups
    return pl.pallas_call(
        functools.partial(route_kernel, tower=tower, count=len(pieces), order=len(after)),
        in_specs=[SCALARS] + [WHOLE] * (1 + len(pieces)) + [ANYWHERE] * len(after),
        out_specs=[WHOLE] * groups,
        out_shape=[jax.ShapeDtypeStruct((span, emb), BF16)] * groups,
        compiler_params=pltpu.CompilerParams(vmem_limit_bytes=VMEM),
        cost_estimate=SMALL,
    )(me, targets, *pieces, *after)


def stack_kernel(*refs, count):
    for k in range(count):
        refs[-1][k] = refs[k][...]


def stack(pieces, after=()):
    return pl.pallas_call(
        functools.partial(stack_kernel, count=len(pieces)),
        in_specs=[WHOLE] * len(pieces) + [ANYWHERE] * len(after),
        out_specs=WHOLE,
        out_shape=jax.ShapeDtypeStruct((len(pieces),) + pieces[0].shape, pieces[0].dtype),
        compiler_params=pltpu.CompilerParams(vmem_limit_bytes=VMEM),
        cost_estimate=SMALL,
    )(*pieces, *after)


def outer_kernel(order_ref, me_ref, *refs, count):
    hidden_refs, grad_refs, out_ref = refs[:count], refs[count:-1], refs[-1]
    blocks, span, _ = hidden_refs[0].shape[-3:]
    groups = hidden_refs[0].shape[0] if count == 1 else count
    for e in range(span // CAP):
        here = slice(e * CAP, (e + 1) * CAP)
        left, right = [], []
        for j in range(blocks):
            block = j if len(grad_refs) == 1 else order_ref[j]
            for k in range(groups):
                if count == 1:
                    left.append(hidden_refs[0][me_ref[0] ^ k, block, here, :])
                else:
                    left.append(hidden_refs[k][block, here, :])
                if len(grad_refs) == 1:
                    right.append(grad_refs[0][j, k, here, :])
                else:
                    right.append(grad_refs[j][k, here, :])
        out_ref[e] = mm(jnp.concatenate(left), jnp.concatenate(right), 0, 0)


def outer(order, me, hidden, grads, cost):
    span, width = hidden[0].shape[-2:]
    emb = grads[0].shape[-1]
    own = span // CAP
    return pl.pallas_call(
        functools.partial(outer_kernel, count=len(hidden)),
        grid=(1,),
        in_specs=[SCALARS, SCALARS]
        + [pl.BlockSpec(g.shape, lambda _, d=g.ndim: (0,) * d) for g in hidden + grads],
        out_specs=pl.BlockSpec((own, width, emb), lambda _: (0, 0, 0)),
        out_shape=jax.ShapeDtypeStruct((own, width, emb), F32),
        compiler_params=pltpu.CompilerParams(vmem_limit_bytes=VMEM),
        cost_estimate=cost,
    )(order, me, *hidden, *grads)


def shards(user_emb, item_emb, user_hidden, item_hidden, user_expert, item_expert, positive):
    rows, emb = user_emb.shape
    groups = lax.axis_size("user")
    parts = lax.axis_size("item")
    width = user_hidden.shape[1] // parts
    lines = parts // CORES
    me = lax.axis_index("user").astype(jnp.int32)
    part = lax.axis_index("item").astype(jnp.int32)
    others = me ^ jnp.arange(groups, dtype=jnp.int32)
    both = part ^ jnp.arange(CORES, dtype=jnp.int32)
    order = (both[:, None] ^ (CORES * jnp.arange(lines, dtype=jnp.int32))[None, :]).reshape(-1)
    first = (part * groups + others) * rows
    me = me.reshape(1)

    packed, targets = pack(user_emb, positive, user_expert, item_expert)
    users = lax.all_gather(packed, "item", axis=0)
    items = exchange([item_emb] * groups, "user")

    def scatter(pieces, axis):
        return lax.all_to_all(pieces, axis, split_axis=0, concat_axis=0, tiled=True)

    user_cols = scatter(cut(user_hidden, parts, items[1]), "item")
    found = stats(first, users, items, rows, packed)
    item_cols = scatter(cut(item_hidden, parts, found), "item")
    gathered = exchange([found] * parts, "item")
    losses, user_part, item_parts = grads(first, users, items, gathered, rows, user_cols)
    row_loss = lax.dynamic_slice_in_dim(losses[0], part * rows, rows)
    user_grad = lax.psum_scatter(user_part, "item", scatter_dimension=0, tiled=True)
    item_pieces = exchange(item_parts, "user")

    user_slots = slot_hidden(me, users, user_cols, groups, 0, True, item_parts[0])
    user_rows = exchange(user_slots, "user")
    item_routed = route(me, targets, item_pieces, 1, groups, user_slots[:1])
    item_sent = stack(exchange(item_routed, "user"))
    item_line = exchange([item_sent] * lines, "item", CORES)
    user_routed = route(me, targets, [user_grad], 0, groups, user_rows[1:])
    item_slots = slot_hidden(me, users, item_cols, groups, 1, False, user_routed[0])
    user_sent = stack(exchange(user_routed, "user"), item_line[1:3] + [item_slots[0]])
    item_rows = [scatter(item_slots[0], "user")]
    item_cross = item_line + [swap(piece, "item", 1) for piece in item_line]
    user_all = lax.all_gather(user_sent, "item", axis=0)
    item_weight_grad = outer(order, me, item_rows, item_cross, SMALL)
    user_weight_grad = outer(order, me, user_rows, [user_all], SMALL)
    return (row_loss, user_weight_grad, item_weight_grad)


def solution(mesh):
    placed = (
        P(("user", "item"), None),
        P(("item", "user"), None),
        P(("user", "item"), None),
        P(("item", "user"), None),
        P(("user", "item"), None),
        P(("item", "user"), None),
        P(("user", "item")),
    )
    return jax.shard_map(
        shards,
        mesh=mesh,
        in_specs=placed,
        out_specs=(P(("user", "item")), P("user", "item", None), P("user", "item", None)),
        check_vma=False,
    )
```

```python
import functools
import math

import jax
import jax.numpy as jnp
from jax import lax
from jax.experimental import pallas as pl
from jax.experimental.pallas import tpu as pltpu
from jax.sharding import PartitionSpec as P

EMB = 256
EXPERTS = 32
CAP = 16
SCALE = 1.0 / math.sqrt(EMB)
EXTRA = 16
DIGIT = 128
MIB = 1 << 20

F32 = jnp.float32
BF16 = jnp.bfloat16
CORES = 2
SCALARS = pl.BlockSpec(memory_space=pltpu.SMEM)
WHOLE = pl.BlockSpec(memory_space=pltpu.VMEM)
ANYWHERE = pl.BlockSpec(memory_space=pl.ANY)
VMEM = 60 * MIB
SMALL = pl.CostEstimate(flops=1024, bytes_accessed=1024, transcendentals=0)


def mm(a, b, ca, cb):
    return lax.dot_general(a, b, (((ca,), (cb,)), ((), ())), preferred_element_type=F32)


def number(rows, index):
    rows = rows.astype(F32)
    high = rows[2 * index : 2 * index + 1]
    return (high * DIGIT + rows[2 * index + 1 : 2 * index + 2]).astype(jnp.int32)


def swap(piece, axis, bits):
    size = lax.axis_size(axis)
    return lax.ppermute(piece, axis, [(j, j ^ bits) for j in range(size)])


def exchange(pieces, axis, unit=1):
    return [piece if k == 0 else swap(piece, axis, k * unit) for k, piece in enumerate(pieces)]


def pack_kernel(emb_ref, positive_ref, user_ref, item_ref, out_ref, target_ref):
    rows = emb_ref.shape[0]
    down = lax.broadcasted_iota(jnp.int32, (rows, rows), 0)
    across = lax.broadcasted_iota(jnp.int32, (rows, rows), 1)

    def slots(expert):
        wide = jnp.broadcast_to(expert.astype(F32), (rows, rows))
        before = jnp.where((wide == wide.T) & (down < across), 1.0, 0.0)
        return expert * CAP + jnp.sum(before, axis=0, keepdims=True).astype(jnp.int32)

    user = slots(user_ref[...])
    item = slots(item_ref[...])
    target_ref[0:1, :] = user
    target_ref[1:2, :] = item
    line = lax.broadcasted_iota(jnp.int32, (EXTRA, rows), 0)
    block = jnp.zeros((EXTRA, rows), jnp.int32)
    for index, values in enumerate((positive_ref[...], user, item)):
        block = jnp.where(line == 2 * index, values // DIGIT, block)
        block = jnp.where(line == 2 * index + 1, values % DIGIT, block)
    out_ref[:rows, :] = emb_ref[...]
    out_ref[rows:, :] = block.astype(F32).astype(BF16)


def pack(emb, positive, user_expert, item_expert):
    rows, width = emb.shape
    return pl.pallas_call(
        pack_kernel,
        out_shape=[
            jax.ShapeDtypeStruct((rows + EXTRA, width), BF16),
            jax.ShapeDtypeStruct((2, rows), jnp.int32),
        ],
        compiler_params=pltpu.CompilerParams(vmem_limit_bytes=VMEM),
        cost_estimate=SMALL,
    )(emb, positive.reshape(1, rows), user_expert.reshape(1, rows), item_expert.reshape(1, rows))


def stats_kernel(first_ref, users_ref, *refs, rows, chunk):
    *items_refs, _, out_ref, s_ref = refs
    own = items_refs[0].shape[0]
    n_cols = own * len(items_refs)
    for half in range(users_ref.shape[0]):
        queries = users_ref[half, :rows, :] * jnp.asarray(SCALE, BF16)
        for k, items_ref in enumerate(items_refs):
            s_ref[half, k * own : (k + 1) * own, :] = mm(items_ref[...], queries, 1, 1)
        positive = number(users_ref[half, rows:, :], 0)
        tops = jnp.full((8, rows), -jnp.inf, F32)
        for c in range(0, n_cols, chunk):
            part = s_ref[half, c : c + chunk, :]
            tops = jnp.maximum(tops, jnp.max(part.reshape(chunk // 8, 8, rows), axis=0))
        top = jnp.max(tops, axis=0, keepdims=True)
        total = jnp.zeros((8, rows), F32)
        picked = jnp.zeros((8, rows), F32)
        for c in range(0, n_cols, chunk):
            part = s_ref[half, c : c + chunk, :]
            probs = jnp.exp(part - top)
            total = total + jnp.sum(probs.reshape(chunk // 8, 8, rows), axis=0)
            wanted = positive - (first_ref[c // own] + c % own)
            hit = lax.broadcasted_iota(jnp.int32, (chunk, rows), 0) == wanted
            chosen = jnp.where(hit, part, 0.0)
            picked = picked + jnp.sum(chosen.reshape(chunk // 8, 8, rows), axis=0)
        here = pl.ds(half * rows, rows)
        out_ref[0:1, here] = top
        out_ref[1:2, here] = jnp.sum(total, axis=0, keepdims=True)
        out_ref[2:3, here] = jnp.sum(picked, axis=0, keepdims=True)


def stats(first, users, items, rows, after):
    blocks, height, emb = users.shape
    own = items[0].shape[0]
    n_cols = own * len(items)
    pair = 2
    return pl.pallas_call(
        functools.partial(stats_kernel, rows=rows, chunk=64),
        grid=(blocks // pair,),
        in_specs=[SCALARS, pl.BlockSpec((pair, height, emb), lambda b: (b, 0, 0))]
        + [pl.BlockSpec((own, emb), lambda b: (0, 0))] * len(items)
        + [ANYWHERE],
        out_specs=pl.BlockSpec((3, pair * rows), lambda b: (0, b)),
        out_shape=jax.ShapeDtypeStruct((3, blocks * rows), F32),
        scratch_shapes=[pltpu.VMEM((pair, n_cols, rows), F32)],
        compiler_params=pltpu.CompilerParams(vmem_limit_bytes=VMEM),
        cost_estimate=SMALL,
    )(first, users, *items, after)


def grad_kernel(first_ref, users_ref, *refs, rows, chunk, count, groups):
    stats_refs, refs = refs[:groups], refs[groups:]
    items_refs, refs = refs[:count], refs[count + 1 :]
    loss_ref, user_ref = refs[:2]
    part_refs = refs[2 : count + 2]
    s_ref, g_ref, flip_ref = refs[count + 2 :]
    own = items_refs[0].shape[0]
    n_cols = own * count
    step = pl.program_id(0)

    @pl.when(step == 0)
    def _():
        for k in range(count):
            flip_ref[:, k * own : (k + 1) * own] = items_refs[k][...].T
            part_refs[k][...] = jnp.zeros_like(part_refs[k])

    for half in range(users_ref.shape[0]):
        here = pl.ds(half * rows, rows)
        queries = users_ref[half, :rows, :]
        scaled = queries * jnp.asarray(SCALE, BF16)
        for k in range(count):
            s_ref[half, k * own : (k + 1) * own, :] = mm(items_refs[k][...], scaled, 1, 1)
        positive = number(users_ref[half, rows:, :], 0)
        top = functools.reduce(jnp.maximum, [ref[0:1, here] for ref in stats_refs])
        total = sum(ref[1:2, here] * jnp.exp(ref[0:1, here] - top) for ref in stats_refs)
        level = top + jnp.log(total)
        loss_ref[0:1, here] = level - sum(ref[2:3, here] for ref in stats_refs)
        for c in range(0, n_cols, chunk):
            probs = jnp.exp(s_ref[half, c : c + chunk, :] - level)
            wanted = positive - (first_ref[c // own] + c % own)
            hit = lax.broadcasted_iota(jnp.int32, (chunk, rows), 0) == wanted
            g_ref[half, c : c + chunk, :] = jnp.where(hit, probs - 1.0, probs).astype(BF16)
        for k in range(count):
            part_refs[k][...] += mm(g_ref[half, k * own : (k + 1) * own, :], queries, 1, 0)
        user_ref[here, :] = mm(flip_ref[...], g_ref[half], 1, 0).T * SCALE

    @pl.when(step == pl.num_programs(0) - 1)
    def _():
        for k in range(count):
            part_refs[k][...] = part_refs[k][...] * SCALE


def grads(first, users, items, gathered, rows, after):
    blocks, height, emb = users.shape
    count = len(items)
    own = items[0].shape[0]
    n_cols = own * count
    pair = 2
    groups = len(gathered)
    results = pl.pallas_call(
        functools.partial(grad_kernel, rows=rows, chunk=64, count=count, groups=groups),
        grid=(blocks // pair,),
        in_specs=[
            SCALARS,
            pl.BlockSpec((pair, height, emb), lambda b: (b, 0, 0)),
        ]
        + [pl.BlockSpec((3, pair * rows), lambda b: (0, b))] * groups
        + [pl.BlockSpec((own, emb), lambda b: (0, 0))] * count
        + [ANYWHERE],
        out_specs=[
            pl.BlockSpec((1, pair * rows), lambda b: (0, b)),
            pl.BlockSpec((pair * rows, emb), lambda b: (b, 0)),
        ]
        + [pl.BlockSpec((own, emb), lambda b: (0, 0))] * count,
        out_shape=[
            jax.ShapeDtypeStruct((1, blocks * rows), F32),
            jax.ShapeDtypeStruct((blocks * rows, emb), F32),
        ]
        + [jax.ShapeDtypeStruct((own, emb), F32)] * count,
        scratch_shapes=[
            pltpu.VMEM((pair, n_cols, rows), F32),
            pltpu.VMEM((pair, n_cols, rows), BF16),
            pltpu.VMEM((emb, n_cols), BF16),
        ],
        compiler_params=pltpu.CompilerParams(vmem_limit_bytes=VMEM),
        cost_estimate=SMALL,
    )(first, users, *gathered, *items, after)
    return results[0], results[1], results[2:]


def cut_kernel(in_ref, _, out_ref):
    width = out_ref.shape[2]
    for k in range(out_ref.shape[0]):
        out_ref[k] = in_ref[:, k * width : (k + 1) * width]


def cut(hidden, parts, after):
    rows, total = hidden.shape
    return pl.pallas_call(
        cut_kernel,
        in_specs=[WHOLE, ANYWHERE],
        out_specs=WHOLE,
        out_shape=jax.ShapeDtypeStruct((parts, rows, total // parts), BF16),
        compiler_params=pltpu.CompilerParams(vmem_limit_bytes=VMEM),
        cost_estimate=SMALL,
    )(hidden, after)


def onehot_of(target, me, groups):
    span = EXPERTS * CAP // groups
    place = lax.broadcasted_iota(jnp.int32, (EXPERTS * CAP, target.shape[1]), 0)
    place = (((place // span) ^ me) * span) + place % span
    return (place == target).astype(F32).astype(BF16)


def hidden_kernel(me_ref, users_ref, hidden_ref, _, *out_refs, tower):
    count, (pair, span, _) = len(out_refs), out_refs[0].shape[-3:]
    groups = out_refs[0].shape[0] if count == 1 else count
    me = 0 if count == 1 else me_ref[0]
    for half in range(pair):
        onehot = onehot_of(number(users_ref[half], 1 + tower), me, groups)
        moved = mm(onehot, hidden_ref[half], 1, 0).astype(BF16)
        for k in range(groups):
            part = moved[k * span : (k + 1) * span, :]
            if count == 1:
                out_refs[0][k, half] = part
            else:
                out_refs[k][half] = part


def slot_hidden(me, users, hidden, groups, tower, apart, after):
    blocks, rows, width = hidden.shape
    span = EXPERTS * CAP // groups
    pair = 2
    if apart:
        out_specs = [pl.BlockSpec((pair, span, width), lambda b: (b, 0, 0))] * groups
        out_shape = [jax.ShapeDtypeStruct((blocks, span, width), BF16)] * groups
    else:
        out_specs = [pl.BlockSpec((groups, pair, span, width), lambda b: (0, b, 0, 0))]
        out_shape = [jax.ShapeDtypeStruct((groups, blocks, span, width), BF16)]
    return pl.pallas_call(
        functools.partial(hidden_kernel, tower=tower),
        grid=(blocks // pair,),
        in_specs=[
            SCALARS,
            pl.BlockSpec((pair, EXTRA, rows), lambda b: (b, rows // EXTRA, 0)),
            pl.BlockSpec((pair, rows, width), lambda b: (b, 0, 0)),
            ANYWHERE,
        ],
        out_specs=out_specs,
        out_shape=out_shape,
        compiler_params=pltpu.CompilerParams(vmem_limit_bytes=VMEM),
        cost_estimate=SMALL,
    )(me, users, hidden, after)


def route_kernel(me_ref, target_ref, *refs, tower, count, order):
    total = refs[0][...]
    for ref in refs[1:count]:
        total = total + ref[...]
    low = total.astype(BF16)
    out_refs = refs[count + order :]
    span = out_refs[0].shape[0]
    onehot = onehot_of(target_ref[tower : tower + 1, :], me_ref[0], len(out_refs))
    moved = mm(onehot, low, 1, 0).astype(BF16)
    for k, out_ref in enumerate(out_refs):
        out_ref[...] = moved[k * span : (k + 1) * span, :]


def route(me, targets, pieces, tower, groups, after):
    rows, emb = pieces[0].shape
    span = EXPERTS * CAP // groups
    return pl.pallas_call(
        functools.partial(route_kernel, tower=tower, count=len(pieces), order=len(after)),
        in_specs=[SCALARS] + [WHOLE] * (1 + len(pieces)) + [ANYWHERE] * len(after),
        out_specs=[WHOLE] * groups,
        out_shape=[jax.ShapeDtypeStruct((span, emb), BF16)] * groups,
        compiler_params=pltpu.CompilerParams(vmem_limit_bytes=VMEM),
        cost_estimate=SMALL,
    )(me, targets, *pieces, *after)


def stack_kernel(*refs, count):
    for k in range(count):
        refs[-1][k] = refs[k][...]


def stack(pieces, after=()):
    return pl.pallas_call(
        functools.partial(stack_kernel, count=len(pieces)),
        in_specs=[WHOLE] * len(pieces) + [ANYWHERE] * len(after),
        out_specs=WHOLE,
        out_shape=jax.ShapeDtypeStruct((len(pieces),) + pieces[0].shape, pieces[0].dtype),
        compiler_params=pltpu.CompilerParams(vmem_limit_bytes=VMEM),
        cost_estimate=SMALL,
    )(*pieces, *after)


def outer_kernel(order_ref, me_ref, *refs, count):
    hidden_refs, grad_refs, out_ref = refs[:count], refs[count:-1], refs[-1]
    blocks, span, _ = hidden_refs[0].shape[-3:]
    groups = hidden_refs[0].shape[0] if count == 1 else count
    for e in range(span // CAP):
        here = slice(e * CAP, (e + 1) * CAP)
        left, right = [], []
        for j in range(blocks):
            block = j if len(grad_refs) == 1 else order_ref[j]
            for k in range(groups):
                if count == 1:
                    left.append(hidden_refs[0][me_ref[0] ^ k, block, here, :])
                else:
                    left.append(hidden_refs[k][block, here, :])
                if len(grad_refs) == 1:
                    right.append(grad_refs[0][j, k, here, :])
                else:
                    right.append(grad_refs[j][k, here, :])
        out_ref[e] = mm(jnp.concatenate(left), jnp.concatenate(right), 0, 0)


def outer(order, me, hidden, grads, cost):
    span, width = hidden[0].shape[-2:]
    emb = grads[0].shape[-1]
    own = span // CAP
    return pl.pallas_call(
        functools.partial(outer_kernel, count=len(hidden)),
        grid=(1,),
        in_specs=[SCALARS, SCALARS]
        + [pl.BlockSpec(g.shape, lambda _, d=g.ndim: (0,) * d) for g in hidden + grads],
        out_specs=pl.BlockSpec((own, width, emb), lambda _: (0, 0, 0)),
        out_shape=jax.ShapeDtypeStruct((own, width, emb), F32),
        compiler_params=pltpu.CompilerParams(vmem_limit_bytes=VMEM),
        cost_estimate=cost,
    )(order, me, *hidden, *grads)


def shards(user_emb, item_emb, user_hidden, item_hidden, user_expert, item_expert, positive):
    rows, emb = user_emb.shape
    groups = lax.axis_size("user")
    parts = lax.axis_size("item")
    width = user_hidden.shape[1] // parts
    lines = parts // CORES
    me = lax.axis_index("user").astype(jnp.int32)
    part = lax.axis_index("item").astype(jnp.int32)
    others = me ^ jnp.arange(groups, dtype=jnp.int32)
    both = part ^ jnp.arange(CORES, dtype=jnp.int32)
    order = (both[:, None] ^ (CORES * jnp.arange(lines, dtype=jnp.int32))[None, :]).reshape(-1)
    first = (part * groups + others) * rows
    me = me.reshape(1)

    packed, targets = pack(user_emb, positive, user_expert, item_expert)
    users = lax.all_gather(packed, "item", axis=0)
    items = exchange([item_emb] * groups, "user")

    def scatter(pieces, axis):
        return lax.all_to_all(pieces, axis, split_axis=0, concat_axis=0, tiled=True)

    user_cols = scatter(cut(user_hidden, parts, items[1]), "item")
    found = stats(first, users, items, rows, packed)
    item_cols = scatter(cut(item_hidden, parts, found), "item")
    gathered = exchange([found] * parts, "item")
    losses, user_part, item_parts = grads(first, users, items, gathered, rows, user_cols)
    row_loss = lax.dynamic_slice_in_dim(losses[0], part * rows, rows)
    user_grad = lax.psum_scatter(user_part, "item", scatter_dimension=0, tiled=True)
    item_pieces = exchange(item_parts, "user")

    user_slots = slot_hidden(me, users, user_cols, groups, 0, True, item_parts[0])
    user_rows = exchange(user_slots, "user")
    item_routed = route(me, targets, item_pieces, 1, groups, user_slots[:1])
    item_slots = slot_hidden(me, users, item_cols, groups, 1, False, item_routed[0])
    user_routed = route(me, targets, [user_grad], 0, groups, [*item_slots, *user_rows[1:]])
    item_sent = stack(exchange(item_routed, "user"), user_routed[:1])
    item_line = exchange([item_sent] * lines, "item", CORES)
    user_sent = stack(exchange(user_routed, "user"), item_line[1:2])
    item_rows = [scatter(item_slots[0], "user")]
    item_cross = item_line + [swap(piece, "item", 1) for piece in item_line]
    user_all = lax.all_gather(user_sent, "item", axis=0)
    item_weight_grad = outer(order, me, item_rows, item_cross, SMALL)
    user_weight_grad = outer(order, me, user_rows, [user_all], SMALL)
    return (row_loss, user_weight_grad, item_weight_grad)


def solution(mesh):
    placed = (
        P(("user", "item"), None),
        P(("item", "user"), None),
        P(("user", "item"), None),
        P(("item", "user"), None),
        P(("user", "item"), None),
        P(("item", "user"), None),
        P(("user", "item")),
    )
    return jax.shard_map(
        shards,
        mesh=mesh,
        in_specs=placed,
        out_specs=(P(("user", "item")), P("user", "item", None), P("user", "item", None)),
        check_vma=False,
    )
```

```python
import functools
import math

import jax
import jax.numpy as jnp
from jax import lax
from jax.experimental import pallas as pl
from jax.experimental.pallas import tpu as pltpu
from jax.sharding import PartitionSpec as P

EMB = 256
EXPERTS = 32
CAP = 16
SCALE = 1.0 / math.sqrt(EMB)
EXTRA = 16
DIGIT = 128
MIB = 1 << 20

F32 = jnp.float32
BF16 = jnp.bfloat16
CORES = 2
SCALARS = pl.BlockSpec(memory_space=pltpu.SMEM)
WHOLE = pl.BlockSpec(memory_space=pltpu.VMEM)
ANYWHERE = pl.BlockSpec(memory_space=pl.ANY)
VMEM = 60 * MIB
SMALL = pl.CostEstimate(flops=1024, bytes_accessed=1024, transcendentals=0)


def mm(a, b, ca, cb):
    return lax.dot_general(a, b, (((ca,), (cb,)), ((), ())), preferred_element_type=F32)


def number(rows, index):
    rows = rows.astype(F32)
    high = rows[2 * index : 2 * index + 1]
    return (high * DIGIT + rows[2 * index + 1 : 2 * index + 2]).astype(jnp.int32)


def swap(piece, axis, bits):
    size = lax.axis_size(axis)
    return lax.ppermute(piece, axis, [(j, j ^ bits) for j in range(size)])


def exchange(pieces, axis, unit=1):
    return [piece if k == 0 else swap(piece, axis, k * unit) for k, piece in enumerate(pieces)]


def pack_kernel(emb_ref, positive_ref, user_ref, item_ref, out_ref, target_ref):
    rows = emb_ref.shape[0]
    down = lax.broadcasted_iota(jnp.int32, (rows, rows), 0)
    across = lax.broadcasted_iota(jnp.int32, (rows, rows), 1)

    def slots(expert):
        wide = jnp.broadcast_to(expert.astype(F32), (rows, rows))
        before = jnp.where((wide == wide.T) & (down < across), 1.0, 0.0)
        return expert * CAP + jnp.sum(before, axis=0, keepdims=True).astype(jnp.int32)

    user = slots(user_ref[...])
    item = slots(item_ref[...])
    target_ref[0:1, :] = user
    target_ref[1:2, :] = item
    line = lax.broadcasted_iota(jnp.int32, (EXTRA, rows), 0)
    block = jnp.zeros((EXTRA, rows), jnp.int32)
    for index, values in enumerate((positive_ref[...], user, item)):
        block = jnp.where(line == 2 * index, values // DIGIT, block)
        block = jnp.where(line == 2 * index + 1, values % DIGIT, block)
    out_ref[:rows, :] = emb_ref[...]
    out_ref[rows:, :] = block.astype(F32).astype(BF16)


def pack(emb, positive, user_expert, item_expert):
    rows, width = emb.shape
    return pl.pallas_call(
        pack_kernel,
        out_shape=[
            jax.ShapeDtypeStruct((rows + EXTRA, width), BF16),
            jax.ShapeDtypeStruct((2, rows), jnp.int32),
        ],
        compiler_params=pltpu.CompilerParams(vmem_limit_bytes=VMEM),
        cost_estimate=SMALL,
    )(emb, positive.reshape(1, rows), user_expert.reshape(1, rows), item_expert.reshape(1, rows))


def stats_kernel(first_ref, users_ref, *refs, rows, chunk):
    *items_refs, _, out_ref, s_ref = refs
    own = items_refs[0].shape[0]
    n_cols = own * len(items_refs)
    for half in range(users_ref.shape[0]):
        queries = users_ref[half, :rows, :] * jnp.asarray(SCALE, BF16)
        for k, items_ref in enumerate(items_refs):
            s_ref[half, k * own : (k + 1) * own, :] = mm(items_ref[...], queries, 1, 1)
        positive = number(users_ref[half, rows:, :], 0)
        tops = jnp.full((8, rows), -jnp.inf, F32)
        for c in range(0, n_cols, chunk):
            part = s_ref[half, c : c + chunk, :]
            tops = jnp.maximum(tops, jnp.max(part.reshape(chunk // 8, 8, rows), axis=0))
        top = jnp.max(tops, axis=0, keepdims=True)
        total = jnp.zeros((8, rows), F32)
        picked = jnp.zeros((8, rows), F32)
        for c in range(0, n_cols, chunk):
            part = s_ref[half, c : c + chunk, :]
            probs = jnp.exp(part - top)
            total = total + jnp.sum(probs.reshape(chunk // 8, 8, rows), axis=0)
            wanted = positive - (first_ref[c // own] + c % own)
            hit = lax.broadcasted_iota(jnp.int32, (chunk, rows), 0) == wanted
            chosen = jnp.where(hit, part, 0.0)
            picked = picked + jnp.sum(chosen.reshape(chunk // 8, 8, rows), axis=0)
        here = pl.ds(half * rows, rows)
        out_ref[0:1, here] = top
        out_ref[1:2, here] = jnp.sum(total, axis=0, keepdims=True)
        out_ref[2:3, here] = jnp.sum(picked, axis=0, keepdims=True)


def stats(first, users, items, rows, after):
    blocks, height, emb = users.shape
    own = items[0].shape[0]
    n_cols = own * len(items)
    pair = 2
    return pl.pallas_call(
        functools.partial(stats_kernel, rows=rows, chunk=64),
        grid=(blocks // pair,),
        in_specs=[SCALARS, pl.BlockSpec((pair, height, emb), lambda b: (b, 0, 0))]
        + [pl.BlockSpec((own, emb), lambda b: (0, 0))] * len(items)
        + [ANYWHERE],
        out_specs=pl.BlockSpec((3, pair * rows), lambda b: (0, b)),
        out_shape=jax.ShapeDtypeStruct((3, blocks * rows), F32),
        scratch_shapes=[pltpu.VMEM((pair, n_cols, rows), F32)],
        compiler_params=pltpu.CompilerParams(vmem_limit_bytes=VMEM),
        cost_estimate=SMALL,
    )(first, users, *items, after)


def grad_kernel(first_ref, users_ref, *refs, rows, chunk, count, groups):
    stats_refs, refs = refs[:groups], refs[groups:]
    items_refs, refs = refs[:count], refs[count + 1 :]
    loss_ref, user_ref = refs[:2]
    part_refs = refs[2 : count + 2]
    s_ref, g_ref, flip_ref = refs[count + 2 :]
    own = items_refs[0].shape[0]
    n_cols = own * count
    step = pl.program_id(0)

    @pl.when(step == 0)
    def _():
        for k in range(count):
            flip_ref[:, k * own : (k + 1) * own] = items_refs[k][...].T
            part_refs[k][...] = jnp.zeros_like(part_refs[k])

    for half in range(users_ref.shape[0]):
        here = pl.ds(half * rows, rows)
        queries = users_ref[half, :rows, :]
        scaled = queries * jnp.asarray(SCALE, BF16)
        for k in range(count):
            s_ref[half, k * own : (k + 1) * own, :] = mm(items_refs[k][...], scaled, 1, 1)
        positive = number(users_ref[half, rows:, :], 0)
        top = functools.reduce(jnp.maximum, [ref[0:1, here] for ref in stats_refs])
        total = sum(ref[1:2, here] * jnp.exp(ref[0:1, here] - top) for ref in stats_refs)
        level = top + jnp.log(total)
        loss_ref[0:1, here] = level - sum(ref[2:3, here] for ref in stats_refs)
        for c in range(0, n_cols, chunk):
            probs = jnp.exp(s_ref[half, c : c + chunk, :] - level)
            wanted = positive - (first_ref[c // own] + c % own)
            hit = lax.broadcasted_iota(jnp.int32, (chunk, rows), 0) == wanted
            g_ref[half, c : c + chunk, :] = jnp.where(hit, probs - 1.0, probs).astype(BF16)
        for k in range(count):
            part_refs[k][...] += mm(g_ref[half, k * own : (k + 1) * own, :], queries, 1, 0)
        user_ref[here, :] = mm(flip_ref[...], g_ref[half], 1, 0).T * SCALE

    @pl.when(step == pl.num_programs(0) - 1)
    def _():
        for k in range(count):
            part_refs[k][...] = part_refs[k][...] * SCALE


def grads(first, users, items, gathered, rows, after):
    blocks, height, emb = users.shape
    count = len(items)
    own = items[0].shape[0]
    n_cols = own * count
    pair = 2
    groups = len(gathered)
    results = pl.pallas_call(
        functools.partial(grad_kernel, rows=rows, chunk=64, count=count, groups=groups),
        grid=(blocks // pair,),
        in_specs=[
            SCALARS,
            pl.BlockSpec((pair, height, emb), lambda b: (b, 0, 0)),
        ]
        + [pl.BlockSpec((3, pair * rows), lambda b: (0, b))] * groups
        + [pl.BlockSpec((own, emb), lambda b: (0, 0))] * count
        + [ANYWHERE],
        out_specs=[
            pl.BlockSpec((1, pair * rows), lambda b: (0, b)),
            pl.BlockSpec((pair * rows, emb), lambda b: (b, 0)),
        ]
        + [pl.BlockSpec((own, emb), lambda b: (0, 0))] * count,
        out_shape=[
            jax.ShapeDtypeStruct((1, blocks * rows), F32),
            jax.ShapeDtypeStruct((blocks * rows, emb), F32),
        ]
        + [jax.ShapeDtypeStruct((own, emb), F32)] * count,
        scratch_shapes=[
            pltpu.VMEM((pair, n_cols, rows), F32),
            pltpu.VMEM((pair, n_cols, rows), BF16),
            pltpu.VMEM((emb, n_cols), BF16),
        ],
        compiler_params=pltpu.CompilerParams(vmem_limit_bytes=VMEM),
        cost_estimate=SMALL,
    )(first, users, *gathered, *items, after)
    return results[0], results[1], results[2:]


def cut_kernel(in_ref, _, out_ref):
    width = out_ref.shape[2]
    for k in range(out_ref.shape[0]):
        out_ref[k] = in_ref[:, k * width : (k + 1) * width]


def cut(hidden, parts, after):
    rows, total = hidden.shape
    return pl.pallas_call(
        cut_kernel,
        in_specs=[WHOLE, ANYWHERE],
        out_specs=WHOLE,
        out_shape=jax.ShapeDtypeStruct((parts, rows, total // parts), BF16),
        compiler_params=pltpu.CompilerParams(vmem_limit_bytes=VMEM),
        cost_estimate=SMALL,
    )(hidden, after)


def onehot_of(target, me, groups):
    span = EXPERTS * CAP // groups
    place = lax.broadcasted_iota(jnp.int32, (EXPERTS * CAP, target.shape[1]), 0)
    place = (((place // span) ^ me) * span) + place % span
    return (place == target).astype(F32).astype(BF16)


def hidden_kernel(me_ref, users_ref, hidden_ref, _, *out_refs, tower):
    count, (pair, span, _) = len(out_refs), out_refs[0].shape[-3:]
    groups = out_refs[0].shape[0] if count == 1 else count
    me = 0 if count == 1 else me_ref[0]
    for half in range(pair):
        onehot = onehot_of(number(users_ref[half], 1 + tower), me, groups)
        moved = mm(onehot, hidden_ref[half], 1, 0).astype(BF16)
        for k in range(groups):
            part = moved[k * span : (k + 1) * span, :]
            if count == 1:
                out_refs[0][k, half] = part
            else:
                out_refs[k][half] = part


def slot_hidden(me, users, hidden, groups, tower, apart, after):
    blocks, rows, width = hidden.shape
    span = EXPERTS * CAP // groups
    pair = 2
    if apart:
        out_specs = [pl.BlockSpec((pair, span, width), lambda b: (b, 0, 0))] * groups
        out_shape = [jax.ShapeDtypeStruct((blocks, span, width), BF16)] * groups
    else:
        out_specs = [pl.BlockSpec((groups, pair, span, width), lambda b: (0, b, 0, 0))]
        out_shape = [jax.ShapeDtypeStruct((groups, blocks, span, width), BF16)]
    return pl.pallas_call(
        functools.partial(hidden_kernel, tower=tower),
        grid=(blocks // pair,),
        in_specs=[
            SCALARS,
            pl.BlockSpec((pair, EXTRA, rows), lambda b: (b, rows // EXTRA, 0)),
            pl.BlockSpec((pair, rows, width), lambda b: (b, 0, 0)),
            ANYWHERE,
        ],
        out_specs=out_specs,
        out_shape=out_shape,
        compiler_params=pltpu.CompilerParams(vmem_limit_bytes=VMEM),
        cost_estimate=SMALL,
    )(me, users, hidden, after)


def route_kernel(me_ref, target_ref, *refs, tower, count, order):
    total = refs[0][...]
    for ref in refs[1:count]:
        total = total + ref[...]
    low = total.astype(BF16)
    out_refs = refs[count + order :]
    span = out_refs[0].shape[0]
    onehot = onehot_of(target_ref[tower : tower + 1, :], me_ref[0], len(out_refs))
    moved = mm(onehot, low, 1, 0).astype(BF16)
    for k, out_ref in enumerate(out_refs):
        out_ref[...] = moved[k * span : (k + 1) * span, :]


def route(me, targets, pieces, tower, groups, after):
    rows, emb = pieces[0].shape
    span = EXPERTS * CAP // groups
    return pl.pallas_call(
        functools.partial(route_kernel, tower=tower, count=len(pieces), order=len(after)),
        in_specs=[SCALARS] + [WHOLE] * (1 + len(pieces)) + [ANYWHERE] * len(after),
        out_specs=[WHOLE] * groups,
        out_shape=[jax.ShapeDtypeStruct((span, emb), BF16)] * groups,
        compiler_params=pltpu.CompilerParams(vmem_limit_bytes=VMEM),
        cost_estimate=SMALL,
    )(me, targets, *pieces, *after)


def stack_kernel(*refs, count):
    for k in range(count):
        refs[-1][k] = refs[k][...]


def stack(pieces, after=()):
    return pl.pallas_call(
        functools.partial(stack_kernel, count=len(pieces)),
        in_specs=[WHOLE] * len(pieces) + [ANYWHERE] * len(after),
        out_specs=WHOLE,
        out_shape=jax.ShapeDtypeStruct((len(pieces),) + pieces[0].shape, pieces[0].dtype),
        compiler_params=pltpu.CompilerParams(vmem_limit_bytes=VMEM),
        cost_estimate=SMALL,
    )(*pieces, *after)


def outer_kernel(order_ref, me_ref, *refs, count):
    hidden_refs, grad_refs, out_ref = refs[:count], refs[count:-1], refs[-1]
    blocks, span, _ = hidden_refs[0].shape[-3:]
    groups = hidden_refs[0].shape[0] if count == 1 else count
    for e in range(span // CAP):
        here = slice(e * CAP, (e + 1) * CAP)
        left, right = [], []
        for j in range(blocks):
            block = j if len(grad_refs) == 1 else order_ref[j]
            for k in range(groups):
                if count == 1:
                    left.append(hidden_refs[0][me_ref[0] ^ k, block, here, :])
                else:
                    left.append(hidden_refs[k][block, here, :])
                if len(grad_refs) == 1:
                    right.append(grad_refs[0][j, k, here, :])
                else:
                    right.append(grad_refs[j][k, here, :])
        out_ref[e] = mm(jnp.concatenate(left), jnp.concatenate(right), 0, 0)


def outer(order, me, hidden, grads, cost):
    span, width = hidden[0].shape[-2:]
    emb = grads[0].shape[-1]
    own = span // CAP
    steps = 2

    def part(array):
        front = array.shape[:-2]
        return pl.BlockSpec(
            front + (span // steps, array.shape[-1]), lambda e, d=len(front): (0,) * d + (e, 0)
        )

    return pl.pallas_call(
        functools.partial(outer_kernel, count=len(hidden)),
        grid=(steps,),
        in_specs=[SCALARS, SCALARS] + [part(array) for array in hidden + grads],
        out_specs=pl.BlockSpec((own // steps, width, emb), lambda e: (e, 0, 0)),
        out_shape=jax.ShapeDtypeStruct((own, width, emb), F32),
        compiler_params=pltpu.CompilerParams(vmem_limit_bytes=VMEM),
        cost_estimate=cost,
    )(order, me, *hidden, *grads)


def shards(user_emb, item_emb, user_hidden, item_hidden, user_expert, item_expert, positive):
    rows, emb = user_emb.shape
    groups = lax.axis_size("user")
    parts = lax.axis_size("item")
    width = user_hidden.shape[1] // parts
    lines = parts // CORES
    me = lax.axis_index("user").astype(jnp.int32)
    part = lax.axis_index("item").astype(jnp.int32)
    others = me ^ jnp.arange(groups, dtype=jnp.int32)
    both = part ^ jnp.arange(CORES, dtype=jnp.int32)
    order = (both[:, None] ^ (CORES * jnp.arange(lines, dtype=jnp.int32))[None, :]).reshape(-1)
    first = (part * groups + others) * rows
    me = me.reshape(1)

    packed, targets = pack(user_emb, positive, user_expert, item_expert)
    users = lax.all_gather(packed, "item", axis=0)
    items = exchange([item_emb] * groups, "user")

    def scatter(pieces, axis):
        return lax.all_to_all(pieces, axis, split_axis=0, concat_axis=0, tiled=True)

    user_cols = scatter(cut(user_hidden, parts, items[1]), "item")
    item_blocks = cut(item_hidden, parts, items[1])
    found = stats(first, users, items, rows, item_blocks)
    item_cols = scatter(item_blocks, "item")
    gathered = exchange([found] * parts, "item")
    losses, user_part, item_parts = grads(first, users, items, gathered, rows, user_cols)
    row_loss = lax.dynamic_slice_in_dim(losses[0], part * rows, rows)
    user_grad = lax.psum_scatter(user_part, "item", scatter_dimension=0, tiled=True)
    item_pieces = exchange(item_parts, "user")

    user_slots = slot_hidden(me, users, user_cols, groups, 0, True, item_parts[0])
    user_rows = exchange(user_slots, "user")
    item_routed = route(me, targets, item_pieces, 1, groups, user_slots[:1])
    item_sent = stack(exchange(item_routed, "user"))
    item_line = exchange([item_sent] * lines, "item", CORES)
    user_routed = route(me, targets, [user_grad], 0, groups, user_rows[1:])
    item_slots = slot_hidden(me, users, item_cols, groups, 1, False, user_routed[0])
    user_sent = stack(exchange(user_routed, "user"), item_line[1:3] + [item_slots[0]])
    item_rows = [scatter(item_slots[0], "user")]
    item_cross = item_line + [swap(piece, "item", 1) for piece in item_line]
    user_all = lax.all_gather(user_sent, "item", axis=0)
    item_weight_grad = outer(order, me, item_rows, item_cross, SMALL)
    user_weight_grad = outer(order, me, user_rows, [user_all], SMALL)
    return (row_loss, user_weight_grad, item_weight_grad)


def solution(mesh):
    placed = (
        P(("user", "item"), None),
        P(("item", "user"), None),
        P(("user", "item"), None),
        P(("item", "user"), None),
        P(("user", "item"), None),
        P(("item", "user"), None),
        P(("user", "item")),
    )
    return jax.shard_map(
        shards,
        mesh=mesh,
        in_specs=placed,
        out_specs=(P(("user", "item")), P("user", "item", None), P("user", "item", None)),
        check_vma=False,
    )
```

```python
import functools
import math

import jax
import jax.numpy as jnp
from jax import lax
from jax.experimental import pallas as pl
from jax.experimental.pallas import tpu as pltpu
from jax.sharding import PartitionSpec as P

EMB = 256
EXPERTS = 32
CAP = 16
SCALE = 1.0 / math.sqrt(EMB)
EXTRA = 16
DIGIT = 128
MIB = 1 << 20

F32 = jnp.float32
BF16 = jnp.bfloat16
CORES = 2
SCALARS = pl.BlockSpec(memory_space=pltpu.SMEM)
WHOLE = pl.BlockSpec(memory_space=pltpu.VMEM)
ANYWHERE = pl.BlockSpec(memory_space=pl.ANY)
VMEM = 60 * MIB
SMALL = pl.CostEstimate(flops=1024, bytes_accessed=1024, transcendentals=0)


def mm(a, b, ca, cb):
    return lax.dot_general(a, b, (((ca,), (cb,)), ((), ())), preferred_element_type=F32)


def number(rows, index):
    rows = rows.astype(F32)
    high = rows[2 * index : 2 * index + 1]
    return (high * DIGIT + rows[2 * index + 1 : 2 * index + 2]).astype(jnp.int32)


def swap(piece, axis, bits):
    size = lax.axis_size(axis)
    return lax.ppermute(piece, axis, [(j, j ^ bits) for j in range(size)])


def exchange(pieces, axis, unit=1):
    return [piece if k == 0 else swap(piece, axis, k * unit) for k, piece in enumerate(pieces)]


def pack_kernel(emb_ref, positive_ref, user_ref, item_ref, out_ref, target_ref):
    rows = emb_ref.shape[0]
    down = lax.broadcasted_iota(jnp.int32, (rows, rows), 0)
    across = lax.broadcasted_iota(jnp.int32, (rows, rows), 1)

    def slots(expert):
        wide = jnp.broadcast_to(expert.astype(F32), (rows, rows))
        before = jnp.where((wide == wide.T) & (down < across), 1.0, 0.0)
        return expert * CAP + jnp.sum(before, axis=0, keepdims=True).astype(jnp.int32)

    user = slots(user_ref[...])
    item = slots(item_ref[...])
    target_ref[0:1, :] = user
    target_ref[1:2, :] = item
    line = lax.broadcasted_iota(jnp.int32, (EXTRA, rows), 0)
    block = jnp.zeros((EXTRA, rows), jnp.int32)
    for index, values in enumerate((positive_ref[...], user, item)):
        block = jnp.where(line == 2 * index, values // DIGIT, block)
        block = jnp.where(line == 2 * index + 1, values % DIGIT, block)
    out_ref[:rows, :] = emb_ref[...]
    out_ref[rows:, :] = block.astype(F32).astype(BF16)


def pack(emb, positive, user_expert, item_expert):
    rows, width = emb.shape
    return pl.pallas_call(
        pack_kernel,
        out_shape=[
            jax.ShapeDtypeStruct((rows + EXTRA, width), BF16),
            jax.ShapeDtypeStruct((2, rows), jnp.int32),
        ],
        compiler_params=pltpu.CompilerParams(vmem_limit_bytes=VMEM),
        cost_estimate=SMALL,
    )(emb, positive.reshape(1, rows), user_expert.reshape(1, rows), item_expert.reshape(1, rows))


def stats_kernel(first_ref, users_ref, *refs, rows, chunk):
    *items_refs, _, out_ref, s_ref = refs
    own = items_refs[0].shape[0]
    n_cols = own * len(items_refs)
    for half in range(users_ref.shape[0]):
        queries = users_ref[half, :rows, :] * jnp.asarray(SCALE, BF16)
        for k, items_ref in enumerate(items_refs):
            s_ref[half, k * own : (k + 1) * own, :] = mm(items_ref[...], queries, 1, 1)
        positive = number(users_ref[half, rows:, :], 0)
        tops = jnp.full((8, rows), -jnp.inf, F32)
        for c in range(0, n_cols, chunk):
            part = s_ref[half, c : c + chunk, :]
            tops = jnp.maximum(tops, jnp.max(part.reshape(chunk // 8, 8, rows), axis=0))
        top = jnp.max(tops, axis=0, keepdims=True)
        total = jnp.zeros((8, rows), F32)
        picked = jnp.zeros((8, rows), F32)
        for c in range(0, n_cols, chunk):
            part = s_ref[half, c : c + chunk, :]
            probs = jnp.exp(part - top)
            total = total + jnp.sum(probs.reshape(chunk // 8, 8, rows), axis=0)
            wanted = positive - (first_ref[c // own] + c % own)
            hit = lax.broadcasted_iota(jnp.int32, (chunk, rows), 0) == wanted
            chosen = jnp.where(hit, part, 0.0)
            picked = picked + jnp.sum(chosen.reshape(chunk // 8, 8, rows), axis=0)
        here = pl.ds(half * rows, rows)
        out_ref[0:1, here] = top
        out_ref[1:2, here] = jnp.sum(total, axis=0, keepdims=True)
        out_ref[2:3, here] = jnp.sum(picked, axis=0, keepdims=True)


def stats(first, users, items, rows, after):
    blocks, height, emb = users.shape
    own = items[0].shape[0]
    n_cols = own * len(items)
    pair = 2
    return pl.pallas_call(
        functools.partial(stats_kernel, rows=rows, chunk=64),
        grid=(blocks // pair,),
        in_specs=[SCALARS, pl.BlockSpec((pair, height, emb), lambda b: (b, 0, 0))]
        + [pl.BlockSpec((own, emb), lambda b: (0, 0))] * len(items)
        + [ANYWHERE],
        out_specs=pl.BlockSpec((3, pair * rows), lambda b: (0, b)),
        out_shape=jax.ShapeDtypeStruct((3, blocks * rows), F32),
        scratch_shapes=[pltpu.VMEM((pair, n_cols, rows), F32)],
        compiler_params=pltpu.CompilerParams(vmem_limit_bytes=VMEM),
        cost_estimate=SMALL,
    )(first, users, *items, after)


def grad_kernel(first_ref, users_ref, *refs, rows, chunk, count, groups):
    stats_refs, refs = refs[:groups], refs[groups:]
    items_refs, refs = refs[:count], refs[count + 1 :]
    loss_ref, user_ref = refs[:2]
    part_refs = refs[2 : count + 2]
    s_ref, g_ref, flip_ref = refs[count + 2 :]
    own = items_refs[0].shape[0]
    n_cols = own * count
    step = pl.program_id(0)

    @pl.when(step == 0)
    def _():
        for k in range(count):
            flip_ref[:, k * own : (k + 1) * own] = items_refs[k][...].T
            part_refs[k][...] = jnp.zeros_like(part_refs[k])

    for half in range(users_ref.shape[0]):
        here = pl.ds(half * rows, rows)
        queries = users_ref[half, :rows, :]
        scaled = queries * jnp.asarray(SCALE, BF16)
        for k in range(count):
            s_ref[half, k * own : (k + 1) * own, :] = mm(items_refs[k][...], scaled, 1, 1)
        positive = number(users_ref[half, rows:, :], 0)
        top = functools.reduce(jnp.maximum, [ref[0:1, here] for ref in stats_refs])
        total = sum(ref[1:2, here] * jnp.exp(ref[0:1, here] - top) for ref in stats_refs)
        level = top + jnp.log(total)
        loss_ref[0:1, here] = level - sum(ref[2:3, here] for ref in stats_refs)
        for c in range(0, n_cols, chunk):
            probs = jnp.exp(s_ref[half, c : c + chunk, :] - level)
            wanted = positive - (first_ref[c // own] + c % own)
            hit = lax.broadcasted_iota(jnp.int32, (chunk, rows), 0) == wanted
            g_ref[half, c : c + chunk, :] = jnp.where(hit, probs - 1.0, probs).astype(BF16)
        for k in range(count):
            part_refs[k][...] += mm(g_ref[half, k * own : (k + 1) * own, :], queries, 1, 0)
        user_ref[here, :] = mm(flip_ref[...], g_ref[half], 1, 0).T * SCALE

    @pl.when(step == pl.num_programs(0) - 1)
    def _():
        for k in range(count):
            part_refs[k][...] = part_refs[k][...] * SCALE


def grads(first, users, items, gathered, rows, after):
    blocks, height, emb = users.shape
    count = len(items)
    own = items[0].shape[0]
    n_cols = own * count
    pair = 2
    groups = len(gathered)
    results = pl.pallas_call(
        functools.partial(grad_kernel, rows=rows, chunk=64, count=count, groups=groups),
        grid=(blocks // pair,),
        in_specs=[
            SCALARS,
            pl.BlockSpec((pair, height, emb), lambda b: (b, 0, 0)),
        ]
        + [pl.BlockSpec((3, pair * rows), lambda b: (0, b))] * groups
        + [pl.BlockSpec((own, emb), lambda b: (0, 0))] * count
        + [ANYWHERE],
        out_specs=[
            pl.BlockSpec((1, pair * rows), lambda b: (0, b)),
            pl.BlockSpec((pair * rows, emb), lambda b: (b, 0)),
        ]
        + [pl.BlockSpec((own, emb), lambda b: (0, 0))] * count,
        out_shape=[
            jax.ShapeDtypeStruct((1, blocks * rows), F32),
            jax.ShapeDtypeStruct((blocks * rows, emb), F32),
        ]
        + [jax.ShapeDtypeStruct((own, emb), F32)] * count,
        scratch_shapes=[
            pltpu.VMEM((pair, n_cols, rows), F32),
            pltpu.VMEM((pair, n_cols, rows), BF16),
            pltpu.VMEM((emb, n_cols), BF16),
        ],
        compiler_params=pltpu.CompilerParams(vmem_limit_bytes=VMEM),
        cost_estimate=SMALL,
    )(first, users, *gathered, *items, after)
    return results[0], results[1], results[2:]


def cut_kernel(in_ref, _, out_ref):
    width = out_ref.shape[2]
    for k in range(out_ref.shape[0]):
        out_ref[k] = in_ref[:, k * width : (k + 1) * width]


def cut(hidden, parts, after):
    rows, total = hidden.shape
    return pl.pallas_call(
        cut_kernel,
        in_specs=[WHOLE, ANYWHERE],
        out_specs=WHOLE,
        out_shape=jax.ShapeDtypeStruct((parts, rows, total // parts), BF16),
        compiler_params=pltpu.CompilerParams(vmem_limit_bytes=VMEM),
        cost_estimate=SMALL,
    )(hidden, after)


def onehot_of(target, me, groups):
    span = EXPERTS * CAP // groups
    place = lax.broadcasted_iota(jnp.int32, (EXPERTS * CAP, target.shape[1]), 0)
    place = (((place // span) ^ me) * span) + place % span
    return (place == target).astype(F32).astype(BF16)


def hidden_kernel(me_ref, users_ref, hidden_ref, *refs, tower, order):
    out_refs = refs[order:]
    count, (pair, span, _) = len(out_refs), out_refs[0].shape[-3:]
    groups = out_refs[0].shape[0] if count == 1 else count
    me = 0 if count == 1 else me_ref[0]
    for half in range(pair):
        onehot = onehot_of(number(users_ref[half], 1 + tower), me, groups)
        moved = mm(onehot, hidden_ref[half], 1, 0).astype(BF16)
        for k in range(groups):
            part = moved[k * span : (k + 1) * span, :]
            if count == 1:
                out_refs[0][k, half] = part
            else:
                out_refs[k][half] = part


def slot_hidden(me, users, hidden, groups, tower, apart, after):
    blocks, rows, width = hidden.shape
    span = EXPERTS * CAP // groups
    pair = 2
    if apart:
        out_specs = [pl.BlockSpec((pair, span, width), lambda b: (b, 0, 0))] * groups
        out_shape = [jax.ShapeDtypeStruct((blocks, span, width), BF16)] * groups
    else:
        out_specs = [pl.BlockSpec((groups, pair, span, width), lambda b: (0, b, 0, 0))]
        out_shape = [jax.ShapeDtypeStruct((groups, blocks, span, width), BF16)]
    return pl.pallas_call(
        functools.partial(hidden_kernel, tower=tower, order=len(after)),
        grid=(blocks // pair,),
        in_specs=[
            SCALARS,
            pl.BlockSpec((pair, EXTRA, rows), lambda b: (b, rows // EXTRA, 0)),
            pl.BlockSpec((pair, rows, width), lambda b: (b, 0, 0)),
        ]
        + [ANYWHERE] * len(after),
        out_specs=out_specs,
        out_shape=out_shape,
        compiler_params=pltpu.CompilerParams(vmem_limit_bytes=VMEM),
        cost_estimate=SMALL,
    )(me, users, hidden, *after)


def route_kernel(me_ref, target_ref, *refs, tower, count, order):
    total = refs[0][...]
    for ref in refs[1:count]:
        total = total + ref[...]
    low = total.astype(BF16)
    out_refs = refs[count + order :]
    span = out_refs[0].shape[0]
    onehot = onehot_of(target_ref[tower : tower + 1, :], me_ref[0], len(out_refs))
    moved = mm(onehot, low, 1, 0).astype(BF16)
    for k, out_ref in enumerate(out_refs):
        out_ref[...] = moved[k * span : (k + 1) * span, :]


def route(me, targets, pieces, tower, groups, after):
    rows, emb = pieces[0].shape
    span = EXPERTS * CAP // groups
    return pl.pallas_call(
        functools.partial(route_kernel, tower=tower, count=len(pieces), order=len(after)),
        in_specs=[SCALARS] + [WHOLE] * (1 + len(pieces)) + [ANYWHERE] * len(after),
        out_specs=[WHOLE] * groups,
        out_shape=[jax.ShapeDtypeStruct((span, emb), BF16)] * groups,
        compiler_params=pltpu.CompilerParams(vmem_limit_bytes=VMEM),
        cost_estimate=SMALL,
    )(me, targets, *pieces, *after)


def stack_kernel(*refs, count):
    for k in range(count):
        refs[-1][k] = refs[k][...]


def stack(pieces, after=()):
    return pl.pallas_call(
        functools.partial(stack_kernel, count=len(pieces)),
        in_specs=[WHOLE] * len(pieces) + [ANYWHERE] * len(after),
        out_specs=WHOLE,
        out_shape=jax.ShapeDtypeStruct((len(pieces),) + pieces[0].shape, pieces[0].dtype),
        compiler_params=pltpu.CompilerParams(vmem_limit_bytes=VMEM),
        cost_estimate=SMALL,
    )(*pieces, *after)


def outer_kernel(order_ref, me_ref, *refs, count):
    hidden_refs, grad_refs, out_ref = refs[:count], refs[count:-1], refs[-1]
    blocks, span, _ = hidden_refs[0].shape[-3:]
    groups = hidden_refs[0].shape[0] if count == 1 else count
    for e in range(span // CAP):
        here = slice(e * CAP, (e + 1) * CAP)
        left, right = [], []
        for j in range(blocks):
            block = j if len(grad_refs) == 1 else order_ref[j]
            for k in range(groups):
                if count == 1:
                    left.append(hidden_refs[0][me_ref[0] ^ k, block, here, :])
                else:
                    left.append(hidden_refs[k][block, here, :])
                if len(grad_refs) == 1:
                    right.append(grad_refs[0][j, k, here, :])
                else:
                    right.append(grad_refs[j][k, here, :])
        out_ref[e] = mm(jnp.concatenate(left), jnp.concatenate(right), 0, 0)


def outer(order, me, hidden, grads, cost):
    span, width = hidden[0].shape[-2:]
    emb = grads[0].shape[-1]
    own = span // CAP
    steps = 2

    def part(array):
        front = array.shape[:-2]
        return pl.BlockSpec(
            front + (span // steps, array.shape[-1]), lambda e, d=len(front): (0,) * d + (e, 0)
        )

    return pl.pallas_call(
        functools.partial(outer_kernel, count=len(hidden)),
        grid=(steps,),
        in_specs=[SCALARS, SCALARS] + [part(array) for array in hidden + grads],
        out_specs=pl.BlockSpec((own // steps, width, emb), lambda e: (e, 0, 0)),
        out_shape=jax.ShapeDtypeStruct((own, width, emb), F32),
        compiler_params=pltpu.CompilerParams(vmem_limit_bytes=VMEM),
        cost_estimate=cost,
    )(order, me, *hidden, *grads)


def shards(user_emb, item_emb, user_hidden, item_hidden, user_expert, item_expert, positive):
    rows, emb = user_emb.shape
    groups = lax.axis_size("user")
    parts = lax.axis_size("item")
    width = user_hidden.shape[1] // parts
    lines = parts // CORES
    me = lax.axis_index("user").astype(jnp.int32)
    part = lax.axis_index("item").astype(jnp.int32)
    others = me ^ jnp.arange(groups, dtype=jnp.int32)
    both = part ^ jnp.arange(CORES, dtype=jnp.int32)
    order = (both[:, None] ^ (CORES * jnp.arange(lines, dtype=jnp.int32))[None, :]).reshape(-1)
    first = (part * groups + others) * rows
    me = me.reshape(1)

    packed, targets = pack(user_emb, positive, user_expert, item_expert)
    users = lax.all_gather(packed, "item", axis=0)
    items = exchange([item_emb] * groups, "user")

    def scatter(pieces, axis):
        return lax.all_to_all(pieces, axis, split_axis=0, concat_axis=0, tiled=True)

    user_cols = scatter(cut(user_hidden, parts, items[1]), "item")
    item_blocks = cut(item_hidden, parts, items[1])
    found = stats(first, users, items, rows, item_blocks)
    item_cols = scatter(item_blocks, "item")
    gathered = exchange([found] * parts, "item")
    losses, user_part, item_parts = grads(first, users, items, gathered, rows, user_cols)
    row_loss = lax.dynamic_slice_in_dim(losses[0], part * rows, rows)
    user_grad = lax.psum_scatter(user_part, "item", scatter_dimension=0, tiled=True)
    item_pieces = exchange(item_parts, "user")

    user_slots = slot_hidden(me, users, user_cols, groups, 0, True, item_pieces[1:])
    user_rows = exchange(user_slots, "user")
    item_routed = route(me, targets, item_pieces, 1, groups, user_slots[:1])
    item_sent = stack(exchange(item_routed, "user"))
    item_line = exchange([item_sent] * lines, "item", CORES)
    user_routed = route(me, targets, [user_grad], 0, groups, [item_sent] + user_rows[1:])
    user_sent = stack(exchange(user_routed, "user"), item_line[1:3])
    item_slots = slot_hidden(me, users, item_cols, groups, 1, False, [user_sent])
    item_rows = [scatter(item_slots[0], "user")]
    user_line = exchange([user_sent] * lines, "item", CORES)
    user_cross = user_line + [swap(piece, "item", 1) for piece in user_line]
    item_cross = item_line + [swap(piece, "item", 1) for piece in item_line]
    user_weight_grad = outer(order, me, user_rows, user_cross, SMALL)
    item_weight_grad = outer(order, me, item_rows, item_cross, SMALL)
    return (row_loss, user_weight_grad, item_weight_grad)


def solution(mesh):
    placed = (
        P(("user", "item"), None),
        P(("item", "user"), None),
        P(("user", "item"), None),
        P(("item", "user"), None),
        P(("user", "item"), None),
        P(("item", "user"), None),
        P(("user", "item")),
    )
    return jax.shard_map(
        shards,
        mesh=mesh,
        in_specs=placed,
        out_specs=(P(("user", "item")), P("user", "item", None), P("user", "item", None)),
        check_vma=False,
    )
```

```python
import functools
import math

import jax
import jax.numpy as jnp
from jax import lax
from jax.experimental import pallas as pl
from jax.experimental.pallas import tpu as pltpu
from jax.sharding import PartitionSpec as P

EMB = 256
EXPERTS = 32
CAP = 16
SCALE = 1.0 / math.sqrt(EMB)
EXTRA = 16
DIGIT = 128
MIB = 1 << 20

F32 = jnp.float32
BF16 = jnp.bfloat16
CORES = 2
SCALARS = pl.BlockSpec(memory_space=pltpu.SMEM)
WHOLE = pl.BlockSpec(memory_space=pltpu.VMEM)
ANYWHERE = pl.BlockSpec(memory_space=pl.ANY)
VMEM = 60 * MIB
SMALL = pl.CostEstimate(flops=1024, bytes_accessed=1024, transcendentals=0)


def mm(a, b, ca, cb):
    return lax.dot_general(a, b, (((ca,), (cb,)), ((), ())), preferred_element_type=F32)


def number(rows, index):
    rows = rows.astype(F32)
    high = rows[2 * index : 2 * index + 1]
    return (high * DIGIT + rows[2 * index + 1 : 2 * index + 2]).astype(jnp.int32)


def swap(piece, axis, bits):
    size = lax.axis_size(axis)
    return lax.ppermute(piece, axis, [(j, j ^ bits) for j in range(size)])


def exchange(pieces, axis, unit=1):
    return [piece if k == 0 else swap(piece, axis, k * unit) for k, piece in enumerate(pieces)]


def pack_kernel(emb_ref, positive_ref, user_ref, item_ref, out_ref, target_ref):
    rows = emb_ref.shape[0]
    down = lax.broadcasted_iota(jnp.int32, (rows, rows), 0)
    across = lax.broadcasted_iota(jnp.int32, (rows, rows), 1)

    def slots(expert):
        wide = jnp.broadcast_to(expert.astype(F32), (rows, rows))
        before = jnp.where((wide == wide.T) & (down < across), 1.0, 0.0)
        return expert * CAP + jnp.sum(before, axis=0, keepdims=True).astype(jnp.int32)

    user = slots(user_ref[...])
    item = slots(item_ref[...])
    target_ref[0:1, :] = user
    target_ref[1:2, :] = item
    line = lax.broadcasted_iota(jnp.int32, (EXTRA, rows), 0)
    block = jnp.zeros((EXTRA, rows), jnp.int32)
    for index, values in enumerate((positive_ref[...], user, item)):
        block = jnp.where(line == 2 * index, values // DIGIT, block)
        block = jnp.where(line == 2 * index + 1, values % DIGIT, block)
    out_ref[:rows, :] = emb_ref[...]
    out_ref[rows:, :] = block.astype(F32).astype(BF16)


def pack(emb, positive, user_expert, item_expert):
    rows, width = emb.shape
    return pl.pallas_call(
        pack_kernel,
        out_shape=[
            jax.ShapeDtypeStruct((rows + EXTRA, width), BF16),
            jax.ShapeDtypeStruct((2, rows), jnp.int32),
        ],
        compiler_params=pltpu.CompilerParams(vmem_limit_bytes=VMEM),
        cost_estimate=SMALL,
    )(emb, positive.reshape(1, rows), user_expert.reshape(1, rows), item_expert.reshape(1, rows))


def stats_kernel(first_ref, users_ref, *refs, rows, chunk):
    *items_refs, _, out_ref, s_ref = refs
    own = items_refs[0].shape[0]
    n_cols = own * len(items_refs)
    for half in range(users_ref.shape[0]):
        queries = users_ref[half, :rows, :] * jnp.asarray(SCALE, BF16)
        for k, items_ref in enumerate(items_refs):
            s_ref[half, k * own : (k + 1) * own, :] = mm(items_ref[...], queries, 1, 1)
        positive = number(users_ref[half, rows:, :], 0)
        tops = jnp.full((8, rows), -jnp.inf, F32)
        for c in range(0, n_cols, chunk):
            part = s_ref[half, c : c + chunk, :]
            tops = jnp.maximum(tops, jnp.max(part.reshape(chunk // 8, 8, rows), axis=0))
        top = jnp.max(tops, axis=0, keepdims=True)
        total = jnp.zeros((8, rows), F32)
        picked = jnp.zeros((8, rows), F32)
        for c in range(0, n_cols, chunk):
            part = s_ref[half, c : c + chunk, :]
            probs = jnp.exp(part - top)
            total = total + jnp.sum(probs.reshape(chunk // 8, 8, rows), axis=0)
            wanted = positive - (first_ref[c // own] + c % own)
            hit = lax.broadcasted_iota(jnp.int32, (chunk, rows), 0) == wanted
            chosen = jnp.where(hit, part, 0.0)
            picked = picked + jnp.sum(chosen.reshape(chunk // 8, 8, rows), axis=0)
        here = pl.ds(half * rows, rows)
        out_ref[0:1, here] = top
        out_ref[1:2, here] = jnp.sum(total, axis=0, keepdims=True)
        out_ref[2:3, here] = jnp.sum(picked, axis=0, keepdims=True)


def stats(first, users, items, rows, after):
    blocks, height, emb = users.shape
    own = items[0].shape[0]
    n_cols = own * len(items)
    pair = 2
    return pl.pallas_call(
        functools.partial(stats_kernel, rows=rows, chunk=64),
        grid=(blocks // pair,),
        in_specs=[SCALARS, pl.BlockSpec((pair, height, emb), lambda b: (b, 0, 0))]
        + [pl.BlockSpec((own, emb), lambda b: (0, 0))] * len(items)
        + [ANYWHERE],
        out_specs=pl.BlockSpec((3, pair * rows), lambda b: (0, b)),
        out_shape=jax.ShapeDtypeStruct((3, blocks * rows), F32),
        scratch_shapes=[pltpu.VMEM((pair, n_cols, rows), F32)],
        compiler_params=pltpu.CompilerParams(vmem_limit_bytes=VMEM),
        cost_estimate=SMALL,
    )(first, users, *items, after)


def grad_kernel(first_ref, users_ref, *refs, rows, chunk, count, groups):
    stats_refs, refs = refs[:groups], refs[groups:]
    items_refs, refs = refs[:count], refs[count + 1 :]
    loss_ref, user_ref = refs[:2]
    part_refs = refs[2 : count + 2]
    s_ref, g_ref, flip_ref = refs[count + 2 :]
    own = items_refs[0].shape[0]
    n_cols = own * count
    step = pl.program_id(0)

    @pl.when(step == 0)
    def _():
        for k in range(count):
            flip_ref[:, k * own : (k + 1) * own] = items_refs[k][...].T
            part_refs[k][...] = jnp.zeros_like(part_refs[k])

    for half in range(users_ref.shape[0]):
        here = pl.ds(half * rows, rows)
        queries = users_ref[half, :rows, :]
        scaled = queries * jnp.asarray(SCALE, BF16)
        for k in range(count):
            s_ref[half, k * own : (k + 1) * own, :] = mm(items_refs[k][...], scaled, 1, 1)
        positive = number(users_ref[half, rows:, :], 0)
        top = functools.reduce(jnp.maximum, [ref[0:1, here] for ref in stats_refs])
        total = sum(ref[1:2, here] * jnp.exp(ref[0:1, here] - top) for ref in stats_refs)
        level = top + jnp.log(total)
        loss_ref[0:1, here] = level - sum(ref[2:3, here] for ref in stats_refs)
        for c in range(0, n_cols, chunk):
            probs = jnp.exp(s_ref[half, c : c + chunk, :] - level)
            wanted = positive - (first_ref[c // own] + c % own)
            hit = lax.broadcasted_iota(jnp.int32, (chunk, rows), 0) == wanted
            g_ref[half, c : c + chunk, :] = jnp.where(hit, probs - 1.0, probs).astype(BF16)
        for k in range(count):
            part_refs[k][...] += mm(g_ref[half, k * own : (k + 1) * own, :], queries, 1, 0)
        user_ref[here, :] = mm(flip_ref[...], g_ref[half], 1, 0).T * SCALE

    @pl.when(step == pl.num_programs(0) - 1)
    def _():
        for k in range(count):
            part_refs[k][...] = part_refs[k][...] * SCALE


def grads(first, users, items, gathered, rows, after):
    blocks, height, emb = users.shape
    count = len(items)
    own = items[0].shape[0]
    n_cols = own * count
    pair = 2
    groups = len(gathered)
    results = pl.pallas_call(
        functools.partial(grad_kernel, rows=rows, chunk=64, count=count, groups=groups),
        grid=(blocks // pair,),
        in_specs=[
            SCALARS,
            pl.BlockSpec((pair, height, emb), lambda b: (b, 0, 0)),
        ]
        + [pl.BlockSpec((3, pair * rows), lambda b: (0, b))] * groups
        + [pl.BlockSpec((own, emb), lambda b: (0, 0))] * count
        + [ANYWHERE],
        out_specs=[
            pl.BlockSpec((1, pair * rows), lambda b: (0, b)),
            pl.BlockSpec((pair * rows, emb), lambda b: (b, 0)),
        ]
        + [pl.BlockSpec((own, emb), lambda b: (0, 0))] * count,
        out_shape=[
            jax.ShapeDtypeStruct((1, blocks * rows), F32),
            jax.ShapeDtypeStruct((blocks * rows, emb), F32),
        ]
        + [jax.ShapeDtypeStruct((own, emb), F32)] * count,
        scratch_shapes=[
            pltpu.VMEM((pair, n_cols, rows), F32),
            pltpu.VMEM((pair, n_cols, rows), BF16),
            pltpu.VMEM((emb, n_cols), BF16),
        ],
        compiler_params=pltpu.CompilerParams(vmem_limit_bytes=VMEM),
        cost_estimate=SMALL,
    )(first, users, *gathered, *items, after)
    return results[0], results[1], results[2:]


def cut_kernel(in_ref, _, out_ref):
    width = out_ref.shape[2]
    for k in range(out_ref.shape[0]):
        out_ref[k] = in_ref[:, k * width : (k + 1) * width]


def cut(hidden, parts, after):
    rows, total = hidden.shape
    return pl.pallas_call(
        cut_kernel,
        in_specs=[WHOLE, ANYWHERE],
        out_specs=WHOLE,
        out_shape=jax.ShapeDtypeStruct((parts, rows, total // parts), BF16),
        compiler_params=pltpu.CompilerParams(vmem_limit_bytes=VMEM),
        cost_estimate=SMALL,
    )(hidden, after)


def onehot_of(target, me, groups):
    span = EXPERTS * CAP // groups
    place = lax.broadcasted_iota(jnp.int32, (EXPERTS * CAP, target.shape[1]), 0)
    place = (((place // span) ^ me) * span) + place % span
    return (place == target).astype(F32).astype(BF16)


def hidden_kernel(me_ref, users_ref, hidden_ref, _, *out_refs, tower):
    count, (pair, span, _) = len(out_refs), out_refs[0].shape[-3:]
    groups = out_refs[0].shape[0] if count == 1 else count
    me = 0 if count == 1 else me_ref[0]
    for half in range(pair):
        onehot = onehot_of(number(users_ref[half], 1 + tower), me, groups)
        moved = mm(onehot, hidden_ref[half], 1, 0).astype(BF16)
        for k in range(groups):
            part = moved[k * span : (k + 1) * span, :]
            if count == 1:
                out_refs[0][k, half] = part
            else:
                out_refs[k][half] = part


def slot_hidden(me, users, hidden, groups, tower, apart, after):
    blocks, rows, width = hidden.shape
    span = EXPERTS * CAP // groups
    pair = 2
    if apart:
        out_specs = [pl.BlockSpec((pair, span, width), lambda b: (b, 0, 0))] * groups
        out_shape = [jax.ShapeDtypeStruct((blocks, span, width), BF16)] * groups
    else:
        out_specs = [pl.BlockSpec((groups, pair, span, width), lambda b: (0, b, 0, 0))]
        out_shape = [jax.ShapeDtypeStruct((groups, blocks, span, width), BF16)]
    return pl.pallas_call(
        functools.partial(hidden_kernel, tower=tower),
        grid=(blocks // pair,),
        in_specs=[
            SCALARS,
            pl.BlockSpec((pair, EXTRA, rows), lambda b: (b, rows // EXTRA, 0)),
            pl.BlockSpec((pair, rows, width), lambda b: (b, 0, 0)),
            ANYWHERE,
        ],
        out_specs=out_specs,
        out_shape=out_shape,
        compiler_params=pltpu.CompilerParams(vmem_limit_bytes=VMEM),
        cost_estimate=SMALL,
    )(me, users, hidden, after)


def route_kernel(me_ref, target_ref, *refs, tower, count, order):
    total = refs[0][...]
    for ref in refs[1:count]:
        total = total + ref[...]
    low = total.astype(BF16)
    out_refs = refs[count + order :]
    span = out_refs[0].shape[0]
    onehot = onehot_of(target_ref[tower : tower + 1, :], me_ref[0], len(out_refs))
    moved = mm(onehot, low, 1, 0).astype(BF16)
    for k, out_ref in enumerate(out_refs):
        out_ref[...] = moved[k * span : (k + 1) * span, :]


def route(me, targets, pieces, tower, groups, after):
    rows, emb = pieces[0].shape
    span = EXPERTS * CAP // groups
    return pl.pallas_call(
        functools.partial(route_kernel, tower=tower, count=len(pieces), order=len(after)),
        in_specs=[SCALARS] + [WHOLE] * (1 + len(pieces)) + [ANYWHERE] * len(after),
        out_specs=[WHOLE] * groups,
        out_shape=[jax.ShapeDtypeStruct((span, emb), BF16)] * groups,
        compiler_params=pltpu.CompilerParams(vmem_limit_bytes=VMEM),
        cost_estimate=SMALL,
    )(me, targets, *pieces, *after)


def stack_kernel(*refs, count):
    for k in range(count):
        refs[-1][k] = refs[k][...]


def stack(pieces, after=()):
    return pl.pallas_call(
        functools.partial(stack_kernel, count=len(pieces)),
        in_specs=[WHOLE] * len(pieces) + [ANYWHERE] * len(after),
        out_specs=WHOLE,
        out_shape=jax.ShapeDtypeStruct((len(pieces),) + pieces[0].shape, pieces[0].dtype),
        compiler_params=pltpu.CompilerParams(vmem_limit_bytes=VMEM),
        cost_estimate=SMALL,
    )(*pieces, *after)


def outer_kernel(order_ref, me_ref, *refs, count):
    hidden_refs, grad_refs, out_ref = refs[:count], refs[count:-1], refs[-1]
    blocks, span, _ = hidden_refs[0].shape[-3:]
    groups = hidden_refs[0].shape[0] if count == 1 else count
    for e in range(span // CAP):
        here = slice(e * CAP, (e + 1) * CAP)
        left, right = [], []
        for j in range(blocks):
            block = j if len(grad_refs) == 1 else order_ref[j]
            for k in range(groups):
                if count == 1:
                    left.append(hidden_refs[0][me_ref[0] ^ k, block, here, :])
                else:
                    left.append(hidden_refs[k][block, here, :])
                if len(grad_refs) == 1:
                    right.append(grad_refs[0][j, k, here, :])
                else:
                    right.append(grad_refs[j][k, here, :])
        out_ref[e] = mm(jnp.concatenate(left), jnp.concatenate(right), 0, 0)


def outer(order, me, hidden, grads, cost):
    span, width = hidden[0].shape[-2:]
    emb = grads[0].shape[-1]
    own = span // CAP
    steps = 2

    def part(array):
        front = array.shape[:-2]
        return pl.BlockSpec(
            front + (span // steps, array.shape[-1]), lambda e, d=len(front): (0,) * d + (e, 0)
        )

    return pl.pallas_call(
        functools.partial(outer_kernel, count=len(hidden)),
        grid=(steps,),
        in_specs=[SCALARS, SCALARS] + [part(array) for array in hidden + grads],
        out_specs=pl.BlockSpec((own // steps, width, emb), lambda e: (e, 0, 0)),
        out_shape=jax.ShapeDtypeStruct((own, width, emb), F32),
        compiler_params=pltpu.CompilerParams(vmem_limit_bytes=VMEM),
        cost_estimate=cost,
    )(order, me, *hidden, *grads)


def shards(user_emb, item_emb, user_hidden, item_hidden, user_expert, item_expert, positive):
    rows, emb = user_emb.shape
    groups = lax.axis_size("user")
    parts = lax.axis_size("item")
    width = user_hidden.shape[1] // parts
    lines = parts // CORES
    me = lax.axis_index("user").astype(jnp.int32)
    part = lax.axis_index("item").astype(jnp.int32)
    others = me ^ jnp.arange(groups, dtype=jnp.int32)
    both = part ^ jnp.arange(CORES, dtype=jnp.int32)
    order = (both[:, None] ^ (CORES * jnp.arange(lines, dtype=jnp.int32))[None, :]).reshape(-1)
    first = (part * groups + others) * rows
    me = me.reshape(1)

    packed, targets = pack(user_emb, positive, user_expert, item_expert)
    users = lax.all_gather(packed, "item", axis=0)
    items = exchange([item_emb] * groups, "user")

    def scatter(pieces, axis):
        return lax.all_to_all(pieces, axis, split_axis=0, concat_axis=0, tiled=True)

    user_cols = scatter(cut(user_hidden, parts, items[1]), "item")
    item_blocks = cut(item_hidden, parts, items[1])
    found = stats(first, users, items, rows, item_blocks)
    item_cols = scatter(item_blocks, "item")
    gathered = exchange([found] * parts, "item")
    losses, user_part, item_parts = grads(first, users, items, gathered, rows, user_cols)
    row_loss = lax.dynamic_slice_in_dim(losses[0], part * rows, rows)
    user_grad = lax.psum_scatter(user_part, "item", scatter_dimension=0, tiled=True)
    item_pieces = exchange(item_parts, "user")

    user_slots = slot_hidden(me, users, user_cols, groups, 0, True, item_parts[0])
    user_rows = exchange(user_slots, "user")
    item_routed = route(me, targets, item_pieces, 1, groups, user_slots[:1])
    item_sent = stack(exchange(item_routed, "user"))
    item_line = exchange([item_sent] * lines, "item", CORES)
    user_routed = route(me, targets, [user_grad], 0, groups, user_rows[1:])
    item_slots = slot_hidden(me, users, item_cols, groups, 1, False, user_routed[0])
    user_sent = stack(exchange(user_routed, "user"), item_line[1:] + [item_slots[0]])
    item_rows = [scatter(item_slots[0], "user")]
    item_cross = item_line + [swap(piece, "item", 1) for piece in item_line]
    user_all = lax.all_gather(user_sent, "item", axis=0)
    item_weight_grad = outer(order, me, item_rows, item_cross, SMALL)
    user_weight_grad = outer(order, me, user_rows, [user_all], SMALL)
    return (row_loss, user_weight_grad, item_weight_grad)


def solution(mesh):
    placed = (
        P(("user", "item"), None),
        P(("item", "user"), None),
        P(("user", "item"), None),
        P(("item", "user"), None),
        P(("user", "item"), None),
        P(("item", "user"), None),
        P(("user", "item")),
    )
    return jax.shard_map(
        shards,
        mesh=mesh,
        in_specs=placed,
        out_specs=(P(("user", "item")), P("user", "item", None), P("user", "item", None)),
        check_vma=False,
    )
```

```python
import functools
import math

import jax
import jax.numpy as jnp
from jax import lax
from jax.experimental import pallas as pl
from jax.experimental.pallas import tpu as pltpu
from jax.sharding import PartitionSpec as P

EMB = 256
EXPERTS = 32
CAP = 16
SCALE = 1.0 / math.sqrt(EMB)
EXTRA = 16
DIGIT = 128
MIB = 1 << 20

F32 = jnp.float32
BF16 = jnp.bfloat16
CORES = 2
SCALARS = pl.BlockSpec(memory_space=pltpu.SMEM)
WHOLE = pl.BlockSpec(memory_space=pltpu.VMEM)
ANYWHERE = pl.BlockSpec(memory_space=pl.ANY)
VMEM = 60 * MIB
SMALL = pl.CostEstimate(flops=1024, bytes_accessed=1024, transcendentals=0)


def mm(a, b, ca, cb):
    return lax.dot_general(a, b, (((ca,), (cb,)), ((), ())), preferred_element_type=F32)


def number(rows, index):
    rows = rows.astype(F32)
    high = rows[2 * index : 2 * index + 1]
    return (high * DIGIT + rows[2 * index + 1 : 2 * index + 2]).astype(jnp.int32)


def swap(piece, axis, bits):
    size = lax.axis_size(axis)
    return lax.ppermute(piece, axis, [(j, j ^ bits) for j in range(size)])


def exchange(pieces, axis, unit=1):
    return [piece if k == 0 else swap(piece, axis, k * unit) for k, piece in enumerate(pieces)]


def pack_kernel(emb_ref, positive_ref, user_ref, item_ref, out_ref, target_ref):
    rows = emb_ref.shape[0]
    down = lax.broadcasted_iota(jnp.int32, (rows, rows), 0)
    across = lax.broadcasted_iota(jnp.int32, (rows, rows), 1)

    def slots(expert):
        wide = jnp.broadcast_to(expert.astype(F32), (rows, rows))
        before = jnp.where((wide == wide.T) & (down < across), 1.0, 0.0)
        return expert * CAP + jnp.sum(before, axis=0, keepdims=True).astype(jnp.int32)

    user = slots(user_ref[...])
    item = slots(item_ref[...])
    target_ref[0:1, :] = user
    target_ref[1:2, :] = item
    line = lax.broadcasted_iota(jnp.int32, (EXTRA, rows), 0)
    block = jnp.zeros((EXTRA, rows), jnp.int32)
    for index, values in enumerate((positive_ref[...], user, item)):
        block = jnp.where(line == 2 * index, values // DIGIT, block)
        block = jnp.where(line == 2 * index + 1, values % DIGIT, block)
    out_ref[:rows, :] = emb_ref[...]
    out_ref[rows:, :] = block.astype(F32).astype(BF16)


def pack(emb, positive, user_expert, item_expert):
    rows, width = emb.shape
    return pl.pallas_call(
        pack_kernel,
        out_shape=[
            jax.ShapeDtypeStruct((rows + EXTRA, width), BF16),
            jax.ShapeDtypeStruct((2, rows), jnp.int32),
        ],
        compiler_params=pltpu.CompilerParams(vmem_limit_bytes=VMEM),
        cost_estimate=SMALL,
    )(emb, positive.reshape(1, rows), user_expert.reshape(1, rows), item_expert.reshape(1, rows))


def stats_kernel(first_ref, users_ref, *refs, rows, chunk):
    *items_refs, _, out_ref, s_ref = refs
    own = items_refs[0].shape[0]
    n_cols = own * len(items_refs)
    for half in range(users_ref.shape[0]):
        queries = users_ref[half, :rows, :] * jnp.asarray(SCALE, BF16)
        for k, items_ref in enumerate(items_refs):
            s_ref[half, k * own : (k + 1) * own, :] = mm(items_ref[...], queries, 1, 1)
        positive = number(users_ref[half, rows:, :], 0)
        tops = jnp.full((8, rows), -jnp.inf, F32)
        for c in range(0, n_cols, chunk):
            part = s_ref[half, c : c + chunk, :]
            tops = jnp.maximum(tops, jnp.max(part.reshape(chunk // 8, 8, rows), axis=0))
        top = jnp.max(tops, axis=0, keepdims=True)
        total = jnp.zeros((8, rows), F32)
        picked = jnp.zeros((8, rows), F32)
        for c in range(0, n_cols, chunk):
            part = s_ref[half, c : c + chunk, :]
            probs = jnp.exp(part - top)
            total = total + jnp.sum(probs.reshape(chunk // 8, 8, rows), axis=0)
            wanted = positive - (first_ref[c // own] + c % own)
            hit = lax.broadcasted_iota(jnp.int32, (chunk, rows), 0) == wanted
            chosen = jnp.where(hit, part, 0.0)
            picked = picked + jnp.sum(chosen.reshape(chunk // 8, 8, rows), axis=0)
        here = pl.ds(half * rows, rows)
        out_ref[0:1, here] = top
        out_ref[1:2, here] = jnp.sum(total, axis=0, keepdims=True)
        out_ref[2:3, here] = jnp.sum(picked, axis=0, keepdims=True)


def stats(first, users, items, rows, after):
    blocks, height, emb = users.shape
    own = items[0].shape[0]
    n_cols = own * len(items)
    pair = 2
    return pl.pallas_call(
        functools.partial(stats_kernel, rows=rows, chunk=64),
        grid=(blocks // pair,),
        in_specs=[SCALARS, pl.BlockSpec((pair, height, emb), lambda b: (b, 0, 0))]
        + [pl.BlockSpec((own, emb), lambda b: (0, 0))] * len(items)
        + [ANYWHERE],
        out_specs=pl.BlockSpec((3, pair * rows), lambda b: (0, b)),
        out_shape=jax.ShapeDtypeStruct((3, blocks * rows), F32),
        scratch_shapes=[pltpu.VMEM((pair, n_cols, rows), F32)],
        compiler_params=pltpu.CompilerParams(vmem_limit_bytes=VMEM),
        cost_estimate=SMALL,
    )(first, users, *items, after)


def grad_kernel(first_ref, users_ref, *refs, rows, chunk, count, groups):
    stats_refs, refs = refs[:groups], refs[groups:]
    items_refs, refs = refs[:count], refs[count + 1 :]
    loss_ref, user_ref = refs[:2]
    part_refs = refs[2 : count + 2]
    s_ref, g_ref, flip_ref = refs[count + 2 :]
    own = items_refs[0].shape[0]
    n_cols = own * count
    step = pl.program_id(0)

    @pl.when(step == 0)
    def _():
        for k in range(count):
            flip_ref[:, k * own : (k + 1) * own] = items_refs[k][...].T
            part_refs[k][...] = jnp.zeros_like(part_refs[k])

    for half in range(users_ref.shape[0]):
        here = pl.ds(half * rows, rows)
        queries = users_ref[half, :rows, :]
        scaled = queries * jnp.asarray(SCALE, BF16)
        for k in range(count):
            s_ref[half, k * own : (k + 1) * own, :] = mm(items_refs[k][...], scaled, 1, 1)
        positive = number(users_ref[half, rows:, :], 0)
        top = functools.reduce(jnp.maximum, [ref[0:1, here] for ref in stats_refs])
        total = sum(ref[1:2, here] * jnp.exp(ref[0:1, here] - top) for ref in stats_refs)
        level = top + jnp.log(total)
        loss_ref[0:1, here] = level - sum(ref[2:3, here] for ref in stats_refs)
        for c in range(0, n_cols, chunk):
            probs = jnp.exp(s_ref[half, c : c + chunk, :] - level)
            wanted = positive - (first_ref[c // own] + c % own)
            hit = lax.broadcasted_iota(jnp.int32, (chunk, rows), 0) == wanted
            g_ref[half, c : c + chunk, :] = jnp.where(hit, probs - 1.0, probs).astype(BF16)
        for k in range(count):
            part_refs[k][...] += mm(g_ref[half, k * own : (k + 1) * own, :], queries, 1, 0)
        user_ref[here, :] = mm(flip_ref[...], g_ref[half], 1, 0).T * SCALE

    @pl.when(step == pl.num_programs(0) - 1)
    def _():
        for k in range(count):
            part_refs[k][...] = part_refs[k][...] * SCALE


def grads(first, users, items, gathered, rows, after):
    blocks, height, emb = users.shape
    count = len(items)
    own = items[0].shape[0]
    n_cols = own * count
    pair = 2
    groups = len(gathered)
    results = pl.pallas_call(
        functools.partial(grad_kernel, rows=rows, chunk=64, count=count, groups=groups),
        grid=(blocks // pair,),
        in_specs=[
            SCALARS,
            pl.BlockSpec((pair, height, emb), lambda b: (b, 0, 0)),
        ]
        + [pl.BlockSpec((3, pair * rows), lambda b: (0, b))] * groups
        + [pl.BlockSpec((own, emb), lambda b: (0, 0))] * count
        + [ANYWHERE],
        out_specs=[
            pl.BlockSpec((1, pair * rows), lambda b: (0, b)),
            pl.BlockSpec((pair * rows, emb), lambda b: (b, 0)),
        ]
        + [pl.BlockSpec((own, emb), lambda b: (0, 0))] * count,
        out_shape=[
            jax.ShapeDtypeStruct((1, blocks * rows), F32),
            jax.ShapeDtypeStruct((blocks * rows, emb), F32),
        ]
        + [jax.ShapeDtypeStruct((own, emb), F32)] * count,
        scratch_shapes=[
            pltpu.VMEM((pair, n_cols, rows), F32),
            pltpu.VMEM((pair, n_cols, rows), BF16),
            pltpu.VMEM((emb, n_cols), BF16),
        ],
        compiler_params=pltpu.CompilerParams(vmem_limit_bytes=VMEM),
        cost_estimate=SMALL,
    )(first, users, *gathered, *items, after)
    return results[0], results[1], results[2:]


def cut_kernel(in_ref, _, out_ref):
    width = out_ref.shape[2]
    for k in range(out_ref.shape[0]):
        out_ref[k] = in_ref[:, k * width : (k + 1) * width]


def cut(hidden, parts, after):
    rows, total = hidden.shape
    return pl.pallas_call(
        cut_kernel,
        in_specs=[WHOLE, ANYWHERE],
        out_specs=WHOLE,
        out_shape=jax.ShapeDtypeStruct((parts, rows, total // parts), BF16),
        compiler_params=pltpu.CompilerParams(vmem_limit_bytes=VMEM),
        cost_estimate=SMALL,
    )(hidden, after)


def onehot_of(target, me, groups):
    span = EXPERTS * CAP // groups
    place = lax.broadcasted_iota(jnp.int32, (EXPERTS * CAP, target.shape[1]), 0)
    place = (((place // span) ^ me) * span) + place % span
    return (place == target).astype(F32).astype(BF16)


def hidden_kernel(me_ref, users_ref, hidden_ref, _, *out_refs, tower):
    count, (pair, span, _) = len(out_refs), out_refs[0].shape[-3:]
    groups = out_refs[0].shape[0] if count == 1 else count
    me = 0 if count == 1 else me_ref[0]
    for half in range(pair):
        onehot = onehot_of(number(users_ref[half], 1 + tower), me, groups)
        moved = mm(onehot, hidden_ref[half], 1, 0).astype(BF16)
        for k in range(groups):
            part = moved[k * span : (k + 1) * span, :]
            if count == 1:
                out_refs[0][k, half] = part
            else:
                out_refs[k][half] = part


def slot_hidden(me, users, hidden, groups, tower, apart, after):
    blocks, rows, width = hidden.shape
    span = EXPERTS * CAP // groups
    pair = 2
    if apart:
        out_specs = [pl.BlockSpec((pair, span, width), lambda b: (b, 0, 0))] * groups
        out_shape = [jax.ShapeDtypeStruct((blocks, span, width), BF16)] * groups
    else:
        out_specs = [pl.BlockSpec((groups, pair, span, width), lambda b: (0, b, 0, 0))]
        out_shape = [jax.ShapeDtypeStruct((groups, blocks, span, width), BF16)]
    return pl.pallas_call(
        functools.partial(hidden_kernel, tower=tower),
        grid=(blocks // pair,),
        in_specs=[
            SCALARS,
            pl.BlockSpec((pair, EXTRA, rows), lambda b: (b, rows // EXTRA, 0)),
            pl.BlockSpec((pair, rows, width), lambda b: (b, 0, 0)),
            ANYWHERE,
        ],
        out_specs=out_specs,
        out_shape=out_shape,
        compiler_params=pltpu.CompilerParams(vmem_limit_bytes=VMEM),
        cost_estimate=SMALL,
    )(me, users, hidden, after)


def route_kernel(me_ref, target_ref, *refs, tower, count, order):
    total = refs[0][...]
    for ref in refs[1:count]:
        total = total + ref[...]
    low = total.astype(BF16)
    out_refs = refs[count + order :]
    span = out_refs[0].shape[0]
    onehot = onehot_of(target_ref[tower : tower + 1, :], me_ref[0], len(out_refs))
    moved = mm(onehot, low, 1, 0).astype(BF16)
    for k, out_ref in enumerate(out_refs):
        out_ref[...] = moved[k * span : (k + 1) * span, :]


def route(me, targets, pieces, tower, groups, after):
    rows, emb = pieces[0].shape
    span = EXPERTS * CAP // groups
    return pl.pallas_call(
        functools.partial(route_kernel, tower=tower, count=len(pieces), order=len(after)),
        in_specs=[SCALARS] + [WHOLE] * (1 + len(pieces)) + [ANYWHERE] * len(after),
        out_specs=[WHOLE] * groups,
        out_shape=[jax.ShapeDtypeStruct((span, emb), BF16)] * groups,
        compiler_params=pltpu.CompilerParams(vmem_limit_bytes=VMEM),
        cost_estimate=SMALL,
    )(me, targets, *pieces, *after)


def stack_kernel(*refs, count):
    for k in range(count):
        refs[-1][k] = refs[k][...]


def stack(pieces, after=()):
    return pl.pallas_call(
        functools.partial(stack_kernel, count=len(pieces)),
        in_specs=[WHOLE] * len(pieces) + [ANYWHERE] * len(after),
        out_specs=WHOLE,
        out_shape=jax.ShapeDtypeStruct((len(pieces),) + pieces[0].shape, pieces[0].dtype),
        compiler_params=pltpu.CompilerParams(vmem_limit_bytes=VMEM),
        cost_estimate=SMALL,
    )(*pieces, *after)


def outer_kernel(order_ref, me_ref, *refs, count):
    hidden_refs, grad_refs, out_ref = refs[:count], refs[count:-1], refs[-1]
    blocks, span, _ = hidden_refs[0].shape[-3:]
    groups = hidden_refs[0].shape[0] if count == 1 else count
    for e in range(span // CAP):
        here = slice(e * CAP, (e + 1) * CAP)
        left, right = [], []
        for j in range(blocks):
            block = j if len(grad_refs) == 1 else order_ref[j]
            for k in range(groups):
                if count == 1:
                    left.append(hidden_refs[0][me_ref[0] ^ k, block, here, :])
                else:
                    left.append(hidden_refs[k][block, here, :])
                if len(grad_refs) == 1:
                    right.append(grad_refs[0][j, k, here, :])
                else:
                    right.append(grad_refs[j][k, here, :])
        out_ref[e] = mm(jnp.concatenate(left), jnp.concatenate(right), 0, 0)


def outer(order, me, hidden, grads, cost):
    span, width = hidden[0].shape[-2:]
    emb = grads[0].shape[-1]
    own = span // CAP
    steps = 2

    def part(array):
        front = array.shape[:-2]
        return pl.BlockSpec(
            front + (span // steps, array.shape[-1]), lambda e, d=len(front): (0,) * d + (e, 0)
        )

    return pl.pallas_call(
        functools.partial(outer_kernel, count=len(hidden)),
        grid=(steps,),
        in_specs=[SCALARS, SCALARS] + [part(array) for array in hidden + grads],
        out_specs=pl.BlockSpec((own // steps, width, emb), lambda e: (e, 0, 0)),
        out_shape=jax.ShapeDtypeStruct((own, width, emb), F32),
        compiler_params=pltpu.CompilerParams(vmem_limit_bytes=VMEM),
        cost_estimate=cost,
    )(order, me, *hidden, *grads)


def shards(user_emb, item_emb, user_hidden, item_hidden, user_expert, item_expert, positive):
    rows, emb = user_emb.shape
    groups = lax.axis_size("user")
    parts = lax.axis_size("item")
    width = user_hidden.shape[1] // parts
    lines = parts // CORES
    me = lax.axis_index("user").astype(jnp.int32)
    part = lax.axis_index("item").astype(jnp.int32)
    others = me ^ jnp.arange(groups, dtype=jnp.int32)
    both = part ^ jnp.arange(CORES, dtype=jnp.int32)
    order = (both[:, None] ^ (CORES * jnp.arange(lines, dtype=jnp.int32))[None, :]).reshape(-1)
    first = (part * groups + others) * rows
    me = me.reshape(1)

    packed, targets = pack(user_emb, positive, user_expert, item_expert)
    users = lax.all_gather(packed, "item", axis=0)
    items = exchange([item_emb] * groups, "user")

    def scatter(pieces, axis):
        return lax.all_to_all(pieces, axis, split_axis=0, concat_axis=0, tiled=True)

    user_cols = scatter(cut(user_hidden, parts, items[1]), "item")
    item_blocks = cut(item_hidden, parts, items[1])
    found = stats(first, users, items, rows, item_blocks)
    item_cols = scatter(item_blocks, "item")
    gathered = exchange([found] * parts, "item")
    losses, user_part, item_parts = grads(first, users, items, gathered, rows, user_cols)
    row_loss = lax.dynamic_slice_in_dim(losses[0], part * rows, rows)
    user_grad = lax.psum_scatter(user_part, "item", scatter_dimension=0, tiled=True)
    item_pieces = exchange(item_parts, "user")

    user_slots = slot_hidden(me, users, user_cols, groups, 0, True, item_parts[0])
    user_rows = exchange(user_slots, "user")
    item_routed = route(me, targets, item_pieces, 1, groups, user_slots[:1])
    item_sent = stack(exchange(item_routed, "user"))
    item_line = exchange([item_sent] * lines, "item", CORES)
    user_routed = route(me, targets, [user_grad], 0, groups, user_rows[1:])
    item_slots = slot_hidden(me, users, item_cols, groups, 1, False, user_routed[0])
    user_sent = stack(exchange(user_routed, "user"), item_line[1:2] + [item_slots[0]])
    item_rows = [scatter(item_slots[0], "user")]
    item_cross = item_line + [swap(piece, "item", 1) for piece in item_line]
    user_all = lax.all_gather(user_sent, "item", axis=0)
    item_weight_grad = outer(order, me, item_rows, item_cross, SMALL)
    user_weight_grad = outer(order, me, user_rows, [user_all], SMALL)
    return (row_loss, user_weight_grad, item_weight_grad)


def solution(mesh):
    placed = (
        P(("user", "item"), None),
        P(("item", "user"), None),
        P(("user", "item"), None),
        P(("item", "user"), None),
        P(("user", "item"), None),
        P(("item", "user"), None),
        P(("user", "item")),
    )
    return jax.shard_map(
        shards,
        mesh=mesh,
        in_specs=placed,
        out_specs=(P(("user", "item")), P("user", "item", None), P("user", "item", None)),
        check_vma=False,
    )
```
